32 devices in a mesh: dp: 2 (over core), seq: 16 (over z, y, x).
Axes of the slice: x: 2, y: 2, z: 4, core: 2. Of those that a mesh axis runs over, the one named last changes fastest.
Arguments:
- long_tokens: bfloat16 [2, 2, 1024, 256], P(None, 'dp', 'seq'), may hold values from -6 to 6
- short_tokens: bfloat16 [2, 32, 128, 256], P(None, ('dp', 'seq')), may hold values from -6 to 6
- long_cotangent: bfloat16 [2, 2, 1024, 256], P(None, 'dp', 'seq'), may hold values from -6 to 6
- short_cotangent: bfloat16 [2, 32, 128, 256], P(None, ('dp', 'seq')), may hold values from -6 to 6
- long_mask: int32 [2, 2, 1024], P(None, 'dp', 'seq'), may hold values 0 or 1
- short_mask: int32 [2, 32, 128], P(None, ('dp', 'seq')), may hold values 0 or 1
- complement: int32 [256], replicated, may hold values from 0 to 255, as said below
- norm_gain: float32 [256], P(('dp', 'seq')), may hold values from 0.5 to 1.5
- in_weight: bfloat16 [256, 1024], P(None, ('dp', 'seq')), may hold values from -0.375 to 0.375
- conv_weight: float32 [4, 512], P(None, ('dp', 'seq')), may hold values from -3 to 3
- conv_bias: float32 [512], P(('dp', 'seq')), may hold values from -0.5 to 0.5
- x_weight: bfloat16 [512, 48], P(('dp', 'seq')), may hold values from -0.25 to 0.25
- dt_weight: bfloat16 [16, 512], P(None, ('dp', 'seq')), may hold values from -1.5 to 1.5
- dt_bias: float32 [512], P(('dp', 'seq')), may hold values from -6 to -2
- a_log: float32 [512, 16], P(('dp', 'seq')), may hold values from -9 to 0.5
- d_skip: float32 [512], P(('dp', 'seq')), may hold values from 0.5 to 1.5
- out_weight: bfloat16 [512, 256], P(('dp', 'seq')), may hold values from -0.75 to 0.75
Outputs:
- long_out: bfloat16 [2, 2, 1024, 256], P(None, 'dp', 'seq')
- short_out: bfloat16 [2, 32, 128, 256], P(None, ('dp', 'seq'))
- long_input_grad: float32 [2, 2, 1024, 256], P(None, 'dp', 'seq')
- short_input_grad: float32 [2, 32, 128, 256], P(None, ('dp', 'seq'))
- grad_gain: float32 [256], P(('dp', 'seq'))
- grad_in: float32 [256, 1024], P(None, ('dp', 'seq'))
- grad_conv_w: float32 [4, 512], P(None, ('dp', 'seq'))
- grad_conv_b: float32 [512], P(('dp', 'seq'))
- grad_x: float32 [512, 48], P(('dp', 'seq'))
- grad_dt: float32 [16, 512], P(None, ('dp', 'seq'))
- grad_dt_b: float32 [512], P(('dp', 'seq'))
- grad_a_log: float32 [512, 16], P(('dp', 'seq'))
- grad_skip: float32 [512], P(('dp', 'seq'))
- grad_out: float32 [512, 256], P(('dp', 'seq'))
The draws below stay inside these ranges and needn't reach their ends.
Inputs may be any that keep to these rules, and one draw needn't show every extreme that they name: complement pairs the channels: complement[complement[c]] = c and complement[c] != c.
All inputs are finite; a program needn't handle non-finite values. No bound on the sum of `long_mask` or of `short_mask` on one device may be relied on, other than what follows from the above.
Results may differ from the reference program's by a relative error of at most 0.0077.
Values may be sent and summed in bfloat16 or wider, within the bound.
No kernel may reach another device: no remote copies, remote signals or barrier semaphores. Data moves between devices by JAX's collectives and lax.ppermute only.
A program may use at most 384 MiB of HBM per device.

```python
import math
import jax
import jax.numpy as jnp
from jax import lax

D = 256
E = 512
N = 16
R = 16
K = 4
MB = 2
SLEN = 128
RN = 48
LONG = 1024
WINDOWS = 2
SHORTS = 32


def draw_complement(key, part):
    key = jax.random.fold_in(key, 7)
    order = jax.random.permutation(key, D).astype(jnp.int32)
    partner = order.reshape(-1, 2)[:, ::-1].reshape(-1)
    return jnp.zeros((D,), jnp.int32).at[order].set(partner)


def plant(array, rng, low, high):
    place = [jax.random.randint(jax.random.fold_in(rng, axis), (), 0, length) for axis, length in enumerate(array.shape)]
    longest = array.shape.index(max(array.shape))
    next_to = place[:longest] + [(place[longest] + 1) % array.shape[longest]] + place[longest + 1:]
    return array.at[tuple(place)].set(low).at[tuple(next_to)].set(high)


def steps_of(rng, dims, shards, smallest, largest):
    level = 1.0
    for axis_at, shards_of in shards:
        steps = jax.random.uniform(jax.random.fold_in(jax.random.fold_in(rng, 6), axis_at), (shards_of,), jnp.float32, smallest / len(shards), largest / len(shards))
        level = level * jnp.repeat(jnp.exp(steps), dims[axis_at] // shards_of).reshape((-1,) + (1,) * (len(dims) - 1 - axis_at))
    return level


def normal_values(rng, shape, deviation, reach, shards=(), kind=jnp.bfloat16):
    values = jax.random.normal(rng, shape, jnp.float32) * deviation
    if len(shards) > 0:
        values = steps_of(rng, shape, shards, -0.22, 0.18) * values
    return jnp.clip(values, min=-reach, max=reach).astype(kind)


def setup_inputs(seed: int = 0) -> dict:
    arg_keys = jax.random.split(jax.random.key(seed), 18)
    return {
        "long_tokens": normal_values(arg_keys[0], (MB, WINDOWS, LONG, D), 1.0, 6.0, ((1, 2), (2, 16))),
        "short_tokens": normal_values(arg_keys[1], (MB, SHORTS, SLEN, D), 1.0, 6.0, ((1, 32),)),
        "long_cotangent": normal_values(arg_keys[2], (MB, WINDOWS, LONG, D), 1.0, 6.0, ((1, 2), (2, 16))),
        "short_cotangent": normal_values(arg_keys[3], (MB, SHORTS, SLEN, D), 1.0, 6.0, ((1, 32),)),
        "long_mask": plant((jax.random.randint(arg_keys[4], (MB, WINDOWS, LONG), 0, 20) < 3).astype(jnp.int32), jax.random.fold_in(arg_keys[4], 1), 0, 1),
        "short_mask": plant((jax.random.randint(arg_keys[5], (MB, SHORTS, SLEN), 0, 20) < 3).astype(jnp.int32), jax.random.fold_in(arg_keys[5], 1), 0, 1),
        "complement": draw_complement(jax.random.fold_in(arg_keys[17], 71), 0),
        "norm_gain": jnp.clip(1.0 + 0.1 * jax.random.normal(arg_keys[7], (D,), jnp.float32), 0.5, 1.5),
        "in_weight": normal_values(arg_keys[8], (D, 2 * E), D ** -0.5, 0.375, ((1, 32),)),
        "conv_weight": normal_values(arg_keys[9], (K, E), 0.5, 3.0, ((1, 32),), jnp.float32),
        "conv_bias": jnp.clip(jax.random.uniform(arg_keys[10], (E,), jnp.float32, -0.5, 0.5) * steps_of(arg_keys[10], (E,), ((0, 32),), -0.4, 0.0), -0.5, 0.5),
        "x_weight": normal_values(arg_keys[11], (E, RN), E ** -0.5, 0.25, ((0, 32),)),
        "dt_weight": normal_values(arg_keys[12], (R, E), R ** -0.5, 1.5, ((1, 32),)),
        "dt_bias": jnp.clip(-6.0 + 4.0 * jax.random.uniform(arg_keys[13], (E,), jnp.float32) ** steps_of(arg_keys[13], (E,), ((0, 32),), -0.2, 0.2), -6.0, -2.0),
        "a_log": jnp.clip(-9.0 + 9.5 * jax.random.uniform(arg_keys[14], (E, N), jnp.float32) ** steps_of(arg_keys[14], (E, N), ((0, 32),), -0.2, 0.2), -9.0, 0.5),
        "d_skip": jnp.clip(0.5 + 1.0 * jax.random.uniform(arg_keys[15], (E,), jnp.float32) ** steps_of(arg_keys[15], (E,), ((0, 32),), -0.2, 0.2), 0.5, 1.5),
        "out_weight": normal_values(arg_keys[16], (E, D), (E // 8) ** -0.5, 0.75, ((0, 32),)),
    }


EPS = 1e-05
EXACT = lax.Precision.HIGHEST

@jax.custom_vjp
def low(v):
    return lax.optimization_barrier(v.astype(jnp.bfloat16)).astype(jnp.float32)

@jax.custom_vjp
def low_back(v):
    return v

def low_keep(v):
    return (low(v), None)

def low_pass(kept, grad):
    return (grad,)

def back_keep(v):
    return (v, None)

def back_low(kept, grad):
    return (low(grad),)
low.defvjp(low_keep, low_pass)
low_back.defvjp(back_keep, back_low)

def affine(earlier, later):
    return (earlier[0] * later[0], later[0] * earlier[1] + later[1])

def convolve(padded, conv_w, conv_b):
    width = conv_w.shape[0]
    count = padded.shape[0] - width + 1
    total = conv_b + conv_w[0] * padded[0:count]
    for offset in range(1, width):
        total = total + conv_w[offset] * padded[offset:offset + count]
    return total

def branch(weights, normed_low, block):
    projected = low_back(jnp.dot(normed_low, weights['in'], precision=EXACT))
    inner_size = weights['in'].shape[1] // 2
    inner_pre = projected[:, :inner_size]
    gate_pre = projected[:, inner_size:]
    halo = weights['conv_w'].shape[0] - 1
    padded = jnp.pad(inner_pre, ((halo, 0), (0, 0)))
    conv_out = convolve(padded, weights['conv_w'], weights['conv_b'])
    inner = jax.nn.silu(conv_out)
    select = jnp.dot(low(inner), weights['x'], precision=EXACT)
    rank = weights['dt'].shape[0]
    state_size = weights['a_log'].shape[1]
    step_low = select[:, :rank]
    input_map = select[:, rank:rank + state_size]
    output_map = select[:, rank + state_size:]
    step_size = jax.nn.softplus(jnp.dot(step_low, weights['dt'], precision=EXACT) + weights['dt_b'])
    rates = -jnp.exp(weights['a_log'])
    length = inner.shape[0]
    count = length // block

    def scan_block(state, pieces):
        step_part, inner_part, input_part, output_part = pieces
        decay = jnp.exp(step_part[:, :, None] * rates[None])
        push = (step_part * inner_part)[:, :, None] * input_part[:, None, :]
        prefix, partial_sum = lax.associative_scan(affine, (decay, push), axis=0)
        states = partial_sum + prefix * state
        return (states[-1], jnp.einsum('ten,tn->te', states, output_part, precision=EXACT))
    pieces = (step_size.reshape(count, block, -1), inner.reshape(count, block, -1), input_map.reshape(count, block, -1), output_map.reshape(count, block, -1))
    start = jnp.zeros(rates.shape, jnp.float32)
    _, readout = lax.scan(jax.checkpoint(scan_block), start, pieces)
    mixed = readout.reshape(length, -1) + weights['skip'] * inner
    gated = mixed * jax.nn.silu(gate_pre)
    return jnp.dot(low(gated), weights['out'], precision=EXACT)

def layer(weights, tokens, complement, block):
    scale = lax.rsqrt(lax.optimization_barrier(jnp.mean(tokens * tokens, 1, keepdims=True)) + EPS)
    normed_low = low(tokens * scale * weights['gain'])
    reverse_low = jnp.take(normed_low[::-1], complement, axis=1)
    out_fwd = branch(weights, normed_low, block)
    out_rev = branch(weights, reverse_low, block)
    return tokens + out_fwd + jnp.take(out_rev[::-1], complement, axis=1)

def window_group(weights, tokens, cotangent, mask, complement, block):
    source = tokens.astype(jnp.float32)
    seed_grad = cotangent.astype(jnp.float32) * mask[..., None].astype(jnp.float32)

    def forward(params, inputs):
        return jax.vmap(lambda single: layer(params, single, complement, block))(inputs)
    result, pull = jax.vjp(forward, weights, source)
    grad_weights, grad_source = pull(seed_grad)
    return (result.astype(jnp.bfloat16), grad_source, grad_weights)

def reference(long_tokens, short_tokens, long_cotangent, short_cotangent, long_mask, short_mask, complement, norm_gain, in_weight, conv_weight, conv_bias, x_weight, dt_weight, dt_bias, a_log, d_skip, out_weight):
    weights = dict(gain=norm_gain.astype(jnp.float32), conv_w=conv_weight.astype(jnp.float32), conv_b=conv_bias.astype(jnp.float32), dt_b=dt_bias.astype(jnp.float32), a_log=a_log.astype(jnp.float32), skip=d_skip.astype(jnp.float32))
    weights['in'] = in_weight.astype(jnp.float32)
    weights['x'] = x_weight.astype(jnp.float32)
    weights['dt'] = dt_weight.astype(jnp.float32)
    weights['out'] = out_weight.astype(jnp.float32)
    zero = jax.tree.map(jnp.zeros_like, weights)
    long_block = math.gcd(LONG, 512)
    short_block = math.gcd(SLEN, 512)
    group = math.gcd(MB * SHORTS, max(1, 4096 // SLEN))

    def long_step(total, pieces):
        tokens, cotangent, mask = pieces
        result, grad_source, grads = window_group(weights, tokens, cotangent, mask, complement, long_block)
        return (jax.tree.map(jnp.add, total, grads), (result, grad_source))

    def short_step(total, pieces):
        tokens, cotangent, mask = pieces
        result, grad_source, grads = window_group(weights, tokens, cotangent, mask, complement, short_block)
        return (jax.tree.map(jnp.add, total, grads), (result, grad_source))
    long_in = (long_tokens.reshape(MB * WINDOWS, 1, LONG, D), long_cotangent.reshape(MB * WINDOWS, 1, LONG, D), long_mask.reshape(MB * WINDOWS, 1, LONG))
    total, (long_res, long_grad) = lax.scan(long_step, zero, long_in)
    steps_short = MB * SHORTS // group
    short_in = (short_tokens.reshape(steps_short, group, SLEN, D), short_cotangent.reshape(steps_short, group, SLEN, D), short_mask.reshape(steps_short, group, SLEN))
    total, (short_res, short_grad) = lax.scan(short_step, total, short_in)
    return (long_res.reshape(MB, WINDOWS, LONG, D), short_res.reshape(MB, SHORTS, SLEN, D), long_grad.reshape(MB, WINDOWS, LONG, D), short_grad.reshape(MB, SHORTS, SLEN, D), total['gain'], total['in'], total['conv_w'], total['conv_b'], total['x'], total['dt'], total['dt_b'], total['a_log'], total['skip'], total['out'])
```

```python
import functools
import types

import jax
import jax.numpy as jnp
from jax import lax
from jax.experimental import pallas as pl
from jax.experimental.pallas import tpu as pltpu
from jax.sharding import PartitionSpec as P

EPS = 1e-05
D, E, N, MB, HALO = 256, 512, 16, 2, 16
LT = 128
NP = N // 2
LOG2E = 1.4426950408889634
LN2 = 0.6931471805599453
F32, BF = jnp.float32, jnp.bfloat16
NT = (((1,), (1,)), ((), ()))
TN = (((0,), (0,)), ((), ()))
BOTH = ("dp", "seq")
IN_ROWS, OUT_ROWS, CH_ROWS = 32, 16, 16
PACK = 2 * IN_ROWS + 2 * OUT_ROWS + CH_ROWS
AT_DT, AT_A, AT_SMALL = 48, 64, 96


def mm(a, b, dims=None):
    if dims is None:
        return jnp.dot(a, b, preferred_element_type=F32)
    return lax.dot_general(a, b, dims, preferred_element_type=F32)


def iota(shape, axis):
    return lax.broadcasted_iota(jnp.int32, shape, axis)


def onehot(cond):
    return jnp.where(cond, 1.0, 0.0).astype(BF)


def eye(n):
    return onehot(iota((n, n), 0) == iota((n, n), 1))


def split(x):
    hi = x.astype(BF)
    return hi, (x - hi.astype(F32)).astype(BF)


def sigmoid(x):
    return 1.0 / (1.0 + jnp.exp(-x))


def loop(count, body):
    lax.fori_loop(0, count, lambda i, c: (body(i), c)[1], 0)


def run(name, body, ins, outs, scratch=None, flops=0, far=()):
    scratch = scratch or {}
    in_names, out_names, scratch_names = list(ins), list(outs), list(scratch)

    def kernel(*refs):
        body(types.SimpleNamespace(**dict(zip(in_names + out_names + scratch_names, refs))))

    def spec(key):
        if key == "place":
            return pl.BlockSpec(memory_space=pltpu.SMEM)
        return pl.BlockSpec(memory_space=pl.ANY if key in far else pltpu.VMEM)

    result = pl.pallas_call(
        kernel,
        out_shape=tuple(jax.ShapeDtypeStruct(*outs[k]) for k in out_names),
        in_specs=[spec(k) for k in in_names],
        out_specs=tuple(pl.BlockSpec(memory_space=pltpu.VMEM) for _ in out_names),
        scratch_shapes=[
            pltpu.VMEM(*scratch[k]) if isinstance(scratch[k], tuple) else scratch[k]
            for k in scratch_names
        ],
        compiler_params=pltpu.CompilerParams(vmem_limit_bytes=60 * 1024 * 1024),
        cost_estimate=pl.CostEstimate(flops=flops, bytes_accessed=1 << 20, transcendentals=0),
        name=name,
    )(*[ins[k] for k in in_names])
    return dict(zip(out_names, result))


def pack_body(r):
    r.rows[...] = jnp.zeros((8, CH_ROWS), F32)
    r.rows[0:4, :] = r.conv_w[...]
    r.rows[4:5, :] = r.conv_b[...]
    r.rows[5:6, :] = r.dt_b[...]
    r.rows[6:7, :] = r.skip[...]
    r.rows[7:8, 0 : r.gain.shape[1]] = r.gain[...]
    in_t = mm(eye(IN_ROWS), r.in_w[...], NT).astype(BF)
    small = jnp.concatenate(split(r.rows[...]), 0)
    id16 = eye(CH_ROWS)

    def place(a, at):
        n = a.shape[1]
        return mm(a.astype(BF), onehot(iota((n, LT), 0) + at == iota((n, LT), 1)))

    a_hi, a_lo = split(r.a_log[...])
    chan = (
        place(r.x_w[...], 0)
        + place(mm(id16, r.dt_w[...], NT), AT_DT)
        + place(a_hi, AT_A)
        + place(a_lo, AT_A + N)
        + place(mm(id16, small, NT), AT_SMALL)
    ).astype(BF)
    out_w = r.out_w[...]
    for j in range(r.buf.shape[0] // PACK):
        at = j * PACK
        for half in range(2):
            lanes = slice(half * LT, (half + 1) * LT)
            r.buf[at + half * IN_ROWS : at + (half + 1) * IN_ROWS, :] = in_t[:, lanes]
            low = at + 2 * IN_ROWS + half * OUT_ROWS
            r.buf[low : low + OUT_ROWS, :] = out_w[:, lanes]
        r.buf[at + PACK - CH_ROWS : at + PACK, :] = chan


def unpack(r):
    count = r.mine.shape[0] // PACK
    mine_at = r.place[0]
    for src, d in ((r.mine, mine_at), (r.other, 1 - mine_at)):
        for j in range(count):
            at = j * PACK
            in_at = pl.multiple_of(d * (count * IN_ROWS) + j * IN_ROWS, IN_ROWS)
            out_at = pl.multiple_of(d * (count * OUT_ROWS) + j * OUT_ROWS, OUT_ROWS)
            for half in range(2):
                lanes = slice(half * LT, (half + 1) * LT)
                r.inT[pl.ds(in_at, IN_ROWS), lanes] = src[
                    at + half * IN_ROWS : at + (half + 1) * IN_ROWS, :
                ]
                low = at + 2 * IN_ROWS + half * OUT_ROWS
                r.outw[pl.ds(out_at, OUT_ROWS), lanes] = src[low : low + OUT_ROWS, :]
            r.pe[pl.ds(out_at, CH_ROWS), :] = src[at + PACK - CH_ROWS : at + PACK, :]


def derive(r):
    peT = mm(eye(LT), r.pe[...], NT)
    small = peT[AT_SMALL : AT_SMALL + 8] + peT[AT_SMALL + 8 : AT_SMALL + 16]
    r.rowp[...] = small
    rate = -jnp.exp(peT[AT_A : AT_A + N] + peT[AT_A + N : AT_A + 2 * N])
    r.rate[...] = rate
    for n in range(N):
        r.r2[4 * n : 4 * n + 4, :] = jnp.broadcast_to(rate[n : n + 1] * LOG2E, (4, E))
    dt = peT[AT_DT : AT_DT + N]
    r.dtw2[...] = jnp.concatenate([dt, dt, jnp.zeros((LT - 2 * N, E), F32)], 0).astype(BF)
    r.xwT[...] = jnp.where(iota((LT, E), 0) < 3 * N, peT, 0.0).astype(BF)


def gain_of(r):
    per = E // (D // 8)
    low = mm(eye(LT), r.pe[...], NT)[AT_SMALL : AT_SMALL + 16].astype(BF)
    lane, col = iota((E, D), 0), iota((E, D), 1)
    pick = onehot(((lane // per) == (col // 8)) & ((lane % per) == (col % 8)))
    g = mm(low, pick)
    return g[0:8] + g[8:16]


def placing(T, transposed):
    shape = (2 * MB * T, 2 * MB * T)
    row, col = iota(shape, 1 if transposed else 0), iota(shape, 0 if transposed else 1)
    t, scan = row >> 2, row & 3
    turn = T.bit_length() - 1
    pos, src = col & (T - 1), col >> turn
    want = jnp.where(scan >= 2, T - 1 - t, t)
    return (src == scan) & (pos == want)


def normalise(tok, gain):
    source = tok.astype(F32)
    scale = lax.rsqrt(jnp.mean(source * source, 1, keepdims=True) + EPS)
    return source, scale, source * scale


def swap_of(r):
    return onehot(iota((D, D), 0) == jnp.broadcast_to(r.comp[...], (D, D)))


def prep(r, T, halo):
    R = 4 * T
    gain = r.gain[0:1, :] if r.gain.shape[0] == 1 else r.gain[7:8, :]
    swap = swap_of(r)
    _, _, unit = normalise(r.tok[...], gain)
    normed = (unit * gain).astype(BF)
    put = placing(T, False)
    r.V[HALO:, :] = mm(
        onehot(put), jnp.concatenate([normed, mm(normed, swap).astype(BF)], 0)
    ).astype(BF)
    mrow = jnp.concatenate([r.mask[0:1, :], r.mask[1:2, :]], 1)
    mrow = jnp.concatenate([mrow, mrow], 1)
    cot = r.cot[...]
    r.GR[...] = mm(
        onehot(put & (mrow != 0)), jnp.concatenate([cot, mm(cot, swap).astype(BF)], 0)
    ).astype(BF)
    if halo:
        hn = (normalise(r.edge[...], gain)[2] * gain).astype(BF)
        r.V[0:HALO, :] = (
            mm(onehot(edge_place(False)), hn)
            + mm(onehot(edge_place(True)), mm(hn, swap).astype(BF))
        ).astype(BF)
        r.ip[0:HALO, :] = mm(r.V[0:HALO, :], r.inT[0:E, :], NT)
    else:
        r.V[0:HALO, :] = jnp.zeros((HALO, D), BF)
        r.ip[0:HALO, :] = jnp.zeros((HALO, E), F32)
    for c in range(0, E, 256):
        r.ip[HALO:, c : c + 256] = mm(r.V[HALO:, :], r.inT[c : c + 256, :], NT)
        r.gate[:, c : c + 256] = mm(r.V[HALO:, :], r.inT[E + c : E + c + 256, :], NT)
        r.gm[:, c : c + 256] = mm(r.GR[...], r.outw[c : c + 256, :], NT)
    w = [r.rowp[k : k + 1, :] for k in range(4)]
    conv_b, dt_b = r.rowp[4:5, :], r.rowp[5:6, :]
    B = 32

    def first(i):
        r0 = pl.multiple_of(i * B, B)
        x = r.ip[pl.ds(r0, B + HALO), :]
        total = conv_b
        for k in range(4):
            total = total + w[k] * x[4 + 4 * k : 4 + 4 * k + B]
        r.co[pl.ds(r0, B), :] = total
        inner = total * sigmoid(total)
        r.si[pl.ds(r0, B), :] = inner
        r.il[pl.ds(r0, B), :] = inner.astype(BF)
        g = r.gate[pl.ds(r0, B), :]
        r.gm[pl.ds(r0, B), :] = r.gm[pl.ds(r0, B), :] * (g * sigmoid(g))

    loop(R // B, first)
    sel = mm(r.il[...], r.pe[...])
    r.sel[...] = sel
    lane = iota((R, LT), 1)
    low = jnp.where(lane < N, sel, 0.0)
    hi = low.astype(BF).astype(F32)
    both = (hi + pltpu.roll(low - hi, N, 1)).astype(BF)
    for c in range(0, E, 256):
        r.st[:, c : c + 256] = mm(both, r.dtw2[:, c : c + 256])

    def second(i):
        r0 = pl.multiple_of(i * B, B)
        z = r.st[pl.ds(r0, B), :] + dt_b
        u = jnp.exp(-jnp.abs(z))
        inv = 1.0 / (1.0 + u)
        near = u * (1.0 - u * (0.5 - u * (1.0 / 3.0)))
        st = jnp.maximum(z, 0.0) + jnp.where(u < 0.01, near, jnp.log(1.0 + u))
        r.sz[pl.ds(r0, B), :] = jnp.where(z >= 0, inv, u * inv)
        r.st[pl.ds(r0, B), :] = st
        r.si[pl.ds(r0, B), :] = r.si[pl.ds(r0, B), :] * st

    loop(R // B, second)


def edge_place(rev):
    row, col = iota((HALO, HALO), 0), iota((HALO, HALO), 1)
    j, scan = row >> 2, row & 3
    if rev:
        return (scan >= 2) & (col == 8 + (scan - 2) * 4 + (3 - j))
    return (scan < 2) & (col == scan * 4 + j)


def maps(r, T):
    R = 4 * T
    sel = r.sel[...]
    lane = iota((R, LT), 1)
    kept = jnp.where((lane >= N) & (lane < 3 * N), sel, 0.0)
    hi = kept.astype(BF).astype(F32)
    both = (hi + pltpu.roll(kept - hi, 64, 1)).astype(BF)
    G = 128
    r8, r4 = iota((2 * G, G), 0), iota((2 * G, G), 1)
    twice = onehot(((r8 >> 3) * 4 + (r8 & 3)) == r4)
    own = (iota((2 * G, LT), 1) & 1) == ((iota((2 * G, LT), 0) >> 2) & 1)
    l, c = iota((LT, NP * LT), 0), iota((LT, NP * LT), 1)
    l = l & 63
    spread_in = onehot((l >= N) & (l < 2 * N) & (((l - N) >> 1) == (c >> 7)))
    spread_out = onehot((l >= 2 * N) & (l < 3 * N) & (((l - 2 * N) >> 1) == (c >> 7)))
    for g in range(R // G):
        left = jnp.where(own, mm(twice, both[g * G : (g + 1) * G]), 0.0).astype(BF)
        r.imb[g * 2 * G : (g + 1) * 2 * G, :] = mm(left, spread_in)
        r.omb[g * 2 * G : (g + 1) * 2 * G, :] = mm(left, spread_out)


def dup(x, low):
    turned = pltpu.roll(x, 4, 0)
    return jnp.where(low, x, turned), jnp.where(low, turned, x)


def lanes_of(e):
    return slice(e * LT, (e + 1) * LT)


def scan_forward(r, T, start, full, U=8):
    low = iota((8, LT), 0) < 4
    for e in range(E // LT):
        es = lanes_of(e)
        if start is None:
            first = tuple(jnp.zeros((8, LT), F32) for _ in range(NP))
        else:
            first = tuple(start[8 * k : 8 * k + 8, es] for k in range(NP))
        if full:
            for k in range(NP):
                r.states[0, 8 * k : 8 * k + 8, es] = first[k]

        def body(i, state):
            state = list(state)
            for u in range(U // 2):
                pair = i * (U // 2) + u
                row = pl.multiple_of(pair * 8, 8)
                st = dup(r.st[pl.ds(row, 8), es], low)
                si = dup(r.si[pl.ds(row, 8), es], low)
                ys = []
                for h in range(2):
                    t = pair * 2 + h
                    r8 = pl.multiple_of(t * 8, 8)
                    acc = None
                    for k in range(NP):
                        decay = jnp.exp2(st[h] * r.r2[8 * k : 8 * k + 8, es])
                        state[k] = decay * state[k] + si[h] * r.imb[pl.ds(r8, 8), lanes_of(k)]
                        if full:
                            r.states[t + 1, 8 * k : 8 * k + 8, es] = state[k]
                            y = state[k] * r.omb[pl.ds(r8, 8), lanes_of(k)]
                            acc = y if acc is None else acc + y
                    if full:
                        ys.append(acc + pltpu.roll(acc, 4, 0))
                if full:
                    r.mix[pl.ds(row, 8), es] = jnp.where(low, ys[0], ys[1])
            return tuple(state)

        last = lax.fori_loop(0, T // U, body, first)
        if not full:
            for k in range(NP):
                r.ends[8 * k : 8 * k + 8, es] = last[k]


def scan_adjoint_local(r, T, U=8):
    low = iota((8, LT), 0) < 4
    for e in range(E // LT):
        es = lanes_of(e)

        def body(i, b):
            b = list(b)
            for u in range(U // 2):
                pair = T // 2 - 1 - (i * (U // 2) + u)
                row = pl.multiple_of(pair * 8, 8)
                st = dup(r.st[pl.ds(row, 8), es], low)
                gm = dup(r.gm[pl.ds(row, 8), es], low)
                for h in (1, 0):
                    r8 = pl.multiple_of((pair * 2 + h) * 8, 8)
                    for k in range(NP):
                        a = gm[h] * r.omb[pl.ds(r8, 8), lanes_of(k)] + b[k]
                        b[k] = jnp.exp2(st[h] * r.r2[8 * k : 8 * k + 8, es]) * a
            return tuple(b)

        last = lax.fori_loop(0, T // U, body, tuple(jnp.zeros((8, LT), F32) for _ in range(NP)))
        for k in range(NP):
            r.ends[64 + 8 * k : 64 + 8 * k + 8, es] = last[k]


def scan_backward(r, T, start, U=8):
    low = iota((8, LT), 0) < 4
    rl, rc = iota((NP * LT, LT), 0), iota((NP * LT, LT), 1)
    r.red[...] = onehot((rl >> 7) == (rc >> 1))
    for e in range(E // LT):
        es = lanes_of(e)
        if start is None:
            first = tuple(jnp.zeros((8, LT), F32) for _ in range(NP))
        else:
            first = tuple(start[64 + 8 * k : 64 + 8 * k + 8, es] for k in range(NP))

        def body(i, carry):
            b, acc = list(carry[0]), list(carry[1])
            base = T // U - 1 - i
            xi = [[None] * U for _ in range(NP)]
            xo = [[None] * U for _ in range(NP)]
            for u in range(U // 2 - 1, -1, -1):
                pair = base * (U // 2) + u
                row = pl.multiple_of(pair * 8, 8)
                st = dup(r.st[pl.ds(row, 8), es], low)
                si = dup(r.si[pl.ds(row, 8), es], low)
                gm = dup(r.gm[pl.ds(row, 8), es], low)
                qs, ps = [None, None], [None, None]
                for h in (1, 0):
                    t = pair * 2 + h
                    r8 = pl.multiple_of(t * 8, 8)
                    q = p = None
                    for k in range(NP):
                        rk = r.r2[8 * k : 8 * k + 8, es]
                        a = gm[h] * r.omb[pl.ds(r8, 8), lanes_of(k)] + b[k]
                        b[k] = jnp.exp2(st[h] * rk) * a
                        w = b[k] * r.states[t, 8 * k : 8 * k + 8, es]
                        q = w * rk if q is None else q + w * rk
                        acc[k] = acc[k] + w * st[h]
                        ai = a * r.imb[pl.ds(r8, 8), lanes_of(k)]
                        p = ai if p is None else p + ai
                        xi[k][2 * u + h] = a * si[h]
                        xo[k][2 * u + h] = r.states[t + 1, 8 * k : 8 * k + 8, es] * gm[h]
                    qs[h] = q + pltpu.roll(q, 4, 0)
                    ps[h] = p + pltpu.roll(p, 4, 0)
                r.q[pl.ds(row, 8), es] = jnp.where(low, qs[0], qs[1])
                r.p[pl.ds(row, 8), es] = jnp.where(low, ps[0], ps[1])
            y = None
            for k in range(0, NP, 2):
                left = jnp.concatenate(
                    [jnp.concatenate(xi[j] + xo[j], 0).astype(BF) for j in (k, k + 1)], 1
                )
                part = mm(left, r.red[k * LT : (k + 2) * LT, :])
                y = part if y is None else y + part
            at = pl.multiple_of(base * U * 8, U * 8)
            if e == 0:
                r.yi[pl.ds(at, U * 8), :] = y[: U * 8]
                r.yo[pl.ds(at, U * 8), :] = y[U * 8 :]
            else:
                r.yi[pl.ds(at, U * 8), :] += y[: U * 8]
                r.yo[pl.ds(at, U * 8), :] += y[U * 8 :]
            return tuple(b), tuple(acc)

        zero = tuple(jnp.zeros((8, LT), F32) for _ in range(NP))
        _, acc = lax.fori_loop(0, T // U, body, (first, zero))
        for k in range(NP):
            r.alog[8 * k : 8 * k + 8, es] = acc[k]
    G = 256
    own = (iota((G, LT), 1) & 1) == ((iota((G, LT), 0) >> 2) & 1)
    valid = own & (iota((G, LT), 1) < N)
    r8, r4 = iota((G // 2, G), 1), iota((G // 2, G), 0)
    fold = onehot(((r8 >> 3) * 4 + (r8 & 3)) == r4)
    for g in range(8 * T // G):
        at = slice(g * G, (g + 1) * G)
        y = pltpu.roll(jnp.where(valid, r.yi[at, :], 0.0), N, 1) + pltpu.roll(
            jnp.where(valid, r.yo[at, :], 0.0), 2 * N, 1
        )
        hi, lo = split(y)
        r.gsel[g * G // 2 : (g + 1) * G // 2, :] = mm(fold, hi) + mm(fold, lo)


def scan_scratch(T):
    return dict(
        states=((T + 1, 8 * NP, E), F32),
        imb=((8 * T, NP * LT), F32),
        omb=((8 * T, NP * LT), F32),
        red=((NP * LT, LT), BF),
        yi=((8 * T, LT), F32),
        yo=((8 * T, LT), F32),
        mix=((4 * T, E), F32),
        q=((4 * T, E), F32),
        p=((4 * T, E), F32),
        alog=((8 * NP, E), F32),
        gsel=((4 * T, LT), F32),
    )


def post(r, T, halo):
    R = 4 * T
    B = 32
    w = [r.rowp[k : k + 1, :] for k in range(4)]
    skip = r.rowp[6:7, :]
    gain = r.gain[0:1, :] if r.gain.shape[0] == 1 else r.gain[7:8, :]
    r.acc[...] = jnp.zeros((64, E), F32)
    for c in range(0, E, 256):
        r.gg[:, c : c + 256] = mm(r.GR[...], r.outw[c : c + 256, :], NT)

    def fold8(x):
        total = x[0:8]
        for j in range(8, x.shape[0], 8):
            total = total + x[j : j + 8]
        return total

    def first(i):
        r0 = pl.multiple_of(i * B, B)
        at = pl.ds(r0, B)
        co, gate, st, gm, p = r.co[at, :], r.gate[at, :], r.st[at, :], r.gm[at, :], r.p[at, :]
        sg = sigmoid(co)
        inner = co * sg
        r.il[at, :] = inner.astype(BF)
        mixed = r.mix[at, :] + skip * inner
        gs = sigmoid(gate)
        silu_gate = gate * gs
        r.gated[at, :] = (mixed * silu_gate).astype(BF)
        r.gp[pl.ds(HALO + r0, B), E:] = (r.gg[at, :] * mixed * (gs + silu_gate * (1.0 - gs))).astype(
            BF
        )
        gz = (r.q[at, :] * LN2 + inner * p) * r.sz[at, :]
        r.gz[at, :] = gz.astype(BF)
        r.acc[40:48, :] += fold8(gz)
        r.acc[48:56, :] += fold8(gm * inner)
        r.gg[at, :] = st * p + gm * skip
        r.slope[at, :] = sg + inner * (1.0 - sg)

    loop(R // B, first)
    lane = iota((R, LT), 1)
    gs_low = jnp.where(lane < N, mm(r.gz[...], r.dtw2[...], NT), r.gsel[...])
    gs_low = jnp.where(lane < 3 * N, gs_low, 0.0)
    r.z[...] = (
        gs_low
        + jnp.where((lane >= AT_DT) & (lane < AT_DT + N), pltpu.roll(r.sel[...], AT_DT, 1), 0.0)
    ).astype(BF)
    gsb = gs_low.astype(BF)
    for c in range(0, E, 256):
        r.mix[:, c : c + 256] = mm(gsb, r.xwT[:, c : c + 256])
    r.gco[0:HALO, :] = jnp.zeros((HALO, E), F32)
    r.gco[HALO + R :, :] = jnp.zeros((HALO, E), F32)

    def second(i):
        r0 = pl.multiple_of(i * B, B)
        at = pl.ds(r0, B)
        gco = (r.gg[at, :] + r.mix[at, :]) * r.slope[at, :]
        r.gco[pl.ds(HALO + r0, B), :] = gco
        x = r.ip[pl.ds(r0, B + HALO), :]
        for k in range(4):
            r.acc[8 * k : 8 * k + 8, :] += fold8(gco * x[4 + 4 * k : 4 + 4 * k + B])
        r.acc[32:40, :] += fold8(gco)

    loop(R // B, second)

    def third(i):
        r0 = pl.multiple_of(i * 16, 16)
        x = r.gco[pl.ds(r0, 32), :]
        total = w[3] * x[0:16]
        for k in range(3):
            total = total + w[k] * x[4 * (3 - k) : 4 * (3 - k) + 16]
        r.gp[pl.ds(r0, 16), :E] = total.astype(BF)

    loop((HALO + R) // 16, third)
    r.gp[0:HALO, E:] = jnp.zeros((HALO, E), BF)
    if not halo:
        r.gp[0:HALO, :E] = jnp.zeros((HALO, E), BF)

    zT = mm(eye(LT), r.z[...], NT).astype(BF)
    row = iota((LT, E), 0)
    peT = jnp.where(row < AT_DT, mm(zT, r.il[...]), 0.0)
    peT = peT + jnp.where((row >= AT_DT) & (row < AT_A), mm(zT, r.gz[...]), 0.0)
    rr, cc = iota((LT, 64), 0), iota((LT, 64), 1)
    hi, lo = split(r.alog[...])
    fold = onehot((rr >= AT_A) & (rr - AT_A == (cc >> 2)))
    rate = jnp.concatenate(
        [jnp.zeros((AT_A, E), F32), r.rate[...], jnp.zeros((LT - AT_A - N, E), F32)], 0
    )
    peT = peT + (mm(fold, hi) + mm(fold, lo)) * rate
    rr, cc = iota((LT, 64), 0), iota((LT, 64), 1)
    hi, lo = split(r.acc[...])
    fold = onehot((rr >= AT_SMALL) & (rr - AT_SMALL == (cc >> 3)))
    peT = peT + mm(fold, hi) + mm(fold, lo)
    r.g_out[...] = mm(r.gated[...], r.GR[...], TN)
    for c in range(0, 2 * E, 256):
        r.g_inT[c : c + 256, :] = mm(r.gp[:, c : c + 256], r.V[...], TN)

    swap = swap_of(r)
    back = onehot(placing(T, True))
    half = MB * T
    gated = mm(back, r.gated[...]).astype(BF)
    source, scale, unit = normalise(r.tok[...], gain)
    outs = mm(r.outw[...], swap).astype(BF)
    result = source + mm(gated[:half], r.outw[...]) + mm(gated[half:], outs)
    r.out[...] = result.astype(BF)
    grad = jnp.zeros((half, D), F32)
    for c in range(0, 2 * E, 256):
        g = mm(back, r.gp[HALO:, c : c + 256]).astype(BF)
        win = r.inT[c : c + 256, :]
        grad = grad + mm(g[:half], win) + mm(g[half:], mm(win, swap).astype(BF))
    gain_term = jnp.sum(grad * unit, 0, keepdims=True)
    g = grad * gain
    mrow = jnp.concatenate([r.mask[0:1, :], r.mask[1:2, :]], 1)
    keep = onehot((iota((half, half), 0) == iota((half, half), 1)) & (mrow != 0))
    r.ing[...] = scale * (g - unit * jnp.mean(g * unit, 1, keepdims=True)) + mm(keep, r.cot[...])
    if halo:
        rows = mm(r.gp[0:HALO, :E], r.inT[0:E, :])
        hi, lo = split(rows)
        rows = jnp.where(
            (iota((HALO, D), 0) & 3) < 2, rows, mm(hi, swap) + mm(lo, swap)
        )
        put = onehot(edge_place(False) | edge_place(True))
        tok = mm(put, r.edge[...])
        _, scale, unit = normalise(tok, gain)
        gain_term = gain_term + jnp.sum(rows * unit, 0, keepdims=True)
        g = rows * gain
        r.delta[...] = scale * (g - unit * jnp.mean(g * unit, 1, keepdims=True))
    r.g_gain[...] = jnp.broadcast_to(gain_term, (8, D))
    r.g_peT[...] = peT


def post_scratch(T):
    R = 4 * T
    return dict(
        acc=((64, E), F32),
        gg=((R, E), F32),
        slope=((R, E), F32),
        gco=((R + 2 * HALO, E), F32),
        il=((R, E), BF),
        gated=((R, E), BF),
        gz=((R, E), BF),
        z=((R, LT), BF),
        gp=((R + HALO, 2 * E), BF),
    )


def post_outs(T):
    return dict(
        out=((MB * T, D), BF),
        ing=((MB * T, D), F32),
        g_inT=((2 * E, D), F32),
        g_out=((E, D), F32),
        g_peT=((LT, E), F32),
        g_gain=((8, D), F32),
    )


def combine_body(r, radix, stride, first, last):
    digit = (r.place[1] // stride) % radix
    for m in range(radix):
        src = r.own if m == 0 else getattr(r, f"recv{m}")
        r.mem[m, 0:128, :] = src[0:128, :].astype(F32)
        both = src[128:144, :].astype(F32)
        r.mem[m, 128:136, :] = both[0:8] + both[8:16]
    fwd = (iota((8, LT), 0) & 3) < 2
    for half in range(2):
        asc = fwd if half == 0 else jnp.logical_not(fwd)
        place = jnp.where(asc, digit, radix - 1 - digit)
        for e in range(E // LT):
            es = lanes_of(e)
            sums = []
            for f in range(radix):
                sums.append(
                    jnp.where(
                        asc,
                        r.mem[f ^ digit, 128:136, es],
                        r.mem[(radix - 1 - f) ^ digit, 128:136, es],
                    )
                )
            before = jnp.zeros((8, LT), F32)
            for f in range(radix):
                before = before + jnp.where(f < place, sums[f], 0.0)
            old = None if first else r.spre[8 * half : 8 * half + 8, es]
            if not last:
                r.spre_new[8 * half : 8 * half + 8, es] = before if first else old + before
            for k in range(NP):
                at = slice(64 * half + 8 * k, 64 * half + 8 * k + 8)
                rk = r.r2[8 * k : 8 * k + 8, es]
                total = prefix = jnp.zeros((8, LT), F32)
                for f in range(radix):
                    part = jnp.where(
                        asc, r.mem[f ^ digit, at, es], r.mem[(radix - 1 - f) ^ digit, at, es]
                    )
                    prefix = jnp.where(place == f, total, prefix)
                    total = jnp.exp2(rk * sums[f]) * total + part
                if not first:
                    prefix = jnp.exp2(rk * old) * prefix + r.prefix[at, es]
                r.prefix_new[at, es] = prefix
                if not last:
                    r.tot[at, es] = total
            if not last and half == 0:
                whole = sums[0]
                for f in range(1, radix):
                    whole = whole + sums[f]
                r.tot[128:136, es] = whole
    if not last:
        write_element(r.element, r.tot)


def write_element(out, f32):
    out[0:128, :] = f32[0:128, :].astype(BF)
    hi, lo = split(f32[128:136, :])
    out[128:144, :] = jnp.concatenate([hi.astype(F32), lo.astype(F32)], 0).astype(BF)


def stages(count):
    stride, result = 1, []
    while stride < count:
        radix = 4 if (count // stride) % 4 == 0 else 2
        result.append((stride, radix))
        stride *= radix
    return result


ELEMENT = ((144, E), BF)


def carry_send(element, count, stage):
    stride, radix = stage
    return [
        lax.ppermute(element, "seq", [(i, i ^ (m * stride)) for i in range(count)])
        for m in range(1, radix)
    ]


def combine(place, element, received, r2, before, stage, first, last):
    stride, radix = stage
    ins = dict(place=place, own=element, r2=r2)
    for m in range(1, radix):
        ins[f"recv{m}"] = received[m - 1]
    if not first:
        ins.update(prefix=before["prefix_new"], spre=before["spre_new"])
    outs = dict(prefix_new=((128, E), F32))
    if not last:
        outs.update(spre_new=((16, E), F32), element=ELEMENT)
    scratch = dict(mem=((radix, 136, E), F32))
    if not last:
        scratch["tot"] = ((136, E), F32)
    return run(
        f"combine{stride}",
        functools.partial(
            combine_body, radix=radix, stride=stride, first=first, last=last
        ),
        ins,
        outs,
        scratch,
    )


def long_start_body(r, T, packed):
    if packed:
        unpack(r)
        r.gain[...] = gain_of(r)
    derive(r)
    prep(r, T, True)
    maps(r, T)
    scan_forward(r, T, None, False)
    scan_adjoint_local(r, T)

    def add(i, total):
        return total + r.st[pl.ds(pl.multiple_of(i * 8, 8), 8), :]

    total = lax.fori_loop(0, T // 2, add, jnp.zeros((8, E), F32))
    r.ends[128:136, :] = total + pltpu.roll(total, 4, 0)
    write_element(r.element, r.ends)


def short_start_body(r, T):
    prep(r, T, False)


def fetch_start(r, names):
    copies = []
    for i, name in enumerate(names):
        copy = pltpu.make_async_copy(getattr(r, name + "_far"), getattr(r, name), r.sems.at[i])
        copy.start()
        copies.append(copy)
    return copies


LATE = ("ip", "gate", "co", "sz", "V", "GR", "tok", "cot", "inT", "outw", "xwT", "dtw2")


def windows_body(r, T, halo, names):
    copies = fetch_start(r, names)
    maps(r, T)
    start = r.carry if halo else None
    scan_forward(r, T, start, True)
    scan_backward(r, T, start)
    for copy in copies:
        copy.wait()
    post(r, T, halo)
    if halo:
        finish_grads(r)


def finish_grads(r):
    g_inT, g_out = r.g_inT, r.g_out
    g_inT[...] += r.s_inT[...]
    g_out[...] += r.s_out[...]
    r.g_peT[...] += r.s_peT[...]
    r.g_gain[...] += r.s_gain[...]
    if not hasattr(r, "keep"):
        return
    lane, col = iota((D, E), 1), iota((D, E), 0)
    pick = onehot(((lane // 16) == (col // 8)) & ((lane % 16) == (col % 8)))
    peT = r.g_peT[...] + jnp.where(
        iota((LT, E), 0) == AT_SMALL + 7, mm(r.g_gain[0:1, :].astype(BF), pick), 0.0
    )
    r.pe_out[...] = peT.T.astype(BF)
    count = r.keep.shape[0] // PACK
    mine = r.place[0]
    for dst, d in ((r.keep, mine), (r.give, 1 - mine)):
        for j in range(count):
            at = j * PACK
            in_at = pl.multiple_of(d * (count * IN_ROWS) + j * IN_ROWS, IN_ROWS)
            out_at = pl.multiple_of(d * (count * OUT_ROWS) + j * OUT_ROWS, OUT_ROWS)
            for half in range(2):
                lanes = slice(half * LT, (half + 1) * LT)
                dst[at + half * IN_ROWS : at + (half + 1) * IN_ROWS, :] = g_inT[
                    pl.ds(in_at, IN_ROWS), lanes
                ].astype(BF)
                low = at + 2 * IN_ROWS + half * OUT_ROWS
                dst[low : low + OUT_ROWS, :] = g_out[pl.ds(out_at, OUT_ROWS), lanes].astype(BF)
            dst[at + PACK - CH_ROWS : at + PACK, :] = r.pe_out[pl.ds(out_at, CH_ROWS), :]


def final_body(r, packed):
    r.grad[...] = r.ing[...]
    T = r.grad.shape[0] // MB
    for mb in range(MB):
        for j in range(4):
            row = mb * T + T - 4 + j
            r.grad[row : row + 1, :] += r.from_next[4 * j + mb : 4 * j + mb + 1, :]
            row = mb * T + 3 - j
            r.grad[row : row + 1, :] += r.from_prev[4 * j + 2 + mb : 4 * j + 3 + mb, :]
    if not packed:
        return
    count = r.parts.shape[0] // PACK
    total = r.parts[0:PACK, :].astype(F32)
    for j in range(1, count):
        total = total + r.parts[j * PACK : (j + 1) * PACK, :].astype(F32)
    for half in range(2):
        lanes = slice(half * LT, (half + 1) * LT)
        hi, lo = split(total[half * IN_ROWS : (half + 1) * IN_ROWS])
        r.in_w[lanes, :] = mm(eye(LT), hi, NT) + mm(eye(LT), lo, NT)
        low = 2 * IN_ROWS + half * OUT_ROWS
        r.out_w[:, lanes] = total[low : low + OUT_ROWS]
    pe = total[PACK - CH_ROWS :]
    hi, lo = split(pe)
    peT = mm(eye(LT), hi, NT) + mm(eye(LT), lo, NT)
    r.x_w[...] = pe[:, : 3 * N]
    r.a_log[...] = pe[:, AT_A : AT_A + N]
    r.dt_w[...] = peT[AT_DT : AT_DT + N]
    small = peT[AT_SMALL : AT_SMALL + 8]
    r.conv_w[...] = small[0:4]
    r.conv_b[...] = small[4:5]
    r.dt_b[...] = small[5:6]
    r.skip[...] = small[6:7]
    r.gain[...] = small[7:8, 0 : r.gain.shape[1]]


PREP_OUTS = ("V", "GR", "ip", "gate", "co", "st", "sz", "si", "gm", "sel")


def prep_outs(T):
    R = 4 * T
    wide = ((R, E), F32)
    return dict(
        V=((R + HALO, D), BF),
        GR=((R, D), BF),
        ip=((R + HALO, E), F32),
        gate=wide,
        co=wide,
        st=wide,
        sz=wide,
        si=wide,
        gm=wide,
        sel=((R, LT), F32),
    )


def local(
    long_tokens,
    short_tokens,
    long_cotangent,
    short_cotangent,
    long_mask,
    short_mask,
    complement,
    norm_gain,
    in_weight,
    conv_weight,
    conv_bias,
    x_weight,
    dt_weight,
    dt_bias,
    a_log,
    d_skip,
    out_weight,
):
    count = lax.axis_size("seq")
    span, short = long_tokens.shape[2], short_tokens.shape[2]
    packed = out_weight.shape[0] == OUT_ROWS and in_weight.shape[1] == IN_ROWS
    place = jnp.stack([lax.axis_index("dp"), lax.axis_index("seq")]).astype(jnp.int32)
    comp = complement.reshape(1, D)
    up = [(i, i + 1) for i in range(count - 1)]
    down = [(i + 1, i) for i in range(count - 1)]

    tail = lax.ppermute(long_tokens[:, 0, span - 4 :, :].reshape(8, D), "seq", up)
    head = lax.ppermute(long_tokens[:, 0, :4, :].reshape(8, D), "seq", down)
    edge = jnp.concatenate([tail, head], 0)
    if packed:
        buf = run(
            "pack",
            pack_body,
            dict(
                gain=norm_gain.reshape(1, -1),
                in_w=in_weight,
                conv_w=conv_weight,
                conv_b=conv_bias.reshape(1, -1),
                x_w=x_weight,
                dt_w=dt_weight,
                dt_b=dt_bias.reshape(1, -1),
                a_log=a_log,
                skip=d_skip.reshape(1, -1),
                out_w=out_weight,
            ),
            dict(buf=((count * PACK, LT), BF)),
            dict(rows=((8, CH_ROWS), F32)),
        )["buf"]
        mine = lax.all_to_all(buf, "seq", 0, 0, tiled=True)
        other = lax.ppermute(mine, "dp", [(0, 1), (1, 0)])
        weights_in = dict(mine=mine, other=other)
    else:

        def whole(a, axis):
            return lax.all_gather(a, BOTH, axis=axis, tiled=True)

        small = jnp.stack([*conv_weight, conv_bias, dt_bias, d_skip, jnp.zeros_like(d_skip)])
        columns = jnp.concatenate([a_log, small.T], 1)
        hi = columns.astype(BF)
        lo = (columns - hi.astype(F32)).astype(BF)
        zero = jnp.zeros((columns.shape[0], LT - AT_SMALL - 16), BF)
        chan = jnp.concatenate(
            [x_weight, dt_weight.T, hi[:, :N], lo[:, :N], hi[:, N:], lo[:, N:], zero], 1
        )
        weights_in = dict(
            inT=whole(in_weight.T, 0),
            outw=whole(out_weight, 0),
            pe=whole(chan, 0),
            gain=whole(norm_gain, 0).reshape(1, D),
        )

    def tokens_of(tok, cot, mask):
        T = tok.shape[2]
        return dict(
            tok=tok.reshape(MB * T, D), cot=cot.reshape(MB * T, D), mask=mask.reshape(MB, T)
        )

    long_in = tokens_of(long_tokens, long_cotangent, long_mask)
    short_in = tokens_of(short_tokens, short_cotangent, short_mask)

    derived = dict(
        r2=((8 * NP, E), F32),
        rowp=((8, E), F32),
        rate=((N, E), F32),
        dtw2=((LT, E), BF),
        xwT=((LT, E), BF),
    )
    unpacked = dict(inT=((2 * E, D), BF), outw=((E, D), BF), pe=((E, LT), BF), gain=((8, D), F32))
    started = run(
        "long_start",
        functools.partial(long_start_body, T=span, packed=packed),
        dict(place=place, comp=comp, edge=edge, **long_in, **weights_in),
        dict(
            element=ELEMENT, **prep_outs(span), **derived, **(unpacked if packed else {})
        ),
        dict(
            il=((4 * span, E), BF),
            imb=((8 * span, NP * LT), F32),
            omb=((8 * span, NP * LT), F32),
            ends=((136, E), F32),
        ),
        flops=1 << 33,
    )
    weights = {k: started[k] for k in derived}
    for k in unpacked:
        weights[k] = started[k] if packed else weights_in[k]

    plan = stages(count)
    element, before = started["element"], None
    received = carry_send(element, count, plan[0])
    prepared = run(
        "short_start",
        functools.partial(short_start_body, T=short),
        dict(comp=comp, **short_in, **{k: weights[k] for k in ("inT", "outw", "pe", "gain", "dtw2", "rowp")}),
        prep_outs(short),
        dict(il=((4 * short, E), BF)),
        flops=1 << 33,
    )

    def windows(name, T, halo, prep_out, inputs, extra, outs_more):
        ins = dict(
            comp=comp,
            mask=inputs["mask"],
            **{k: weights[k] for k in ("r2", "rowp", "rate", "gain")},
            **{k: prep_out[k] for k in ("st", "si", "gm", "sel")},
            **extra,
        )
        late = dict(
            {k: prep_out[k] for k in ("ip", "gate", "co", "sz", "V", "GR")},
            tok=inputs["tok"],
            cot=inputs["cot"],
            **{k: weights[k] for k in ("inT", "outw", "xwT", "dtw2")},
        )
        for k in ("s_inT", "s_out", "s_peT", "s_gain"):
            if k in ins:
                late[k] = ins.pop(k)
        ins.update({k + "_far": v for k, v in late.items()})
        names = tuple(late)
        return run(
            name,
            functools.partial(windows_body, T=T, halo=halo, names=names),
            ins,
            dict(post_outs(T), **outs_more),
            dict(
                scan_scratch(T),
                **post_scratch(T),
                **{k: (v.shape, v.dtype) for k, v in late.items()},
                sems=pltpu.SemaphoreType.DMA((len(names),)),
                **(dict(pe_out=((E, LT), BF)) if halo and packed else {}),
            ),
            flops=1 << 35,
            far=tuple(k + "_far" for k in names),
        )

    for at, stage in enumerate(plan[:-1]):
        before = combine(place, element, received, weights["r2"], before, stage, at == 0, False)
        element = before["element"]
        received = carry_send(element, count, plan[at + 1])
    shorts = windows("short_windows", short, False, prepared, short_in, {}, {})
    last = len(plan) - 1
    carry = combine(
        place, element, received, weights["r2"], before, plan[last], last == 0, True
    )["prefix_new"]
    more = dict(delta=((HALO, D), F32))
    if packed:
        more.update(keep=((count * PACK, LT), BF), give=((count * PACK, LT), BF))
    longs = windows(
        "long_windows",
        span,
        True,
        started,
        long_in,
        dict(
            place=place,
            carry=carry,
            edge=edge,
            s_inT=shorts["g_inT"],
            s_out=shorts["g_out"],
            s_peT=shorts["g_peT"],
            s_gain=shorts["g_gain"],
        ),
        more,
    )
    from_next = lax.ppermute(longs["delta"], "seq", down)
    from_prev = lax.ppermute(longs["delta"], "seq", up)
    ins = dict(ing=longs["ing"], from_next=from_next, from_prev=from_prev)
    outs = dict(grad=((MB * span, D), F32))
    if packed:
        got = lax.ppermute(longs["give"], "dp", [(0, 1), (1, 0)])
        ins["parts"] = lax.all_to_all(longs["keep"] + got, "seq", 0, 0, tiled=True)
        outs.update(
            gain=((1, D // (2 * count)), F32),
            in_w=((D, IN_ROWS), F32),
            conv_w=((4, CH_ROWS), F32),
            conv_b=((1, CH_ROWS), F32),
            x_w=((CH_ROWS, 3 * N), F32),
            dt_w=((N, CH_ROWS), F32),
            dt_b=((1, CH_ROWS), F32),
            a_log=((CH_ROWS, N), F32),
            skip=((1, CH_ROWS), F32),
            out_w=((OUT_ROWS, D), F32),
        )
    done = run("final", functools.partial(final_body, packed=packed), ins, outs)
    if packed:
        grads = {k: done[k] for k in outs if k != "grad"}
        for k in ("gain", "conv_b", "dt_b", "skip"):
            grads[k] = grads[k].reshape(-1)
    else:

        def own(a, axis=0):
            return lax.psum_scatter(a, BOTH, scatter_dimension=axis, tiled=True)

        pe = own(longs["g_peT"].T)
        grads = dict(
            gain=own(longs["g_gain"][0]),
            in_w=own(longs["g_inT"]).T,
            conv_w=pe[:, AT_SMALL : AT_SMALL + 4].T,
            conv_b=pe[:, AT_SMALL + 4],
            x_w=pe[:, : 3 * N],
            dt_w=pe[:, AT_DT : AT_DT + N].T,
            dt_b=pe[:, AT_SMALL + 5],
            a_log=pe[:, AT_A : AT_A + N],
            skip=pe[:, AT_SMALL + 6],
            out_w=own(longs["g_out"]),
        )
    order = ("gain", "in_w", "conv_w", "conv_b", "x_w", "dt_w", "dt_b", "a_log", "skip", "out_w")
    return (
        longs["out"].reshape(long_tokens.shape),
        shorts["out"].reshape(short_tokens.shape),
        done["grad"].reshape(long_tokens.shape),
        shorts["ing"].reshape(short_tokens.shape),
    ) + tuple(grads[k] for k in order)


def solution(mesh):
    long_spec, short_spec = P(None, "dp", "seq", None), P(None, BOTH, None, None)
    rows, columns, vector = P(BOTH, None), P(None, BOTH), P(BOTH)
    params = (vector, columns, columns, vector, rows, columns, vector, rows, vector, rows)
    return jax.shard_map(
        local,
        mesh=mesh,
        in_specs=(
            long_spec,
            short_spec,
            long_spec,
            short_spec,
            P(None, "dp", "seq"),
            P(None, BOTH, None),
            P(),
        )
        + params,
        out_specs=(long_spec, short_spec, long_spec, short_spec) + params,
        check_vma=False,
    )
```

```python
import functools
import types

import jax
import jax.numpy as jnp
from jax import lax
from jax.experimental import pallas as pl
from jax.experimental.pallas import tpu as pltpu
from jax.sharding import PartitionSpec as P

EPS = 1e-05
D, E, N, MB, HALO = 256, 512, 16, 2, 16
LT = 128
NP = N // 2
LOG2E = 1.4426950408889634
LN2 = 0.6931471805599453
F32, BF = jnp.float32, jnp.bfloat16
NT = (((1,), (1,)), ((), ()))
TN = (((0,), (0,)), ((), ()))
BOTH = ("dp", "seq")
IN_ROWS, OUT_ROWS, CH_ROWS = 32, 16, 16
PACK = 2 * IN_ROWS + 2 * OUT_ROWS + CH_ROWS
EDGE = 16
BLOCK = PACK + EDGE
AT_DT, AT_A, AT_SMALL = 48, 64, 96


def mm(a, b, dims=None):
    if dims is None:
        return jnp.dot(a, b, preferred_element_type=F32)
    return lax.dot_general(a, b, dims, preferred_element_type=F32)


def iota(shape, axis):
    return lax.broadcasted_iota(jnp.int32, shape, axis)


def onehot(cond):
    return jnp.where(cond, 1.0, 0.0).astype(BF)


def eye(n):
    return onehot(iota((n, n), 0) == iota((n, n), 1))


def split(x):
    hi = x.astype(BF)
    return hi, (x - hi.astype(F32)).astype(BF)


def sigmoid(x):
    return 0.5 * jnp.tanh(0.5 * x) + 0.5


def loop(count, body):
    lax.fori_loop(0, count, lambda i, c: (body(i), c)[1], 0)


def run(name, body, ins, outs, scratch=None, flops=0, far=(), early=(), vmem=60):
    scratch = dict(scratch or {}, **{k: outs[k] for k in early})
    if early:
        scratch["out_sems"] = pltpu.SemaphoreType.DMA((len(early),))
    in_names, scratch_names = list(ins), list(scratch)
    out_names = [k + "_out" if k in early else k for k in outs]

    def kernel(*refs):
        r = types.SimpleNamespace(**dict(zip(in_names + out_names + scratch_names, refs)))
        r.early = tuple(early)
        body(r)

    def spec(key):
        return pl.BlockSpec(memory_space=pl.ANY if key in far else pltpu.VMEM)

    result = pl.pallas_call(
        kernel,
        out_shape=tuple(jax.ShapeDtypeStruct(*v) for v in outs.values()),
        in_specs=[spec(k) for k in in_names],
        out_specs=tuple(
            pl.BlockSpec(memory_space=pl.ANY if k in early else pltpu.VMEM) for k in outs
        ),
        scratch_shapes=[
            pltpu.VMEM(*scratch[k]) if isinstance(scratch[k], tuple) else scratch[k]
            for k in scratch_names
        ],
        compiler_params=pltpu.CompilerParams(vmem_limit_bytes=vmem << 20),
        cost_estimate=pl.CostEstimate(flops=flops, bytes_accessed=1 << 20, transcendentals=0),
        name=name,
    )(*[ins[k] for k in in_names])
    return dict(zip(outs, result))


def send(r, names):
    copies = []
    for name in names:
        at = r.early.index(name)
        copy = pltpu.make_async_copy(getattr(r, name), getattr(r, name + "_out"), r.out_sems.at[at])
        copy.start()
        copies.append(copy)
    return copies


def pack_body(r):
    r.rows[...] = jnp.zeros((8, CH_ROWS), F32)
    r.rows[0:4, :] = r.conv_w[...]
    r.rows[4:5, :] = r.conv_b[...]
    r.rows[5:6, :] = r.dt_b[...]
    r.rows[6:7, :] = r.skip[...]
    r.rows[7:8, 0 : r.gain.shape[1]] = r.gain[...]
    in_t = r.in_wT[...]
    small = jnp.concatenate(split(r.rows[...]), 0)
    id16 = eye(CH_ROWS)

    def place(a, at):
        n = a.shape[1]
        return mm(a.astype(BF), onehot(iota((n, LT), 0) + at == iota((n, LT), 1)))

    a_hi, a_lo = split(r.a_log[...])
    chan = (
        place(r.x_w[...], 0)
        + place(mm(id16, r.dt_w[...], NT), AT_DT)
        + place(a_hi, AT_A)
        + place(a_lo, AT_A + N)
        + place(mm(id16, small, NT), AT_SMALL)
    ).astype(BF)
    out_w = r.out_w[...]
    count = r.buf.shape[0] // BLOCK
    for j in range(count):
        at = j * BLOCK
        for half in range(2):
            lanes = slice(half * LT, (half + 1) * LT)
            r.buf[at + half * IN_ROWS : at + (half + 1) * IN_ROWS, :] = in_t[:, lanes]
            low = at + 2 * IN_ROWS + half * OUT_ROWS
            r.buf[low : low + OUT_ROWS, :] = out_w[:, lanes]
        r.buf[at + PACK - CH_ROWS : at + PACK, :] = chan
        r.buf[at + PACK : at + BLOCK, :] = jnp.zeros((EDGE, LT), BF)
    T = r.tok.shape[0] // MB

    def edge(first):
        rows = [r.tok[mb * T + first : mb * T + first + 16, :].astype(F32) for mb in range(MB)]
        at = 12 if first else 0
        return jnp.concatenate([x[at : at + 4] for x in rows], 0)

    put_edges(r.buf, edge(T - 16), edge(0))


def put_edges(buf, to_next, to_prev):
    seq = lax.axis_index("seq")
    count = buf.shape[0] // BLOCK

    def halves(x):
        return jnp.concatenate([x[:, :LT], x[:, LT:]], 0).astype(BF)

    @pl.when(seq < count - 1)
    def _():
        buf[pl.ds(pl.multiple_of((seq + 1) * BLOCK + PACK, 16), EDGE), :] = halves(to_next)

    @pl.when(seq > 0)
    def _():
        buf[pl.ds(pl.multiple_of((seq - 1) * BLOCK + PACK, 16), EDGE), :] = halves(to_prev)


def get_edges(buf):
    seq = lax.axis_index("seq")
    count = buf.shape[0] // BLOCK
    result = []
    for j, there in ((jnp.maximum(seq - 1, 0), seq > 0), (jnp.minimum(seq + 1, count - 1), seq < count - 1)):
        x = buf[pl.ds(pl.multiple_of(j * BLOCK + PACK, 16), EDGE), :].astype(F32)
        x = jnp.concatenate([x[:8], x[8:]], 1)
        result.append(jnp.where(there, x, 0.0))
    return result


def unpack(r):
    count = r.mine.shape[0] // BLOCK
    mine_at = lax.axis_index("dp")
    r.edge[...] = jnp.concatenate(get_edges(r.mine), 0).astype(BF)
    for src, d in ((r.mine, mine_at), (r.other, 1 - mine_at)):
        for j in range(count):
            at = j * BLOCK
            in_at = pl.multiple_of(d * (count * IN_ROWS) + j * IN_ROWS, IN_ROWS)
            out_at = pl.multiple_of(d * (count * OUT_ROWS) + j * OUT_ROWS, OUT_ROWS)
            for half in range(2):
                lanes = slice(half * LT, (half + 1) * LT)
                r.inT[pl.ds(in_at, IN_ROWS), lanes] = src[
                    at + half * IN_ROWS : at + (half + 1) * IN_ROWS, :
                ]
                low = at + 2 * IN_ROWS + half * OUT_ROWS
                r.outw[pl.ds(out_at, OUT_ROWS), lanes] = src[low : low + OUT_ROWS, :]
            r.pe[pl.ds(out_at, CH_ROWS), :] = src[at + PACK - CH_ROWS : at + PACK, :]


def derive(r):
    peT = mm(eye(LT), r.pe[...], NT)
    small = peT[AT_SMALL : AT_SMALL + 8] + peT[AT_SMALL + 8 : AT_SMALL + 16]
    r.rowp[...] = small
    rate = -jnp.exp(peT[AT_A : AT_A + N] + peT[AT_A + N : AT_A + 2 * N])
    r.rate[...] = rate
    for n in range(N):
        r.r2[4 * n : 4 * n + 4, :] = jnp.broadcast_to(rate[n : n + 1] * LOG2E, (4, E))
    dt = peT[AT_DT : AT_DT + N]
    r.dtw2[...] = jnp.concatenate([dt, dt, jnp.zeros((LT - 2 * N, E), F32)], 0).astype(BF)
    r.xwT[...] = jnp.where(iota((LT, E), 0) < 3 * N, peT, 0.0).astype(BF)


def gain_of(r):
    per = E // (D // 8)
    low = mm(eye(LT), r.pe[...], NT)[AT_SMALL : AT_SMALL + 16].astype(BF)
    lane, col = iota((E, D), 0), iota((E, D), 1)
    pick = onehot(((lane // per) == (col // 8)) & ((lane % per) == (col % 8)))
    g = mm(low, pick)
    return g[0:8] + g[8:16]


def placing(T, transposed):
    shape = (2 * MB * T, 2 * MB * T)
    row, col = iota(shape, 1 if transposed else 0), iota(shape, 0 if transposed else 1)
    t, scan = row >> 2, row & 3
    turn = T.bit_length() - 1
    pos, src = col & (T - 1), col >> turn
    want = jnp.where(scan >= 2, T - 1 - t, t)
    return (src == scan) & (pos == want)


def gain_row(r):
    return r.gain[0:1, :] if r.gain.shape[0] == 1 else r.gain[7:8, :]


def normalise(tok):
    source = tok.astype(F32)
    scale = lax.rsqrt(jnp.mean(source * source, 1, keepdims=True) + EPS)
    return source, scale, source * scale


def swap_of(r):
    return onehot(iota((D, D), 0) == jnp.broadcast_to(r.comp[...], (D, D)))


def prep(r, T, halo):
    R = 4 * T
    gain = gain_row(r)
    swap = swap_of(r)
    _, _, unit = normalise(r.tok[...])
    normed = (unit * gain).astype(BF)
    put = placing(T, False)
    r.V[HALO:, :] = mm(
        onehot(put), jnp.concatenate([normed, mm(normed, swap).astype(BF)], 0)
    ).astype(BF)
    mrow = jnp.concatenate([r.mask[0:1, :], r.mask[1:2, :]], 1)
    mrow = jnp.concatenate([mrow, mrow], 1)
    cot = r.cot[...]
    r.GR[...] = mm(
        onehot(put & (mrow != 0)), jnp.concatenate([cot, mm(cot, swap).astype(BF)], 0)
    ).astype(BF)
    if halo:
        hn = (normalise(r.edge[...])[2] * gain).astype(BF)
        r.V[0:HALO, :] = (
            mm(onehot(edge_place(False)), hn)
            + mm(onehot(edge_place(True)), mm(hn, swap).astype(BF))
        ).astype(BF)
        r.ip[0:HALO, :] = mm(r.V[0:HALO, :], r.inT[0:E, :], NT)
    else:
        r.V[0:HALO, :] = jnp.zeros((HALO, D), BF)
        r.ip[0:HALO, :] = jnp.zeros((HALO, E), F32)
    for c in range(0, E, 256):
        r.ip[HALO:, c : c + 256] = mm(r.V[HALO:, :], r.inT[c : c + 256, :], NT)
        r.gate[:, c : c + 256] = mm(r.V[HALO:, :], r.inT[E + c : E + c + 256, :], NT)
        r.gm[:, c : c + 256] = mm(r.GR[...], r.outw[c : c + 256, :], NT)
    w = [r.rowp[k : k + 1, :] for k in range(4)]
    conv_b, dt_b = r.rowp[4:5, :], r.rowp[5:6, :]
    B = 32

    def first(i):
        r0 = pl.multiple_of(i * B, B)
        x = r.ip[pl.ds(r0, B + HALO), :]
        total = conv_b
        for k in range(4):
            total = total + w[k] * x[4 + 4 * k : 4 + 4 * k + B]
        r.co[pl.ds(r0, B), :] = total
        inner = total * sigmoid(total)
        r.si[pl.ds(r0, B), :] = inner
        r.il[pl.ds(r0, B), :] = inner.astype(BF)
        g = r.gate[pl.ds(r0, B), :]
        r.gm[pl.ds(r0, B), :] = r.gm[pl.ds(r0, B), :] * (g * sigmoid(g))

    loop(R // B, first)
    sel = mm(r.il[...], r.pe[...])
    r.sel[...] = sel
    lane = iota((R, LT), 1)
    low = jnp.where(lane < N, sel, 0.0)
    hi = low.astype(BF).astype(F32)
    both = (hi + pltpu.roll(low - hi, N, 1)).astype(BF)
    for c in range(0, E, 256):
        r.st[:, c : c + 256] = mm(both, r.dtw2[:, c : c + 256])

    def second(i):
        r0 = pl.multiple_of(i * B, B)
        z = r.st[pl.ds(r0, B), :] + dt_b
        u = jnp.exp(-jnp.abs(z))
        inv = 1.0 / (1.0 + u)
        near = u * (1.0 - u * (0.5 - u * (1.0 / 3.0)))
        st = jnp.maximum(z, 0.0) + jnp.where(u < 0.01, near, jnp.log(1.0 + u))
        r.sz[pl.ds(r0, B), :] = jnp.where(z >= 0, inv, u * inv)
        r.st[pl.ds(r0, B), :] = st
        r.si[pl.ds(r0, B), :] = r.si[pl.ds(r0, B), :] * st

    loop(R // B, second)


def edge_place(rev):
    row, col = iota((HALO, HALO), 0), iota((HALO, HALO), 1)
    j, scan = row >> 2, row & 3
    if rev:
        return (scan >= 2) & (col == 8 + (scan - 2) * 4 + (3 - j))
    return (scan < 2) & (col == scan * 4 + j)


def maps(r, T):
    R = 4 * T
    sel = r.sel[...]
    lane = iota((R, LT), 1)
    kept = jnp.where((lane >= N) & (lane < 3 * N), sel, 0.0)
    hi = kept.astype(BF).astype(F32)
    both = (hi + pltpu.roll(kept - hi, 64, 1)).astype(BF)
    G = 128
    r8, r4 = iota((2 * G, G), 0), iota((2 * G, G), 1)
    twice = onehot(((r8 >> 3) * 4 + (r8 & 3)) == r4)
    own = (iota((2 * G, LT), 1) & 1) == ((iota((2 * G, LT), 0) >> 2) & 1)
    l, c = iota((LT, NP * LT), 0), iota((LT, NP * LT), 1)
    l = l & 63
    spread_in = onehot((l >= N) & (l < 2 * N) & (((l - N) >> 1) == (c >> 7)))
    spread_out = onehot((l >= 2 * N) & (l < 3 * N) & (((l - 2 * N) >> 1) == (c >> 7)))
    for g in range(R // G):
        left = jnp.where(own, mm(twice, both[g * G : (g + 1) * G]), 0.0).astype(BF)
        r.imb[g * 2 * G : (g + 1) * 2 * G, :] = mm(left, spread_in)
        r.omb[g * 2 * G : (g + 1) * 2 * G, :] = mm(left, spread_out)


def dup(x, low):
    turned = pltpu.roll(x, 4, 0)
    return jnp.where(low, x, turned), jnp.where(low, turned, x)


def lanes_of(e):
    return slice(e * LT, (e + 1) * LT)


def scan_forward(r, T, start, full, U=16):
    low = iota((8, LT), 0) < 4
    for e in range(E // LT):
        es = lanes_of(e)
        if start is None:
            first = tuple(jnp.zeros((8, LT), F32) for _ in range(NP))
        else:
            first = tuple(start[8 * k : 8 * k + 8, es] for k in range(NP))
        if full:
            for k in range(NP):
                r.states[0, 8 * k : 8 * k + 8, es] = first[k]

        def body(i, state):
            state = list(state)
            for u in range(U // 2):
                pair = i * (U // 2) + u
                row = pl.multiple_of(pair * 8, 8)
                st = dup(r.st[pl.ds(row, 8), es], low)
                si = dup(r.si[pl.ds(row, 8), es], low)
                ys = []
                for h in range(2):
                    t = pair * 2 + h
                    r8 = pl.multiple_of(t * 8, 8)
                    acc = None
                    for k in range(NP):
                        decay = jnp.exp2(st[h] * r.r2[8 * k : 8 * k + 8, es])
                        state[k] = decay * state[k] + si[h] * r.imb[pl.ds(r8, 8), lanes_of(k)]
                        if full:
                            r.states[t + 1, 8 * k : 8 * k + 8, es] = state[k]
                            y = state[k] * r.omb[pl.ds(r8, 8), lanes_of(k)]
                            acc = y if acc is None else acc + y
                    if full:
                        ys.append(acc + pltpu.roll(acc, 4, 0))
                if full:
                    r.mix[pl.ds(row, 8), es] = jnp.where(low, ys[0], ys[1])
            return tuple(state)

        last = lax.fori_loop(0, T // U, body, first)
        if not full:
            for k in range(NP):
                r.ends[8 * k : 8 * k + 8, es] = last[k]


def scan_adjoint_local(r, T, U=8):
    low = iota((8, LT), 0) < 4
    for e in range(E // LT):
        es = lanes_of(e)

        def body(i, b):
            b = list(b)
            for u in range(U // 2):
                pair = T // 2 - 1 - (i * (U // 2) + u)
                row = pl.multiple_of(pair * 8, 8)
                st = dup(r.st[pl.ds(row, 8), es], low)
                gm = dup(r.gm[pl.ds(row, 8), es], low)
                for h in (1, 0):
                    r8 = pl.multiple_of((pair * 2 + h) * 8, 8)
                    for k in range(NP):
                        a = gm[h] * r.omb[pl.ds(r8, 8), lanes_of(k)] + b[k]
                        b[k] = jnp.exp2(st[h] * r.r2[8 * k : 8 * k + 8, es]) * a
            return tuple(b)

        last = lax.fori_loop(0, T // U, body, tuple(jnp.zeros((8, LT), F32) for _ in range(NP)))
        for k in range(NP):
            r.ends[64 + 8 * k : 64 + 8 * k + 8, es] = last[k]


def scan_backward(r, T, start, group=2, unroll=4):
    low = iota((8, LT), 0) < 4
    r.alog[...] = jnp.zeros((8 * NP, E), F32)
    r.b[...] = jnp.zeros((8 * NP, E), F32) if start is None else start[64:128, :]
    groups = E // LT // group
    for g in range(groups):
        tiles = [lanes_of(g * group + e) for e in range(group)]

        def body(i, g=g, tiles=tiles):
            for u in range(unroll):
                pair = T // 2 - 1 - (i * unroll + u)
                row = pl.multiple_of(pair * 8, 8)
                r16 = pl.multiple_of(pair * 16, 16)
                st = [dup(r.st[pl.ds(row, 8), es], low) for es in tiles]
                si = [dup(r.si[pl.ds(row, 8), es], low) for es in tiles]
                gm = [dup(r.gm[pl.ds(row, 8), es], low) for es in tiles]
                q = [[0.0, 0.0] for _ in tiles]
                p = [[0.0, 0.0] for _ in tiles]
                for k in range(NP):
                    ks = slice(8 * k, 8 * k + 8)
                    im = [r.imb[pl.ds(r16 + 8 * h, 8), lanes_of(k)] for h in range(2)]
                    om = [r.omb[pl.ds(r16 + 8 * h, 8), lanes_of(k)] for h in range(2)]
                    xi, xo = [0.0, 0.0], [0.0, 0.0]
                    for e, es in enumerate(tiles):
                        rk = r.r2[ks, es]
                        b = r.b[ks, es]
                        states = [r.states[2 * pair + h, ks, es] for h in range(3)]
                        rates = 0.0
                        for h in (1, 0):
                            a = gm[e][h] * om[h] + b
                            b = jnp.exp2(st[e][h] * rk) * a
                            w = b * states[h]
                            q[e][h] = w * rk + q[e][h]
                            rates = w * st[e][h] + rates
                            p[e][h] = a * im[h] + p[e][h]
                            xi[h] = a * si[e][h] + xi[h]
                            xo[h] = states[h + 1] * gm[e][h] + xo[h]
                        r.b[ks, es] = b
                        r.alog[ks, es] += rates
                    cs = lanes_of(g * NP + k)
                    r.xi[pl.ds(r16, 16), cs] = jnp.concatenate(xi, 0).astype(BF)
                    r.xo[pl.ds(r16, 16), cs] = jnp.concatenate(xo, 0).astype(BF)
                for e, es in enumerate(tiles):
                    for out, v in ((r.q, q[e]), (r.p, p[e])):
                        v = [x + pltpu.roll(x, 4, 0) for x in v]
                        out[pl.ds(row, 8), es] = jnp.where(low, v[0], v[1])

        loop(T // 2 // unroll, body)
    rl, rc = iota((NP * LT, LT), 0), iota((NP * LT, LT), 1)
    red = onehot((rl >> 7) == (rc >> 1))
    W = NP * LT
    for out, x in ((r.yi, r.xi), (r.yo, r.xo)):
        total = x[:, :W]
        for g in range(1, groups):
            total = total + x[:, g * W : (g + 1) * W]
        out[...] = mm(total, red)
    G = 256
    own = (iota((G, LT), 1) & 1) == ((iota((G, LT), 0) >> 2) & 1)
    valid = own & (iota((G, LT), 1) < N)
    r8, r4 = iota((G // 2, G), 1), iota((G // 2, G), 0)
    fold = onehot(((r8 >> 3) * 4 + (r8 & 3)) == r4)
    for g in range(8 * T // G):
        at = slice(g * G, (g + 1) * G)
        y = pltpu.roll(jnp.where(valid, r.yi[at, :], 0.0), N, 1) + pltpu.roll(
            jnp.where(valid, r.yo[at, :], 0.0), 2 * N, 1
        )
        hi, lo = split(y)
        r.gsel[g * G // 2 : (g + 1) * G // 2, :] = mm(fold, hi) + mm(fold, lo)


def scan_scratch(T):
    return dict(
        states=((T + 1, 8 * NP, E), F32),
        imb=((8 * T, NP * LT), F32),
        omb=((8 * T, NP * LT), F32),
        xi=((8 * T, 2 * NP * LT), BF),
        xo=((8 * T, 2 * NP * LT), BF),
        b=((8 * NP, E), F32),
        yi=((8 * T, LT), F32),
        yo=((8 * T, LT), F32),
        mix=((4 * T, E), F32),
        q=((4 * T, E), F32),
        p=((4 * T, E), F32),
        alog=((8 * NP, E), F32),
        gsel=((4 * T, LT), F32),
    )


def post(r, T, halo):
    R = 4 * T
    B = 32
    w = [r.rowp[k : k + 1, :] for k in range(4)]
    skip = r.rowp[6:7, :]
    r.acc[...] = jnp.zeros((64, E), F32)
    for c in range(0, E, 256):
        r.gg[:, c : c + 256] = mm(r.GR[...], r.outw[c : c + 256, :], NT)

    def fold8(x):
        total = x[0:8]
        for j in range(8, x.shape[0], 8):
            total = total + x[j : j + 8]
        return total

    def first(i):
        r0 = pl.multiple_of(i * B, B)
        at = pl.ds(r0, B)
        co, gate, st, gm, p = r.co[at, :], r.gate[at, :], r.st[at, :], r.gm[at, :], r.p[at, :]
        sg = sigmoid(co)
        inner = co * sg
        r.il[at, :] = inner.astype(BF)
        mixed = r.mix[at, :] + skip * inner
        gs = sigmoid(gate)
        silu_gate = gate * gs
        r.gated[at, :] = (mixed * silu_gate).astype(BF)
        r.gp[pl.ds(HALO + r0, B), E:] = (r.gg[at, :] * mixed * (gs + silu_gate * (1.0 - gs))).astype(
            BF
        )
        gz = (r.q[at, :] * LN2 + inner * p) * r.sz[at, :]
        r.gz[at, :] = gz.astype(BF)
        r.acc[40:48, :] += fold8(gz)
        r.acc[48:56, :] += fold8(gm * inner)
        r.gg[at, :] = st * p + gm * skip
        r.slope[at, :] = sg + inner * (1.0 - sg)

    loop(R // B, first)
    lane = iota((R, LT), 1)
    gs_low = jnp.where(lane < N, mm(r.gz[...], r.dtw2[...], NT), r.gsel[...])
    gs_low = jnp.where(lane < 3 * N, gs_low, 0.0)
    r.z[...] = (
        gs_low
        + jnp.where((lane >= AT_DT) & (lane < AT_DT + N), pltpu.roll(r.sel[...], AT_DT, 1), 0.0)
    ).astype(BF)
    gsb = gs_low.astype(BF)
    for c in range(0, E, 256):
        r.mix[:, c : c + 256] = mm(gsb, r.xwT[:, c : c + 256])
    r.gco[0:HALO, :] = jnp.zeros((HALO, E), F32)
    r.gco[HALO + R :, :] = jnp.zeros((HALO, E), F32)

    def second(i):
        r0 = pl.multiple_of(i * B, B)
        at = pl.ds(r0, B)
        gco = (r.gg[at, :] + r.mix[at, :]) * r.slope[at, :]
        r.gco[pl.ds(HALO + r0, B), :] = gco
        x = r.ip[pl.ds(r0, B + HALO), :]
        for k in range(4):
            r.acc[8 * k : 8 * k + 8, :] += fold8(gco * x[4 + 4 * k : 4 + 4 * k + B])
        r.acc[32:40, :] += fold8(gco)

    loop(R // B, second)

    def third(i):
        r0 = pl.multiple_of(i * 16, 16)
        x = r.gco[pl.ds(r0, 32), :]
        total = w[3] * x[0:16]
        for k in range(3):
            total = total + w[k] * x[4 * (3 - k) : 4 * (3 - k) + 16]
        r.gp[pl.ds(r0, 16), :E] = total.astype(BF)

    loop((HALO + R) // 16, third)
    r.gp[0:HALO, E:] = jnp.zeros((HALO, E), BF)
    if not halo:
        r.gp[0:HALO, :E] = jnp.zeros((HALO, E), BF)


def param_grads(r):
    zT = mm(eye(LT), r.z[...], NT).astype(BF)
    row = iota((LT, E), 0)
    peT = jnp.where(row < AT_DT, mm(zT, r.il[...]), 0.0)
    peT = peT + jnp.where((row >= AT_DT) & (row < AT_A), mm(zT, r.gz[...]), 0.0)
    rr, cc = iota((LT, 64), 0), iota((LT, 64), 1)
    hi, lo = split(r.alog[...])
    fold = onehot((rr >= AT_A) & (rr - AT_A == (cc >> 2)))
    rate = jnp.concatenate(
        [jnp.zeros((AT_A, E), F32), r.rate[...], jnp.zeros((LT - AT_A - N, E), F32)], 0
    )
    peT = peT + (mm(fold, hi) + mm(fold, lo)) * rate
    hi, lo = split(r.acc[...])
    fold = onehot((rr >= AT_SMALL) & (rr - AT_SMALL == (cc >> 3)))
    r.g_peT[...] = peT + mm(fold, hi) + mm(fold, lo)
    r.g_out[...] = mm(r.gated[...], r.GR[...], TN)
    for c in range(0, 2 * E, 256):
        r.g_inT[c : c + 256, :] = mm(r.gp[:, c : c + 256], r.V[...], TN)
    rows = mm(r.gp[...], r.inT[...])
    r.rows[...] = rows
    term = rows * r.V[...].astype(F32)
    first = (iota(term.shape, 0) & 3) < 2
    fwd = jnp.sum(jnp.where(first, term, 0.0), 0, keepdims=True)
    rev = jnp.sum(jnp.where(first, 0.0, term), 0, keepdims=True)
    both = jnp.concatenate([fwd, rev, jnp.zeros((6, D), F32)], 0)
    hi, lo = split(both)
    swap = swap_of(r)
    r.g_gain[...] = both + pltpu.roll(mm(hi, swap) + mm(lo, swap), 7, 0)


def edge_delta(r):
    swap = swap_of(r)
    hi, lo = split(r.rows[0:HALO, :])
    grad = jnp.where(
        (iota((HALO, D), 0) & 3) < 2, r.rows[0:HALO, :], mm(hi, swap) + mm(lo, swap)
    )
    _, scale, unit = normalise(mm(onehot(edge_place(False) | edge_place(True)), r.edge[...]))
    g = grad * gain_row(r)
    return scale * (g - unit * jnp.mean(g * unit, 1, keepdims=True))


def window_outputs(r, tok, cot, mask, gated, rows, out, ing):
    half = tok.shape[0]
    T = half // MB
    gain = gain_row(r)
    swap = swap_of(r)
    back = onehot(placing(T, True))
    g = mm(back, gated[...]).astype(BF)
    source, scale, unit = normalise(tok[...])
    outs = mm(r.outw[...], swap).astype(BF)
    out[...] = (source + mm(g[:half], r.outw[...]) + mm(g[half:], outs)).astype(BF)
    hi, lo = split(rows[HALO:, :])
    grad = (
        mm(back[:half], hi)
        + mm(back[:half], lo)
        + mm(back[half:], mm(hi, swap).astype(BF))
        + mm(back[half:], mm(lo, swap).astype(BF))
    )
    g = grad * gain
    mrow = jnp.concatenate([mask[0:1, :], mask[1:2, :]], 1)
    keep = onehot((iota((half, half), 0) == iota((half, half), 1)) & (mrow != 0))
    ing[...] = scale * (g - unit * jnp.mean(g * unit, 1, keepdims=True)) + mm(keep, cot[...])


def outputs_body(r):
    window_outputs(r, r.l_tok, r.l_cot, r.l_mask, r.l_gated, r.l_rows, r.l_out, r.l_ing)
    window_outputs(r, r.s_tok, r.s_cot, r.s_mask, r.s_gated, r.s_rows, r.s_out, r.s_ing)


def post_scratch(T):
    R = 4 * T
    return dict(
        acc=((64, E), F32),
        gg=((R, E), F32),
        slope=((R, E), F32),
        gco=((R + 2 * HALO, E), F32),
        il=((R, E), BF),
        gated=((R, E), BF),
        gz=((R, E), BF),
        z=((R, LT), BF),
        gp=((R + HALO, 2 * E), BF),
    )


GRADS = dict(
    g_inT=((2 * E, D), F32), g_out=((E, D), F32), g_peT=((LT, E), F32), g_gain=((8, D), F32)
)


def rows_out(T):
    return dict(rows=((4 * T + HALO, D), F32))


def combine_body(r, stride, radix, first, following):
    seq = lax.axis_index("seq")
    digit = (seq // stride) % radix
    last = following is None
    fwd = (iota((8, LT), 0) & 3) < 2
    rows = r.recv1.shape[0] - 16
    for m in range(radix):
        if m == 0 and last:
            continue
        src = r.own if m == 0 else getattr(r, f"recv{m}")
        r.mem[m, 0:rows, :] = src[0:rows, :].astype(F32)
        both = src[rows : rows + 16, :].astype(F32)
        r.mem[m, rows : rows + 8, :] = both[0:8] + both[8:16]
    for half in range(2):
        asc = fwd if half == 0 else jnp.logical_not(fwd)
        place = jnp.where(asc, digit, radix - 1 - digit)
        members = radix - 1 if last else radix
        low = 0 if last else 64 * half

        def member(f, at, es):
            return jnp.where(asc, r.mem[f ^ digit, at, es], r.mem[(radix - 1 - f) ^ digit, at, es])

        for e in range(E // LT):
            es = lanes_of(e)
            sums = [member(f, slice(rows, rows + 8), es) for f in range(members)]
            before = jnp.zeros((8, LT), F32)
            for f in range(members):
                before = before + jnp.where(f < place, sums[f], 0.0)
            old = None if first else r.spre[8 * half : 8 * half + 8, es]
            if not last:
                r.spre_new[8 * half : 8 * half + 8, es] = before if first else old + before
            for k in range(NP):
                at = slice(64 * half + 8 * k, 64 * half + 8 * k + 8)
                rk = r.r2[8 * k : 8 * k + 8, es]
                total = prefix = jnp.zeros((8, LT), F32)
                for f in range(members):
                    part = member(f, slice(low + 8 * k, low + 8 * k + 8), es)
                    if last:
                        here = f < place
                        total = jnp.where(here, jnp.exp2(rk * sums[f]) * total + part, total)
                    else:
                        prefix = jnp.where(place == f, total, prefix)
                        total = jnp.exp2(rk * sums[f]) * total + part
                if last:
                    prefix = total
                if not first:
                    prefix = jnp.exp2(rk * old) * prefix + r.prefix[at, es]
                r.prefix_new[at, es] = prefix
                if not last:
                    r.tot[at, es] = total
            if not last and half == 0:
                whole = sums[0]
                for f in range(1, radix):
                    whole = whole + sums[f]
                r.tot[128:136, es] = whole
    if last:
        return
    if not following[1]:
        write_element(r.element, r.tot)
        return
    next_stride, next_radix = following[0]
    digit = (seq // next_stride) % next_radix
    hi, lo = split(r.tot[128:136, :])
    sums = jnp.concatenate([hi.astype(F32), lo.astype(F32)], 0).astype(BF)
    first_half = (iota((64, E), 0) & 3) < 2
    for m in range(1, next_radix):
        out = getattr(r, f"half{m}")
        up = (digit ^ m) > digit
        out[0:64, :] = jnp.where(first_half == up, r.tot[0:64, :], r.tot[64:128, :]).astype(BF)
        out[64:80, :] = sums


def write_element(out, f32):
    out[0:128, :] = f32[0:128, :].astype(BF)
    hi, lo = split(f32[128:136, :])
    out[128:144, :] = jnp.concatenate([hi.astype(F32), lo.astype(F32)], 0).astype(BF)


def stages(count):
    stride, result = 1, []
    while stride < count:
        radix = 4 if (count // stride) % 4 == 0 else 2
        result.append((stride, radix))
        stride *= radix
    return result


ELEMENT = ((144, E), BF)


def carry_send(elements, count, stage):
    stride, radix = stage
    return [
        lax.ppermute(elements[m - 1], "seq", [(i, i ^ (m * stride)) for i in range(count)])
        for m in range(1, radix)
    ]


def combine_parts(own, received, r2, before, plan, at):
    stride, radix = plan[at]
    first, last = at == 0, at == len(plan) - 1
    ins = dict(r2=r2)
    if not last:
        ins["own"] = own
    for m in range(1, radix):
        ins[f"recv{m}"] = received[m - 1]
    if not first:
        ins.update(prefix=before["prefix_new"], spre=before["spre_new"])
    outs = dict(prefix_new=((128, E), F32))
    following = None
    if not last:
        ends = at + 1 == len(plan) - 1
        following = (plan[at + 1], ends)
        outs["spre_new"] = ((16, E), F32)
        if ends:
            outs.update({f"half{m}": ((80, E), BF) for m in range(1, plan[at + 1][1])})
        else:
            outs["element"] = ELEMENT
    scratch = dict(mem=((radix, received[0].shape[0] - 8, E), F32))
    if not last:
        scratch["tot"] = ((136, E), F32)
    body = functools.partial(
        combine_body, stride=stride, radix=radix, first=first, following=following
    )
    return ins, outs, scratch, body


def long_start_body(r, T, packed):
    if packed:
        unpack(r)
        r.gain[...] = gain_of(r)
    derive(r)
    copies = send(r, [k for k in r.early if k not in PREP_OUTS])
    prep(r, T, True)
    copies += send(r, PREP_OUTS)
    maps(r, T)
    scan_forward(r, T, None, False)
    scan_adjoint_local(r, T)

    def add(i, total):
        return total + r.st[pl.ds(pl.multiple_of(i * 8, 8), 8), :]

    total = lax.fori_loop(0, T // 2, add, jnp.zeros((8, E), F32))
    r.ends[128:136, :] = total + pltpu.roll(total, 4, 0)
    write_element(r.element, r.ends)
    for copy in copies:
        copy.wait()


def short_windows_body(r, T):
    prep(r, T, False)
    copies = send(r, r.early)
    maps(r, T)
    scan_forward(r, T, None, True)
    scan_backward(r, T, None)
    post(r, T, False)
    for copy in copies:
        copy.wait()


def fetch_start(r, names):
    copies = []
    for i, name in enumerate(names):
        copy = pltpu.make_async_copy(getattr(r, name + "_far"), getattr(r, name), r.sems.at[i])
        copy.start()
        copies.append(copy)
    return copies


def long_windows_body(r, T, names, combining):
    copies = fetch_start(r, names)
    combining(r)
    maps(r, T)
    scan_forward(r, T, r.prefix_new, True)
    scan_backward(r, T, r.prefix_new)
    for copy in copies:
        copy.wait()
    post(r, T, True)
    param_grads(r)
    finish_grads(r)


def finish_grads(r):
    g_inT, g_out = r.g_inT, r.g_out
    g_inT[...] += r.s_inT[...]
    g_out[...] += r.s_out[...]
    r.g_peT[...] += r.s_peT[...]
    r.g_gain[...] = (r.g_gain[...] + r.s_gain[...]) / gain_row(r)
    if not hasattr(r, "keep"):
        r.delta[...] = edge_delta(r)
        return
    lane, col = iota((D, E), 1), iota((D, E), 0)
    pick = onehot(((lane // 16) == (col // 8)) & ((lane % 16) == (col % 8)))
    peT = r.g_peT[...] + jnp.where(
        iota((LT, E), 0) == AT_SMALL + 7, mm(r.g_gain[0:1, :].astype(BF), pick), 0.0
    )
    r.pe_out[...] = peT.T.astype(BF)
    count = r.keep.shape[0] // BLOCK
    mine = lax.axis_index("dp")
    for dst, d, step in ((r.keep, mine, BLOCK), (r.give, 1 - mine, PACK)):
        for j in range(count):
            at = j * step
            in_at = pl.multiple_of(d * (count * IN_ROWS) + j * IN_ROWS, IN_ROWS)
            out_at = pl.multiple_of(d * (count * OUT_ROWS) + j * OUT_ROWS, OUT_ROWS)
            for half in range(2):
                lanes = slice(half * LT, (half + 1) * LT)
                dst[at + half * IN_ROWS : at + (half + 1) * IN_ROWS, :] = g_inT[
                    pl.ds(in_at, IN_ROWS), lanes
                ].astype(BF)
                low = at + 2 * IN_ROWS + half * OUT_ROWS
                dst[low : low + OUT_ROWS, :] = g_out[pl.ds(out_at, OUT_ROWS), lanes].astype(BF)
            dst[at + PACK - CH_ROWS : at + PACK, :] = r.pe_out[pl.ds(out_at, CH_ROWS), :]
    for j in range(count):
        r.keep[j * BLOCK + PACK : (j + 1) * BLOCK, :] = jnp.zeros((EDGE, LT), BF)
    delta = edge_delta(r).astype(BF)
    row, col = iota((8, HALO), 0), iota((8, HALO), 1)
    of = 4 * (row & 3) + (row >> 2)
    put_edges(r.keep, mm(onehot(col == of + 2), delta), mm(onehot(col == of), delta))


def add_body(r):
    count = r.keep.shape[0] // BLOCK
    for j in range(count):
        at = j * BLOCK
        r.buf[at : at + PACK, :] = (
            r.keep[at : at + PACK, :].astype(F32)
            + r.got[j * PACK : (j + 1) * PACK, :].astype(F32)
        ).astype(BF)
        r.buf[at + PACK : at + BLOCK, :] = r.keep[at + PACK : at + BLOCK, :]


def final_body(r, packed):
    r.grad[...] = r.ing[...]
    T = r.grad.shape[0] // MB
    if packed:
        from_prev, from_next = get_edges(r.parts)
    else:
        from_prev, from_next = r.from_prev[...], r.from_next[...]
    for mb in range(MB):
        for j in range(4):
            prev = 4 * mb + j if packed else 4 * j + 2 + mb
            follow = 4 * mb + j if packed else 4 * j + mb
            row = mb * T + T - 4 + j
            r.grad[row : row + 1, :] += from_next[follow : follow + 1, :]
            row = mb * T + 3 - j
            r.grad[row : row + 1, :] += from_prev[prev : prev + 1, :]
    if not packed:
        return
    count = r.parts.shape[0] // BLOCK
    total = r.parts[0:PACK, :].astype(F32)
    for j in range(1, count):
        total = total + r.parts[j * BLOCK : j * BLOCK + PACK, :].astype(F32)
    for half in range(2):
        lanes = slice(half * LT, (half + 1) * LT)
        r.in_wT[:, lanes] = total[half * IN_ROWS : (half + 1) * IN_ROWS]
        low = 2 * IN_ROWS + half * OUT_ROWS
        r.out_w[:, lanes] = total[low : low + OUT_ROWS]
    pe = total[PACK - CH_ROWS :]
    hi, lo = split(pe)
    peT = mm(eye(LT), hi, NT) + mm(eye(LT), lo, NT)
    r.x_w[...] = pe[:, : 3 * N]
    r.a_log[...] = pe[:, AT_A : AT_A + N]
    r.dt_w[...] = peT[AT_DT : AT_DT + N]
    small = peT[AT_SMALL : AT_SMALL + 8]
    r.conv_w[...] = small[0:4]
    r.conv_b[...] = small[4:5]
    r.dt_b[...] = small[5:6]
    r.skip[...] = small[6:7]
    r.gain[...] = small[7:8, 0 : r.gain.shape[1]]


PREP_OUTS = ("V", "GR", "ip", "gate", "co", "st", "sz", "si", "gm", "sel")


def prep_outs(T):
    R = 4 * T
    wide = ((R, E), F32)
    return dict(
        V=((R + HALO, D), BF),
        GR=((R, D), BF),
        ip=((R + HALO, E), F32),
        gate=wide,
        co=wide,
        st=wide,
        sz=wide,
        si=wide,
        gm=wide,
        sel=((R, LT), F32),
    )


def local(
    long_tokens,
    short_tokens,
    long_cotangent,
    short_cotangent,
    long_mask,
    short_mask,
    complement,
    norm_gain,
    in_weight,
    conv_weight,
    conv_bias,
    x_weight,
    dt_weight,
    dt_bias,
    a_log,
    d_skip,
    out_weight,
):
    count = lax.axis_size("seq")
    span, short = long_tokens.shape[2], short_tokens.shape[2]
    packed = out_weight.shape[0] == OUT_ROWS and in_weight.shape[1] == IN_ROWS
    comp = complement.reshape(1, D)
    up = [(i, i + 1) for i in range(count - 1)]
    down = [(i + 1, i) for i in range(count - 1)]

    if packed:
        buf = run(
            "pack",
            pack_body,
            dict(
                gain=norm_gain.reshape(1, -1),
                in_wT=in_weight.T,
                conv_w=conv_weight,
                conv_b=conv_bias.reshape(1, -1),
                x_w=x_weight,
                dt_w=dt_weight,
                dt_b=dt_bias.reshape(1, -1),
                a_log=a_log,
                skip=d_skip.reshape(1, -1),
                out_w=out_weight,
                tok=long_tokens.reshape(MB * span, D),
            ),
            dict(buf=((count * BLOCK, LT), BF)),
            dict(rows=((8, CH_ROWS), F32)),
        )["buf"]
        mine = lax.all_to_all(buf, "seq", 0, 0, tiled=True)
        other = lax.ppermute(mine, "dp", [(0, 1), (1, 0)])
        weights_in = dict(mine=mine, other=other)
    else:
        tail = lax.ppermute(long_tokens[:, 0, span - 4 :, :].reshape(8, D), "seq", up)
        head = lax.ppermute(long_tokens[:, 0, :4, :].reshape(8, D), "seq", down)

        def whole(a, axis):
            return lax.all_gather(a, BOTH, axis=axis, tiled=True)

        small = jnp.stack([*conv_weight, conv_bias, dt_bias, d_skip, jnp.zeros_like(d_skip)])
        columns = jnp.concatenate([a_log, small.T], 1)
        hi = columns.astype(BF)
        lo = (columns - hi.astype(F32)).astype(BF)
        zero = jnp.zeros((columns.shape[0], LT - AT_SMALL - 16), BF)
        chan = jnp.concatenate(
            [x_weight, dt_weight.T, hi[:, :N], lo[:, :N], hi[:, N:], lo[:, N:], zero], 1
        )
        weights_in = dict(
            inT=whole(in_weight.T, 0),
            outw=whole(out_weight, 0),
            pe=whole(chan, 0),
            gain=whole(norm_gain, 0).reshape(1, D),
            edge=jnp.concatenate([tail, head], 0),
        )

    def tokens_of(tok, cot, mask):
        T = tok.shape[2]
        return dict(
            tok=tok.reshape(MB * T, D), cot=cot.reshape(MB * T, D), mask=mask.reshape(MB, T)
        )

    long_in = tokens_of(long_tokens, long_cotangent, long_mask)
    short_in = tokens_of(short_tokens, short_cotangent, short_mask)

    derived = dict(
        r2=((8 * NP, E), F32),
        rowp=((8, E), F32),
        rate=((N, E), F32),
        dtw2=((LT, E), BF),
        xwT=((LT, E), BF),
    )
    unpacked = dict(
        inT=((2 * E, D), BF),
        outw=((E, D), BF),
        pe=((E, LT), BF),
        gain=((8, D), F32),
        edge=((HALO, D), BF),
    )
    started = run(
        "long_start",
        functools.partial(long_start_body, T=span, packed=packed),
        dict(comp=comp, **long_in, **weights_in),
        dict(
            element=ELEMENT, **prep_outs(span), **derived, **(unpacked if packed else {})
        ),
        dict(
            il=((4 * span, E), BF),
            imb=((8 * span, NP * LT), F32),
            omb=((8 * span, NP * LT), F32),
            ends=((136, E), F32),
        ),
        flops=1 << 33,
        early=PREP_OUTS + tuple(derived) + (tuple(unpacked) if packed else ()),
        vmem=62,
    )
    weights = {k: started[k] for k in derived}
    for k in unpacked:
        weights[k] = started[k] if packed else weights_in[k]

    plan = stages(count)
    own, before = started["element"], None
    received = carry_send([own] * 3, count, plan[0])
    middle = dict(
        gated=((4 * short, E), BF),
        gp=((4 * short + HALO, 2 * E), BF),
        il=((4 * short, E), BF),
        gz=((4 * short, E), BF),
        z=((4 * short, LT), BF),
        V=((4 * short + HALO, D), BF),
        GR=((4 * short, D), BF),
        alog=((8 * NP, E), F32),
        acc=((64, E), F32),
    )
    shorts = run(
        "short_windows",
        functools.partial(short_windows_body, T=short),
        dict(
            comp=comp,
            **short_in,
            **{k: weights[k] for k in ("inT", "outw", "pe", "gain", "dtw2", "xwT", "rowp", "r2")},
        ),
        middle,
        {
            k: v
            for k, v in dict(scan_scratch(short), **post_scratch(short), **prep_outs(short)).items()
            if k not in middle
        },
        flops=1 << 35,
        early=("V", "GR"),
        vmem=63,
    )
    for at in range(len(plan) - 1):
        ins, outs, scratch, body = combine_parts(own, received, weights["r2"], before, plan, at)
        before = run(f"combine{at}", body, ins, outs, scratch, vmem=8)
        if at + 1 == len(plan) - 1:
            sending = [before[f"half{m}"] for m in range(1, plan[at + 1][1])]
        else:
            own = before["element"]
            sending = [own] * 3
        received = carry_send(sending, count, plan[at + 1])
    short_grads = run(
        "short_grads",
        param_grads,
        dict(
            comp=comp, rate=weights["rate"], inT=weights["inT"], **{k: shorts[k] for k in middle}
        ),
        dict(GRADS, **rows_out(short)),
        flops=1 << 33,
    )

    ins, _, scratch, combining = combine_parts(
        own, received, weights["r2"], before, plan, len(plan) - 1
    )
    ins.update(
        comp=comp,
        edge=weights["edge"],
        **{k: weights[k] for k in ("rowp", "rate", "gain")},
        **{k: started[k] for k in ("st", "si", "gm", "sel")},
    )
    late = dict(
        {k: started[k] for k in ("ip", "gate", "co", "sz", "V", "GR")},
        **{k: weights[k] for k in ("inT", "outw", "xwT", "dtw2")},
        s_inT=short_grads["g_inT"],
        s_out=short_grads["g_out"],
        s_peT=short_grads["g_peT"],
        s_gain=short_grads["g_gain"],
    )
    names = tuple(late)
    ins.update({k + "_far": v for k, v in late.items()})
    outs = dict(rows_out(span), gated=((4 * span, E), BF))
    if packed:
        outs.update(keep=((count * BLOCK, LT), BF), give=((count * PACK, LT), BF))
        scratch.update(GRADS, pe_out=((E, LT), BF))
    else:
        outs.update(GRADS, delta=((HALO, D), F32))
    scratch.update(prefix_new=((128, E), F32), sems=pltpu.SemaphoreType.DMA((len(names),)))
    scratch.update(scan_scratch(span), **{k: (v.shape, v.dtype) for k, v in late.items()})
    scratch.update({k: v for k, v in post_scratch(span).items() if k not in outs})
    longs = run(
        "long_windows",
        functools.partial(long_windows_body, T=span, names=names, combining=combining),
        ins,
        outs,
        scratch,
        flops=1 << 35,
        far=tuple(k + "_far" for k in names),
    )

    outs = dict(
        l_out=((MB * span, D), BF),
        l_ing=((MB * span, D), F32),
        s_out=((MB * short, D), BF),
        s_ing=((MB * short, D), F32),
    )
    ins = dict(comp=comp, outw=weights["outw"], gain=weights["gain"])
    ins.update({"l_" + k: v for k, v in long_in.items()}, l_gated=longs["gated"], l_rows=longs["rows"])
    ins.update(
        {"s_" + k: v for k, v in short_in.items()},
        s_gated=shorts["gated"],
        s_rows=short_grads["rows"],
    )
    finished = run("outputs", outputs_body, ins, outs, flops=1 << 32, vmem=32)
    ins = dict(ing=finished["l_ing"])
    outs = dict(grad=((MB * span, D), F32))
    if packed:
        got = lax.ppermute(longs["give"], "dp", [(0, 1), (1, 0)])
        buf = run(
            "add",
            add_body,
            dict(keep=longs["keep"], got=got),
            dict(buf=((count * BLOCK, LT), BF)),
            vmem=8,
        )["buf"]
        ins["parts"] = lax.all_to_all(buf, "seq", 0, 0, tiled=True)
        outs.update(
            gain=((1, D // (2 * count)), F32),
            in_wT=((IN_ROWS, D), F32),
            conv_w=((4, CH_ROWS), F32),
            conv_b=((1, CH_ROWS), F32),
            x_w=((CH_ROWS, 3 * N), F32),
            dt_w=((N, CH_ROWS), F32),
            dt_b=((1, CH_ROWS), F32),
            a_log=((CH_ROWS, N), F32),
            skip=((1, CH_ROWS), F32),
            out_w=((OUT_ROWS, D), F32),
        )
    else:
        ins["from_next"] = lax.ppermute(longs["delta"], "seq", down)
        ins["from_prev"] = lax.ppermute(longs["delta"], "seq", up)
    done = run("final", functools.partial(final_body, packed=packed), ins, outs, vmem=8)
    if packed:
        grads = {k: done[k] for k in outs if k != "grad"}
        grads["in_w"] = grads["in_wT"].T
        for k in ("gain", "conv_b", "dt_b", "skip"):
            grads[k] = grads[k].reshape(-1)
    else:

        def own(a, axis=0):
            return lax.psum_scatter(a, BOTH, scatter_dimension=axis, tiled=True)

        pe = own(longs["g_peT"].T)
        grads = dict(
            gain=own(longs["g_gain"][0]),
            in_w=own(longs["g_inT"]).T,
            conv_w=pe[:, AT_SMALL : AT_SMALL + 4].T,
            conv_b=pe[:, AT_SMALL + 4],
            x_w=pe[:, : 3 * N],
            dt_w=pe[:, AT_DT : AT_DT + N].T,
            dt_b=pe[:, AT_SMALL + 5],
            a_log=pe[:, AT_A : AT_A + N],
            skip=pe[:, AT_SMALL + 6],
            out_w=own(longs["g_out"]),
        )
    order = ("gain", "in_w", "conv_w", "conv_b", "x_w", "dt_w", "dt_b", "a_log", "skip", "out_w")
    return (
        finished["l_out"].reshape(long_tokens.shape),
        finished["s_out"].reshape(short_tokens.shape),
        done["grad"].reshape(long_tokens.shape),
        finished["s_ing"].reshape(short_tokens.shape),
    ) + tuple(grads[k] for k in order)


def solution(mesh):
    long_spec, short_spec = P(None, "dp", "seq", None), P(None, BOTH, None, None)
    rows, columns, vector = P(BOTH, None), P(None, BOTH), P(BOTH)
    params = (vector, columns, columns, vector, rows, columns, vector, rows, vector, rows)
    return jax.shard_map(
        local,
        mesh=mesh,
        in_specs=(
            long_spec,
            short_spec,
            long_spec,
            short_spec,
            P(None, "dp", "seq"),
            P(None, BOTH, None),
            P(),
        )
        + params,
        out_specs=(long_spec, short_spec, long_spec, short_spec) + params,
        check_vma=False,
    )
```

```python
import functools
import types

import jax
import jax.numpy as jnp
from jax import lax
from jax.experimental import pallas as pl
from jax.experimental.pallas import tpu as pltpu
from jax.sharding import PartitionSpec as P

EPS = 1e-05
D, E, N, MB, HALO = 256, 512, 16, 2, 16
LT = 128
NP = N // 2
LOG2E = 1.4426950408889634
LN2 = 0.6931471805599453
F32, BF = jnp.float32, jnp.bfloat16
NT = (((1,), (1,)), ((), ()))
TN = (((0,), (0,)), ((), ()))
BOTH = ("dp", "seq")
IN_ROWS, OUT_ROWS, CH_ROWS = 32, 16, 16
PACK = 2 * IN_ROWS + 2 * OUT_ROWS + CH_ROWS
EDGE = 16
GATHER = PACK + 2 * EDGE
FAR = (8, 4)
SLOTS = (0, 8, 4, 12)
SUM_SLOTS = (0, 4, 8, 12)
AT_DT, AT_A, AT_SMALL = 48, 64, 96


def mm(a, b, dims=None):
    if dims is None:
        return jnp.dot(a, b, preferred_element_type=F32)
    return lax.dot_general(a, b, dims, preferred_element_type=F32)


def iota(shape, axis):
    return lax.broadcasted_iota(jnp.int32, shape, axis)


def onehot(cond):
    return jnp.where(cond, 1.0, 0.0).astype(BF)


def eye(n):
    return onehot(iota((n, n), 0) == iota((n, n), 1))


def split(x):
    hi = x.astype(BF)
    return hi, (x - hi.astype(F32)).astype(BF)


def silu_of_half(h):
    th = jnp.tanh(h)
    value = h * th + h
    u = 0.5 * th
    return value, (0.5 + u) + value * (0.5 - u)


def plus(total, x):
    return x if total is None else total + x


def loop(count, body):
    lax.fori_loop(0, count, lambda i, c: (body(i), c)[1], 0)


def run(name, body, ins, outs, scratch=None, flops=0, far=(), early=(), placed=(), vmem=60):
    scratch = dict(scratch or {}, **{k: outs[k] for k in early})
    scratch.update({k: (ins[k].shape, ins[k].dtype) for k in far})
    if far:
        scratch["in_sems"] = pltpu.SemaphoreType.DMA((len(far),))
    if early:
        scratch["out_sems"] = pltpu.SemaphoreType.DMA((len(early),))
    in_names, scratch_names = [k + "_far" if k in far else k for k in ins], list(scratch)
    out_names = [k + "_out" if k in early or k in placed else k for k in outs]

    def kernel(*refs):
        r = types.SimpleNamespace(**dict(zip(in_names + out_names + scratch_names, refs)))
        r.early, r.sent, r.fetched = tuple(early), [], []
        body(r)
        for copy in r.sent:
            copy.wait()

    def spec(key):
        return pl.BlockSpec(memory_space=pltpu.HBM if key in far else pltpu.VMEM)

    result = pl.pallas_call(
        kernel,
        out_shape=tuple(jax.ShapeDtypeStruct(*v) for v in outs.values()),
        in_specs=[spec(k) for k in ins],
        out_specs=tuple(
            pl.BlockSpec(memory_space=pltpu.HBM if k in early or k in placed else pltpu.VMEM)
            for k in outs
        ),
        scratch_shapes=[
            pltpu.VMEM(*scratch[k]) if isinstance(scratch[k], tuple) else scratch[k]
            for k in scratch_names
        ],
        compiler_params=pltpu.CompilerParams(vmem_limit_bytes=vmem << 20),
        cost_estimate=pl.CostEstimate(flops=flops, bytes_accessed=1 << 20, transcendentals=0),
        name=name,
    )(*ins.values())
    return dict(zip(outs, result))


def send(r, *names):
    for name in names:
        if name in r.early:
            copy = pltpu.make_async_copy(
                getattr(r, name), getattr(r, name + "_out"), r.out_sems.at[r.early.index(name)]
            )
            copy.start()
            r.sent.append(copy)


def fetch(r, *names):
    for name in names:
        copy = pltpu.make_async_copy(
            getattr(r, name + "_far"), getattr(r, name), r.in_sems.at[len(r.fetched)]
        )
        copy.start()
        r.fetched.append((name, copy))


def arrived(r, *names):
    for name, copy in r.fetched:
        if name in names:
            copy.wait()


def pack_body(r):
    r.rows[...] = jnp.zeros((8, CH_ROWS), F32)
    r.rows[0:4, :] = r.conv_w[...]
    r.rows[4:5, :] = r.conv_b[...]
    r.rows[5:6, :] = r.dt_b[...]
    r.rows[6:7, :] = r.skip[...]
    r.rows[7:8, 0 : r.gain.shape[1]] = r.gain[...]
    in_t = r.in_wT[...]
    small = jnp.concatenate(split(r.rows[...]), 0)

    def place(a, at, turned=False):
        n = a.shape[0 if turned else 1]
        return mm(a, onehot(iota((n, LT), 0) + at == iota((n, LT), 1)), TN if turned else None)

    a_hi, a_lo = split(r.a_log[...])
    chan = (
        place(r.x_w[...], 0)
        + place(r.dt_w[...], AT_DT, True)
        + place(a_hi, AT_A)
        + place(a_lo, AT_A + N)
        + place(small, AT_SMALL, True)
    ).astype(BF)
    out_w = r.out_w[...]
    for half in range(2):
        lanes = slice(half * LT, (half + 1) * LT)
        r.buf[half * IN_ROWS : (half + 1) * IN_ROWS, :] = in_t[:, lanes]
        low = 2 * IN_ROWS + half * OUT_ROWS
        r.buf[low : low + OUT_ROWS, :] = out_w[:, lanes]
    r.buf[PACK - CH_ROWS : PACK, :] = chan
    T = r.tok.shape[0] // MB
    for which, first in enumerate((T - 16, 0)):
        rows = [r.tok[mb * T + first : mb * T + first + 16, :].astype(F32) for mb in range(MB)]
        at = 12 if first else 0
        x = jnp.concatenate([x[at : at + 4] for x in rows], 0)
        r.buf[PACK + which * EDGE : PACK + (which + 1) * EDGE, :] = halves(x)


def halves(x):
    return jnp.concatenate([x[:, :LT], x[:, LT:]], 0).astype(BF)


def get_edges(buf, step, at):
    seq = lax.axis_index("seq")
    count = buf.shape[0] // step
    result = []
    before, after = jnp.maximum(seq - 1, 0), jnp.minimum(seq + 1, count - 1)
    for j, low, there in ((before, at[0], seq > 0), (after, at[1], seq < count - 1)):
        x = buf[pl.ds(pl.multiple_of(j * step + low, 16), EDGE), :].astype(F32)
        x = jnp.concatenate([x[:8], x[8:]], 1)
        result.append(jnp.where(there, x, 0.0))
    return result


def unpack(r):
    mine, seq = lax.axis_index("dp"), lax.axis_index("seq")
    count = E // (2 * OUT_ROWS)
    for near in range(4):
        for src, d in ((getattr(r, f"mine{near}"), mine), (getattr(r, f"other{near}"), 1 - mine)):
            for q, far in enumerate(SLOTS):
                at = q * GATHER
                dev = seq ^ (near | far)
                in_at = pl.multiple_of((d * count + dev) * IN_ROWS, IN_ROWS)
                out_at = pl.multiple_of((d * count + dev) * OUT_ROWS, OUT_ROWS)
                for half in range(2):
                    lanes = slice(half * LT, (half + 1) * LT)
                    r.inT[pl.ds(in_at, IN_ROWS), lanes] = src[
                        at + half * IN_ROWS : at + (half + 1) * IN_ROWS, :
                    ]
                    low = at + 2 * IN_ROWS + half * OUT_ROWS
                    r.outw[pl.ds(out_at, OUT_ROWS), lanes] = src[low : low + OUT_ROWS, :]
                r.pe[pl.ds(out_at, CH_ROWS), :] = src[at + PACK - CH_ROWS : at + PACK, :]
                if d is mine:
                    r.edges[pl.ds(pl.multiple_of(dev * 2 * EDGE, 2 * EDGE), 2 * EDGE), :] = src[
                        at + PACK : at + GATHER, :
                    ]
    r.edge[...] = jnp.concatenate(get_edges(r.edges, 2 * EDGE, (0, EDGE)), 0).astype(BF)


def join_body(r):
    rows = r.a.shape[0]
    r.both[0:rows, :] = r.a[...]
    r.both[rows:, :] = r.b[...]


def gather(buf):
    def swapped(x, mask):
        count = lax.axis_size("seq")
        return lax.ppermute(x, "seq", [(i, i ^ mask) for i in range(count)])

    for mask in FAR:
        buf = run(
            f"join{mask}",
            join_body,
            dict(a=buf, b=swapped(buf, mask)),
            dict(both=((2 * buf.shape[0], LT), BF)),
            vmem=8,
        )["both"]
    mine = [buf] + [swapped(buf, near) for near in range(1, 4)]
    other = [lax.ppermute(x, "dp", [(0, 1), (1, 0)]) for x in mine]
    return dict(
        {f"mine{i}": x for i, x in enumerate(mine)}, **{f"other{i}": x for i, x in enumerate(other)}
    )


def derive(r):
    peT = mm(eye(LT), r.pe[...], NT)
    small = peT[AT_SMALL : AT_SMALL + 8] + peT[AT_SMALL + 8 : AT_SMALL + 16]
    r.rowp[...] = small
    rate = -jnp.exp(peT[AT_A : AT_A + N] + peT[AT_A + N : AT_A + 2 * N])
    r.rate[...] = rate
    for n in range(N):
        r.r2[4 * n : 4 * n + 4, :] = jnp.broadcast_to(rate[n : n + 1] * LOG2E, (4, E))
    dt = peT[AT_DT : AT_DT + N]
    r.dtw2[...] = jnp.concatenate([dt, dt, jnp.zeros((LT - 2 * N, E), F32)], 0).astype(BF)
    r.xwT[...] = jnp.where(iota((LT, E), 0) < 3 * N, peT, 0.0).astype(BF)


def gain_of(r):
    per = E // (D // 8)
    low = mm(eye(LT), r.pe[...], NT)[AT_SMALL : AT_SMALL + 16].astype(BF)
    lane, col = iota((E, D), 0), iota((E, D), 1)
    pick = onehot(((lane // per) == (col // 8)) & ((lane % per) == (col % 8)))
    g = mm(low, pick)
    return g[0:8] + g[8:16]


def placing(T, transposed):
    shape = (2 * MB * T, 2 * MB * T)
    row, col = iota(shape, 1 if transposed else 0), iota(shape, 0 if transposed else 1)
    t, scan = row >> 2, row & 3
    turn = T.bit_length() - 1
    pos, src = col & (T - 1), col >> turn
    want = jnp.where(scan >= 2, T - 1 - t, t)
    return (src == scan) & (pos == want)


def gain_row(r):
    return r.gain[0:1, :] if r.gain.shape[0] == 1 else r.gain[7:8, :]


def normalise(tok):
    source = tok.astype(F32)
    scale = lax.rsqrt(jnp.mean(source * source, 1, keepdims=True) + EPS)
    return source, scale, source * scale


def swap_of(r):
    return onehot(iota((D, D), 0) == jnp.broadcast_to(r.comp[...], (D, D)))


def prep(r, T, halo, ready=None):
    R = 4 * T
    B = 64
    swap = swap_of(r)
    put = placing(T, False)
    mrow = jnp.concatenate([r.mask[0:1, :], r.mask[1:2, :]], 1)
    mrow = jnp.concatenate([mrow, mrow], 1)
    cot = r.cot[...]
    r.GR[...] = mm(
        onehot(put & (mrow != 0)), jnp.concatenate([cot, mm(cot, swap).astype(BF)], 0)
    ).astype(BF)
    _, _, unit = normalise(r.tok[...])
    if ready is not None:
        ready()
    gain = gain_row(r)
    normed = (unit * gain).astype(BF)
    r.V[HALO:, :] = mm(
        onehot(put), jnp.concatenate([normed, mm(normed, swap).astype(BF)], 0)
    ).astype(BF)
    if halo:
        hn = (normalise(r.edge[...])[2] * gain).astype(BF)
        r.V[0:HALO, :] = (
            mm(onehot(edge_place(False)), hn)
            + mm(onehot(edge_place(True)), mm(hn, swap).astype(BF))
        ).astype(BF)
        r.ip[0:HALO, :] = mm(r.V[0:HALO, :], r.inT[0:E, :], NT)
    else:
        r.V[0:HALO, :] = jnp.zeros((HALO, D), BF)
        r.ip[0:HALO, :] = jnp.zeros((HALO, E), F32)
    for c in range(0, E, 256):
        r.ip[HALO:, c : c + 256] = mm(r.V[HALO:, :], r.inT[c : c + 256, :], NT)
        r.silu[:, c : c + 256] = mm(r.V[HALO:, :], r.inT[E + c : E + c + 256, :], NT)
    for c in range(0, E, 256):
        r.gm[:, c : c + 256] = mm(r.GR[...], r.outw[c : c + 256, :], NT)
    w = [0.5 * r.rowp[k : k + 1, :] for k in range(5)]

    def first(i):
        r0 = pl.multiple_of(i * B, B)
        at = pl.ds(r0, B)
        x, mid = shifted(r.ip, r0, True, B)
        half = w[4] + w[0] * mid[8 : 8 + B] + w[1] * x[8 : 8 + B]
        half = half + w[2] * mid[HALO : HALO + B] + w[3] * x[HALO : HALO + B]
        inner, slope = silu_of_half(half)
        r.inner[at, :] = inner
        r.slope[at, :] = slope
        r.il[at, :] = inner.astype(BF)
        silu, slope = silu_of_half(0.5 * r.silu[at, :])
        r.silu[at, :] = silu
        r.gslope[at, :] = slope
        r.gm[at, :] = r.gm[at, :] * silu

    loop(R // B, first)
    sel = mm(r.il[...], r.pe[...])
    r.sel[...] = sel
    lane = iota((R, LT), 1)
    low = jnp.where(lane < N, sel, 0.0)
    hi = low.astype(BF).astype(F32)
    both = (hi + pltpu.roll(low - hi, N, 1)).astype(BF)
    for c in range(0, E, 256):
        r.st[:, c : c + 256] = mm(both, r.dtw2[:, c : c + 256])

    def second(i):
        at = pl.ds(pl.multiple_of(i * B, B), B)
        z = r.st[at, :] + r.rowp[5:6, :]
        u = jnp.exp2(jnp.abs(z) * -LOG2E)
        near = u * (1.0 - u * (0.5 - u * (1.0 / 3.0)))
        st = jnp.maximum(z, 0.0) + jnp.where(u < 0.01, near, jnp.log(1.0 + u))
        r.st[at, :] = st
        r.sz[at, :] = jnp.exp(z - st)
        r.si[at, :] = r.inner[at, :] * st

    loop(R // B, second)


B = 32


def shifted(ref, r0, before, B=B):
    x = ref[pl.ds(r0 + (0 if before else HALO), B + HALO), :]
    return x, pltpu.roll(x, 4 if before else B + HALO - 4, 0)


def edge_place(rev):
    row, col = iota((HALO, HALO), 0), iota((HALO, HALO), 1)
    j, scan = row >> 2, row & 3
    if rev:
        return (scan >= 2) & (col == 8 + (scan - 2) * 4 + (3 - j))
    return (scan < 2) & (col == scan * 4 + j)


def maps(r, T):
    R = 4 * T
    sel = r.sel[...]
    lane = iota((R, LT), 1)
    kept = jnp.where((lane >= N) & (lane < 3 * N), sel, 0.0)
    hi = kept.astype(BF).astype(F32)
    both = (hi + pltpu.roll(kept - hi, 64, 1)).astype(BF)
    G = 128
    r8, r4 = iota((2 * G, G), 0), iota((2 * G, G), 1)
    twice = onehot(((r8 >> 3) * 4 + (r8 & 3)) == r4)
    own = (iota((2 * G, LT), 1) & 1) == ((iota((2 * G, LT), 0) >> 2) & 1)
    l, c = iota((LT, NP * LT), 0), iota((LT, NP * LT), 1)
    l = l & 63
    spread_in = onehot((l >= N) & (l < 2 * N) & (((l - N) >> 1) == (c >> 7)))
    spread_out = onehot((l >= 2 * N) & (l < 3 * N) & (((l - 2 * N) >> 1) == (c >> 7)))
    for g in range(R // G):
        left = jnp.where(own, mm(twice, both[g * G : (g + 1) * G]), 0.0).astype(BF)
        r.imb[g * 2 * G : (g + 1) * 2 * G, :] = mm(left, spread_in)
        r.omb[g * 2 * G : (g + 1) * 2 * G, :] = mm(left, spread_out)


def dup(x, low):
    turned = pltpu.roll(x, 4, 0)
    return jnp.where(low, x, turned), jnp.where(low, turned, x)


def lanes_of(e):
    return slice(e * LT, (e + 1) * LT)


def scan_forward(r, T, start, full, U=16, tiles=range(E // LT)):
    low = iota((8, LT), 0) < 4
    for e in tiles:
        es = lanes_of(e)
        if start is None:
            first = tuple(jnp.zeros((8, LT), F32) for _ in range(NP))
        else:
            first = tuple(start[8 * k : 8 * k + 8, es] for k in range(NP))
        if full:
            for k in range(NP):
                r.states[0, 8 * k : 8 * k + 8, es] = first[k]

        def body(i, state):
            state = list(state)
            for u in range(U // 2):
                pair = i * (U // 2) + u
                row = pl.multiple_of(pair * 8, 8)
                st = dup(r.st[pl.ds(row, 8), es], low)
                si = dup(r.si[pl.ds(row, 8), es], low)
                ys = []
                for h in range(2):
                    t = pair * 2 + h
                    r8 = pl.multiple_of(t * 8, 8)
                    acc = None
                    for k in range(NP):
                        decay = jnp.exp2(st[h] * r.r2[8 * k : 8 * k + 8, es])
                        state[k] = decay * state[k] + si[h] * r.imb[pl.ds(r8, 8), lanes_of(k)]
                        if full:
                            r.states[t + 1, 8 * k : 8 * k + 8, es] = state[k]
                            y = state[k] * r.omb[pl.ds(r8, 8), lanes_of(k)]
                            acc = y if acc is None else acc + y
                    if full:
                        ys.append(acc + pltpu.roll(acc, 4, 0))
                if full:
                    r.mix[pl.ds(row, 8), es] = jnp.where(low, ys[0], ys[1])
            return tuple(state)

        last = lax.fori_loop(0, T // U, body, first)
        if not full:
            for k in range(NP):
                r.ends[8 * k : 8 * k + 8, es] = last[k]


def scan_adjoint_local(r, T, U=8, tiles=range(E // LT)):
    low = iota((8, LT), 0) < 4
    for e in tiles:
        es = lanes_of(e)

        def body(i, b):
            b = list(b)
            for u in range(U // 2):
                pair = T // 2 - 1 - (i * (U // 2) + u)
                row = pl.multiple_of(pair * 8, 8)
                st = dup(r.st[pl.ds(row, 8), es], low)
                gm = dup(r.gm[pl.ds(row, 8), es], low)
                for h in (1, 0):
                    r8 = pl.multiple_of((pair * 2 + h) * 8, 8)
                    for k in range(NP):
                        a = gm[h] * r.omb[pl.ds(r8, 8), lanes_of(k)] + b[k]
                        b[k] = jnp.exp2(st[h] * r.r2[8 * k : 8 * k + 8, es]) * a
            return tuple(b)

        last = lax.fori_loop(0, T // U, body, tuple(jnp.zeros((8, LT), F32) for _ in range(NP)))
        for k in range(NP):
            r.ends[64 + 8 * k : 64 + 8 * k + 8, es] = last[k]


def scan_backward(r, T, start, group=2, unroll=4):
    low = iota((8, LT), 0) < 4
    r.alog[...] = jnp.zeros((8 * NP, E), F32)
    r.b[...] = jnp.zeros((8 * NP, E), F32) if start is None else start[64:128, :]
    groups = E // LT // group
    for g in range(groups):
        tiles = [lanes_of(g * group + e) for e in range(group)]

        def body(i, g=g, tiles=tiles):
            for u in range(unroll):
                pair = T // 2 - 1 - (i * unroll + u)
                row = pl.multiple_of(pair * 8, 8)
                r16 = pl.multiple_of(pair * 16, 16)
                st = [dup(r.st[pl.ds(row, 8), es], low) for es in tiles]
                si = [dup(r.si[pl.ds(row, 8), es], low) for es in tiles]
                gm = [dup(r.gm[pl.ds(row, 8), es], low) for es in tiles]
                q = [[None, None] for _ in tiles]
                p = [[None, None] for _ in tiles]
                for k in range(NP):
                    ks = slice(8 * k, 8 * k + 8)
                    im = [r.imb[pl.ds(r16 + 8 * h, 8), lanes_of(k)] for h in range(2)]
                    om = [r.omb[pl.ds(r16 + 8 * h, 8), lanes_of(k)] for h in range(2)]
                    xi, xo = [None, None], [None, None]
                    for e, es in enumerate(tiles):
                        rk = r.r2[ks, es]
                        b = r.b[ks, es]
                        states = [r.states[2 * pair + h, ks, es] for h in range(3)]
                        rates = None
                        for h in (1, 0):
                            a = gm[e][h] * om[h] + b
                            b = jnp.exp2(st[e][h] * rk) * a
                            w = b * states[h]
                            q[e][h] = plus(q[e][h], w * rk)
                            rates = plus(rates, w * st[e][h])
                            p[e][h] = plus(p[e][h], a * im[h])
                            xi[h] = plus(xi[h], a * si[e][h])
                            xo[h] = plus(xo[h], states[h + 1] * gm[e][h])
                        r.b[ks, es] = b
                        r.alog[ks, es] += rates
                    cs = lanes_of(g * NP + k)
                    r.xi[pl.ds(r16, 16), cs] = jnp.concatenate(xi, 0).astype(BF)
                    r.xo[pl.ds(r16, 16), cs] = jnp.concatenate(xo, 0).astype(BF)
                for e, es in enumerate(tiles):
                    for out, v in ((r.q, q[e]), (r.p, p[e])):
                        v = [x + pltpu.roll(x, 4, 0) for x in v]
                        out[pl.ds(row, 8), es] = jnp.where(low, v[0], v[1])

        loop(T // 2 // unroll, body)
    rl, rc = iota((NP * LT, LT), 0), iota((NP * LT, LT), 1)
    red = onehot((rl >> 7) == (rc >> 1))
    W = NP * LT
    for out, x in ((r.yi, r.xi), (r.yo, r.xo)):
        total = x[:, :W]
        for g in range(1, groups):
            total = total + x[:, g * W : (g + 1) * W]
        out[...] = mm(total, red)
    G = 256
    own = (iota((G, LT), 1) & 1) == ((iota((G, LT), 0) >> 2) & 1)
    valid = own & (iota((G, LT), 1) < N)
    r8, r4 = iota((G // 2, G), 1), iota((G // 2, G), 0)
    fold = onehot(((r8 >> 3) * 4 + (r8 & 3)) == r4)
    for g in range(8 * T // G):
        at = slice(g * G, (g + 1) * G)
        y = pltpu.roll(jnp.where(valid, r.yi[at, :], 0.0), N, 1) + pltpu.roll(
            jnp.where(valid, r.yo[at, :], 0.0), 2 * N, 1
        )
        hi, lo = split(y)
        r.gsel[g * G // 2 : (g + 1) * G // 2, :] = mm(fold, hi) + mm(fold, lo)


def scan_scratch(T):
    return dict(
        states=((T + 1, 8 * NP, E), F32),
        imb=((8 * T, NP * LT), F32),
        omb=((8 * T, NP * LT), F32),
        xi=((8 * T, 2 * NP * LT), BF),
        xo=((8 * T, 2 * NP * LT), BF),
        b=((8 * NP, E), F32),
        yi=((8 * T, LT), F32),
        yo=((8 * T, LT), F32),
        mix=((4 * T, E), F32),
        q=((4 * T, E), F32),
        p=((4 * T, E), F32),
        alog=((8 * NP, E), F32),
        gsel=((4 * T, LT), F32),
    )


LATE = ("ip", "inner", "slope", "silu", "gslope", "sz", "V", "GR", "xwT", "rate")
LATE_LONG = LATE + ("inT", "outw", "dtw2")


def post(r, T, halo):
    R = 4 * T
    r.acc[...] = jnp.zeros((64, E), F32)
    arrived(r, *LATE)
    for c in range(0, E, 256):
        r.gg[:, c : c + 256] = mm(r.GR[...], r.outw[c : c + 256, :], NT)

    def first(i):
        at = pl.ds(pl.multiple_of(i * B, B), B)
        gp_at = pl.ds(pl.multiple_of(HALO + i * B, 16), B)
        for e in range(E // LT):
            es = lanes_of(e)
            skip = r.rowp[6:7, es]
            inner, gm, p = r.inner[at, es], r.gm[at, es], r.p[at, es]
            mixed = r.mix[at, es] + skip * inner
            r.il[at, es] = inner.astype(BF)
            r.gated[at, es] = (mixed * r.silu[at, es]).astype(BF)
            gate = r.gg[at, es] * mixed * r.gslope[at, es]
            r.gp[gp_at, E + e * LT : E + (e + 1) * LT] = gate.astype(BF)
            r.gz[at, es] = ((r.q[at, es] * LN2 + inner * p) * r.sz[at, es]).astype(BF)
            r.acc[48:56, es] += fold8(gm * inner)
            r.gg[at, es] = r.st[at, es] * p + gm * skip

    loop(R // B, first)
    lane = iota((R, LT), 1)
    gs_low = jnp.where(lane < N, mm(r.gz[...], r.dtw2[...], NT), r.gsel[...])
    gs_low = jnp.where(lane < 3 * N, gs_low, 0.0)
    r.z[...] = (
        gs_low
        + jnp.where((lane >= AT_DT) & (lane < AT_DT + N), pltpu.roll(r.sel[...], AT_DT, 1), 0.0)
        + jnp.where(lane == AT_SMALL + 5, 1.0, 0.0)
    ).astype(BF)
    gsb = gs_low.astype(BF)
    for c in range(0, E, 256):
        r.mix[:, c : c + 256] = mm(gsb, r.xwT[:, c : c + 256])
    r.gco[0:HALO, :] = jnp.zeros((HALO, E), F32)
    r.gco[HALO + R :, :] = jnp.zeros((HALO, E), F32)

    def second(i):
        r0 = pl.multiple_of(i * B, B)
        at = pl.ds(r0, B)
        x, mid = shifted(r.ip, r0, True)
        gco = (r.gg[at, :] + r.mix[at, :]) * r.slope[at, :]
        r.gco[pl.ds(r0 + HALO, B), :] = gco
        taps = (mid[8 : 8 + B], x[8 : 8 + B], mid[HALO : HALO + B], x[HALO : HALO + B])
        for k, v in enumerate(taps):
            r.acc[8 * k : 8 * k + 8, :] += fold8(gco * v)
        r.acc[32:40, :] += fold8(gco)

    loop(R // B, second)
    w = [r.rowp[k : k + 1, :] for k in range(4)]

    def third(i):
        r0 = pl.multiple_of(i * B, B)
        x, mid = shifted(r.gco, r0, False)
        rows = w[3] * x[0:B] + w[2] * mid[0:B] + w[1] * x[8 : 8 + B] + w[0] * mid[8 : 8 + B]
        r.gp[pl.ds(pl.multiple_of(r0 + HALO, 16), B), :E] = rows.astype(BF)

    loop(R // B, third)
    if halo:
        x = r.gco[0 : 2 * HALO, :]
        mid = pltpu.roll(x, 2 * HALO - 4, 0)
        rows = w[3] * x[0:16] + w[2] * mid[0:16] + w[1] * x[8:24] + w[0] * mid[8:24]
        r.gp[0:HALO, :E] = rows.astype(BF)
        r.gp[0:HALO, E:] = jnp.zeros((HALO, E), BF)
    else:
        r.gp[0:HALO, :] = jnp.zeros((HALO, 2 * E), BF)


def fold8(x):
    result = x[0:8]
    for j in range(8, x.shape[0], 8):
        result = result + x[j : j + 8]
    return result


def param_grads(r):
    zT = mm(eye(LT), r.z[...], NT).astype(BF)
    row = iota((LT, E), 0)
    peT = jnp.where(row < AT_DT, mm(zT, r.il[...]), 0.0)
    from_gz = ((row >= AT_DT) & (row < AT_A)) | (row == AT_SMALL + 5)
    peT = peT + jnp.where(from_gz, mm(zT, r.gz[...]), 0.0)
    rr, cc = iota((LT, 64), 0), iota((LT, 64), 1)
    hi, lo = split(r.alog[...])
    fold = onehot((rr >= AT_A) & (rr - AT_A == (cc >> 2)))
    rate = jnp.concatenate(
        [jnp.zeros((AT_A, E), F32), r.rate[...], jnp.zeros((LT - AT_A - N, E), F32)], 0
    )
    peT = peT + (mm(fold, hi) + mm(fold, lo)) * rate
    hi, lo = split(r.acc[...])
    fold = onehot((rr >= AT_SMALL) & (rr - AT_SMALL == (cc >> 3)))
    r.g_peT[...] = peT + mm(fold, hi) + mm(fold, lo)
    r.g_out[...] = mm(r.gated[...], r.GR[...], TN)
    for c in range(0, 2 * E, 256):
        r.g_inT[c : c + 256, :] = mm(r.gp[:, c : c + 256], r.V[...], TN)
    rows = mm(r.gp[...], r.inT[...])
    r.rows[...] = rows
    term = rows * r.V[...].astype(F32)
    first = (iota(term.shape, 0) & 3) < 2
    fwd = jnp.sum(jnp.where(first, term, 0.0), 0, keepdims=True)
    rev = jnp.sum(jnp.where(first, 0.0, term), 0, keepdims=True)
    both = jnp.concatenate([fwd, rev, jnp.zeros((6, D), F32)], 0)
    hi, lo = split(both)
    swap = swap_of(r)
    r.g_gain[...] = both + pltpu.roll(mm(hi, swap) + mm(lo, swap), 7, 0)


def edge_delta(r):
    swap = swap_of(r)
    hi, lo = split(r.rows[0:HALO, :])
    grad = jnp.where(
        (iota((HALO, D), 0) & 3) < 2, r.rows[0:HALO, :], mm(hi, swap) + mm(lo, swap)
    )
    _, scale, unit = normalise(mm(onehot(edge_place(False) | edge_place(True)), r.edge[...]))
    g = grad * gain_row(r)
    return scale * (g - unit * jnp.mean(g * unit, 1, keepdims=True))


def window_outputs(r, tok, cot, mask, gated, rows, out, ing):
    half = tok.shape[0]
    T = half // MB
    gain = gain_row(r)
    swap = swap_of(r)
    back = onehot(placing(T, True))
    g = mm(back, gated[...]).astype(BF)
    source, scale, unit = normalise(tok[...])
    outs = mm(r.outw[...], swap).astype(BF)
    out[...] = (source + mm(g[:half], r.outw[...]) + mm(g[half:], outs)).astype(BF)
    hi, lo = split(rows[HALO:, :])
    grad = (
        mm(back[:half], hi)
        + mm(back[:half], lo)
        + mm(back[half:], mm(hi, swap).astype(BF))
        + mm(back[half:], mm(lo, swap).astype(BF))
    )
    g = grad * gain
    mrow = jnp.concatenate([mask[0:1, :], mask[1:2, :]], 1)
    keep = onehot((iota((half, half), 0) == iota((half, half), 1)) & (mrow != 0))
    ing[...] = scale * (g - unit * jnp.mean(g * unit, 1, keepdims=True)) + mm(keep, cot[...])


def outputs_body(r):
    window_outputs(r, r.l_tok, r.l_cot, r.l_mask, r.l_gated, r.l_rows, r.l_out, r.l_ing)
    window_outputs(r, r.s_tok, r.s_cot, r.s_mask, r.s_gated, r.s_rows, r.s_out, r.s_ing)
    r.mark[...] = jnp.zeros((8, LT), F32)


def post_scratch(T):
    R = 4 * T
    return dict(
        acc=((64, E), F32),
        gg=((R, E), F32),
        gco=((R + 2 * HALO, E), F32),
        il=((R, E), BF),
        gated=((R, E), BF),
        gz=((R, E), BF),
        z=((R, LT), BF),
        gp=((R + HALO, 2 * E), BF),
    )


GRADS = dict(
    g_inT=((2 * E, D), F32), g_out=((E, D), F32), g_peT=((LT, E), F32), g_gain=((8, D), F32)
)


def rows_out(T):
    return dict(rows=((4 * T + HALO, D), F32))


STATE_ROWS = 4 * 8 * NP
ELEMENT = STATE_ROWS + 4 * 8


def to_spans(r, at, rows):
    seq = lax.axis_index("seq")
    count = r.carry_out.shape[0] // ELEMENT

    def start(j):
        dst = r.carry_out.at[pl.ds(pl.multiple_of(j * ELEMENT + at, 32), rows), :]

        @pl.when(j > seq)
        def _():
            pltpu.make_async_copy(r.later.at[at : at + rows, :], dst, r.carry_sem).start()

        @pl.when(j <= seq)
        def _():
            pltpu.make_async_copy(r.earlier.at[at : at + rows, :], dst, r.carry_sem).start()

    loop(count, start)


def send_sums(r, T):
    def add(i, total):
        return total + r.st[pl.ds(pl.multiple_of(i * 8, 8), 8), :]

    sums = lax.fori_loop(0, T // 2, add, jnp.zeros((8, E), F32))
    sums = sums + pltpu.roll(sums, 4, 0)
    sums = jnp.concatenate([sums[:, lanes_of(e)] for e in range(E // LT)], 0).astype(BF)
    r.later[STATE_ROWS:, :] = sums
    r.earlier[STATE_ROWS:, :] = sums
    to_spans(r, STATE_ROWS, 32)


def send_elements(r, e):
    normed = (iota((8 * NP, LT), 0) & 3) < 2
    state, adjoint = r.ends[0:64, lanes_of(e)], r.ends[64:128, lanes_of(e)]
    at = 64 * e
    r.later[at : at + 64, :] = jnp.where(normed, state, adjoint).astype(BF)
    r.earlier[at : at + 64, :] = jnp.where(normed, adjoint, state).astype(BF)
    to_spans(r, at, 64)


def wait_elements(r):
    pltpu.make_async_copy(r.carry_out, r.carry_out, r.carry_sem).wait()


def enter(r):
    seq = lax.axis_index("seq")
    count = r.elements.shape[0] // ELEMENT
    r.fold[...] = jnp.zeros((16 * NP, E), F32)

    def add(half, j):
        base = j * ELEMENT
        sums = r.elements[pl.ds(pl.multiple_of(base + STATE_ROWS, 32), 32), :].astype(F32)
        for e in range(E // LT):
            es = lanes_of(e)
            x = r.elements[pl.ds(pl.multiple_of(base + e * 64, 32), 64), :].astype(F32)
            for k in range(NP):
                ks = slice(8 * k, 8 * k + 8)
                at = slice(64 * half + 8 * k, 64 * half + 8 * k + 8)
                decay = jnp.exp2(r.r2[ks, es] * sums[8 * e : 8 * e + 8])
                r.fold[at, es] = decay * r.fold[at, es] + x[ks]

    loop(seq, lambda i: add(0, i))
    loop(count - 1 - seq, lambda i: add(1, count - 1 - i))
    normed = (iota((8 * NP, E), 0) & 3) < 2
    r.entering[0:64, :] = jnp.where(normed, r.fold[0:64, :], r.fold[64:128, :])
    r.entering[64:128, :] = jnp.where(normed, r.fold[64:128, :], r.fold[0:64, :])


def long_start_body(r, T, packed):

    def ready():
        if packed:
            unpack(r)
            r.gain[...] = gain_of(r)
        derive(r)
        send(r, *(k for k in r.early if k not in PREP_OUTS))

    prep(r, T, True, ready)
    send(r, *PREP_OUTS)
    maps(r, T)
    send_sums(r, T)
    for e in range(E // LT):
        scan_forward(r, T, None, False, tiles=(e,))
        scan_adjoint_local(r, T, tiles=(e,))
        send_elements(r, e)
    wait_elements(r)


def short_windows_body(r, T):
    prep(r, T, False)
    maps(r, T)
    scan_forward(r, T, None, True)
    scan_backward(r, T, None)
    post(r, T, False)
    param_grads(r)


FROM_SHORT = ("s_inT", "s_out", "s_peT", "s_gain")
LONG_FIRST = ("sel", "elements", "r2", "st", "si", "gm")
LONG_FAR = LONG_FIRST + LATE_LONG + FROM_SHORT


def long_windows_body(r, T):
    fetch(r, *LONG_FIRST)
    arrived(r, "sel")
    maps(r, T)
    arrived(r, "elements", "r2")
    enter(r)
    arrived(r, "st", "si", "gm")
    fetch(r, *LATE_LONG, *FROM_SHORT)
    scan_forward(r, T, r.entering, True)
    scan_backward(r, T, r.entering)
    arrived(r, "inT", "outw", "dtw2")
    post(r, T, True)
    param_grads(r)
    arrived(r, *FROM_SHORT)
    finish_grads(r)


def finish_grads(r):
    r.g_peT[...] += r.s_peT[...]
    r.g_gain[...] = (r.g_gain[...] + r.s_gain[...]) / gain_row(r)
    if not hasattr(r, "give"):
        r.g_inT[...] += r.s_inT[...]
        r.g_out[...] += r.s_out[...]
        r.delta[...] = edge_delta(r)
        return
    lane, col = iota((D, E), 1), iota((D, E), 0)
    pick = onehot(((lane // 16) == (col // 8)) & ((lane % 16) == (col % 8)))
    peT = r.g_peT[...] + jnp.where(
        iota((LT, E), 0) == AT_SMALL + 7, mm(r.g_gain[0:1, :].astype(BF), pick), 0.0
    )
    r.pe_out[...] = peT.T.astype(BF)
    mine, seq = lax.axis_index("dp"), lax.axis_index("seq")
    count = E // (2 * OUT_ROWS)
    delta = edge_delta(r).astype(BF)
    row, col = iota((8, HALO), 0), iota((8, HALO), 1)
    of = 4 * (row & 3) + (row >> 2)
    r.deltas[0:EDGE, :] = halves(mm(onehot(col == of), delta))
    r.deltas[EDGE:, :] = halves(mm(onehot(col == of + 2), delta))
    slots = [(4 * near + q, seq ^ (near | far)) for near in range(4) for q, far in enumerate(SUM_SLOTS)]
    for dst, d, step in ((r.give, 1 - mine, PACK), (r.keep, mine, GATHER)):
        for slot, dev in slots:
            at = slot * step
            in_at = pl.multiple_of((d * count + dev) * IN_ROWS, IN_ROWS)
            out_at = pl.multiple_of((d * count + dev) * OUT_ROWS, OUT_ROWS)
            for half in range(2):
                lanes = slice(half * LT, (half + 1) * LT)
                rows = pl.ds(in_at, IN_ROWS)
                dst[at + half * IN_ROWS : at + (half + 1) * IN_ROWS, :] = (
                    r.g_inT[rows, lanes] + r.s_inT[rows, lanes]
                ).astype(BF)
                low = at + 2 * IN_ROWS + half * OUT_ROWS
                rows = pl.ds(out_at, OUT_ROWS)
                dst[low : low + OUT_ROWS, :] = (r.g_out[rows, lanes] + r.s_out[rows, lanes]).astype(BF)
            dst[at + PACK - CH_ROWS : at + PACK, :] = r.pe_out[pl.ds(out_at, CH_ROWS), :]
    zero = jnp.zeros((EDGE, LT), BF)
    for slot, dev in slots:
        at = slot * GATHER + PACK
        r.keep[at : at + EDGE, :] = jnp.where(dev == seq - 1, r.deltas[0:EDGE, :], zero)
        r.keep[at + EDGE : at + 2 * EDGE, :] = jnp.where(dev == seq + 1, r.deltas[EDGE:, :], zero)


def total(*parts):
    result = parts[0].astype(F32)
    for x in parts[1:]:
        result = result + x.astype(F32)
    return result


def add_core_body(r):
    fetch(r, "keep")
    arrived(r, "keep")
    for near in range(4):
        part = getattr(r, f"part{near}")
        for q in range(4):
            at, keep, got = q * GATHER, (4 * near + q) * GATHER, (4 * near + q) * PACK
            part[at : at + PACK, :] = total(
                r.keep[keep : keep + PACK, :], r.got[got : got + PACK, :]
            ).astype(BF)
            part[at + PACK : at + GATHER, :] = r.keep[keep + PACK : keep + GATHER, :]


def add_near_body(r):
    for i, dst in enumerate((r.low, r.high)):
        at = slice(i * 2 * GATHER, (i + 1) * 2 * GATHER)
        dst[...] = total(r.part0[at, :], r.got1[at, :], r.got2[at, :], r.got3[at, :]).astype(BF)


def add_far_body(r):
    r.own[...] = total(r.low[0:GATHER, :], r.got[0:GATHER, :]).astype(BF)
    r.last[...] = total(r.low[GATHER:, :], r.got[GATHER:, :]).astype(BF)


def scatter(give, keep, after):
    def swapped(x, mask):
        count = lax.axis_size("seq")
        return lax.ppermute(x, "seq", [(i, i ^ mask) for i in range(count)])

    got = lax.ppermute(give, "dp", [(0, 1), (1, 0)])
    four = ((4 * GATHER, LT), BF)
    parts = run(
        "add_core",
        add_core_body,
        dict(got=got, keep=keep),
        {f"part{i}": four for i in range(4)},
        far=("keep",),
        vmem=8,
    )
    near = {f"got{i}": swapped(parts[f"part{i}"], i) for i in range(1, 4)}
    two = ((2 * GATHER, LT), BF)
    sums = run(
        "add_near",
        add_near_body,
        dict(part0=parts["part0"], after=after, **near),
        dict(low=two, high=two),
        vmem=8,
    )
    one = ((GATHER, LT), BF)
    ends = run(
        "add_far",
        add_far_body,
        dict(low=sums["low"], got=swapped(sums["high"], 8)),
        dict(own=one, last=one),
        vmem=8,
    )
    return ends["own"], swapped(ends["last"], 4)


def final_body(r, packed):
    r.grad[...] = r.ing[...]
    T = r.grad.shape[0] // MB
    if packed:
        block = total(r.own[...], r.got[...])
        from_next, from_prev = (
            jnp.concatenate([x[:8], x[8:]], 1)
            for x in (block[PACK : PACK + EDGE], block[PACK + EDGE :])
        )
    else:
        from_prev, from_next = r.from_prev[...], r.from_next[...]
    for mb in range(MB):
        for j in range(4):
            prev = 4 * mb + j if packed else 4 * j + 2 + mb
            follow = 4 * mb + j if packed else 4 * j + mb
            row = mb * T + T - 4 + j
            r.grad[row : row + 1, :] += from_next[follow : follow + 1, :]
            row = mb * T + 3 - j
            r.grad[row : row + 1, :] += from_prev[prev : prev + 1, :]
    if not packed:
        return
    for half in range(2):
        lanes = slice(half * LT, (half + 1) * LT)
        r.in_wT[:, lanes] = block[half * IN_ROWS : (half + 1) * IN_ROWS]
        low = 2 * IN_ROWS + half * OUT_ROWS
        r.out_w[:, lanes] = block[low : low + OUT_ROWS]
    pe = block[PACK - CH_ROWS : PACK]
    hi, lo = split(pe)
    peT = mm(eye(LT), hi, NT) + mm(eye(LT), lo, NT)
    r.x_w[...] = pe[:, : 3 * N]
    r.a_log[...] = pe[:, AT_A : AT_A + N]
    r.dt_w[...] = peT[AT_DT : AT_DT + N]
    small = peT[AT_SMALL : AT_SMALL + 8]
    r.conv_w[...] = small[0:4]
    r.conv_b[...] = small[4:5]
    r.dt_b[...] = small[5:6]
    r.skip[...] = small[6:7]
    r.gain[...] = small[7:8, 0 : r.gain.shape[1]]


PREP_OUTS = ("V", "GR", "ip", "inner", "slope", "silu", "gslope", "st", "sz", "si", "gm", "sel")


def prep_outs(T):
    R = 4 * T
    wide = ((R, E), F32)
    return dict(
        V=((R + HALO, D), BF),
        GR=((R, D), BF),
        ip=((R + HALO, E), F32),
        inner=wide,
        slope=wide,
        silu=wide,
        gslope=wide,
        st=wide,
        sz=wide,
        si=wide,
        gm=wide,
        sel=((R, LT), F32),
    )


def local(
    long_tokens,
    short_tokens,
    long_cotangent,
    short_cotangent,
    long_mask,
    short_mask,
    complement,
    norm_gain,
    in_weight,
    conv_weight,
    conv_bias,
    x_weight,
    dt_weight,
    dt_bias,
    a_log,
    d_skip,
    out_weight,
):
    count = lax.axis_size("seq")
    span, short = long_tokens.shape[2], short_tokens.shape[2]
    packed = count == 16 and out_weight.shape[0] == OUT_ROWS and in_weight.shape[1] == IN_ROWS
    comp = complement.reshape(1, D)
    up = [(i, i + 1) for i in range(count - 1)]
    down = [(i + 1, i) for i in range(count - 1)]

    if packed:
        buf = run(
            "pack",
            pack_body,
            dict(
                gain=norm_gain.reshape(1, -1),
                in_wT=in_weight.T,
                conv_w=conv_weight,
                conv_b=conv_bias.reshape(1, -1),
                x_w=x_weight,
                dt_w=dt_weight,
                dt_b=dt_bias.reshape(1, -1),
                a_log=a_log,
                skip=d_skip.reshape(1, -1),
                out_w=out_weight,
                tok=long_tokens.reshape(MB * span, D),
            ),
            dict(buf=((GATHER, LT), BF)),
            dict(rows=((8, CH_ROWS), F32)),
        )["buf"]
        weights_in = gather(buf)
    else:
        tail = lax.ppermute(long_tokens[:, 0, span - 4 :, :].reshape(8, D), "seq", up)
        head = lax.ppermute(long_tokens[:, 0, :4, :].reshape(8, D), "seq", down)

        def whole(a, axis):
            return lax.all_gather(a, BOTH, axis=axis, tiled=True)

        small = jnp.stack([*conv_weight, conv_bias, dt_bias, d_skip, jnp.zeros_like(d_skip)])
        columns = jnp.concatenate([a_log, small.T], 1)
        hi = columns.astype(BF)
        lo = (columns - hi.astype(F32)).astype(BF)
        zero = jnp.zeros((columns.shape[0], LT - AT_SMALL - 16), BF)
        chan = jnp.concatenate(
            [x_weight, dt_weight.T, hi[:, :N], lo[:, :N], hi[:, N:], lo[:, N:], zero], 1
        )
        weights_in = dict(
            inT=whole(in_weight.T, 0),
            outw=whole(out_weight, 0),
            pe=whole(chan, 0),
            gain=whole(norm_gain, 0).reshape(1, D),
            edge=jnp.concatenate([tail, head], 0),
        )

    def tokens_of(tok, cot, mask):
        T = tok.shape[2]
        return dict(
            tok=tok.reshape(MB * T, D), cot=cot.reshape(MB * T, D), mask=mask.reshape(MB, T)
        )

    long_in = tokens_of(long_tokens, long_cotangent, long_mask)
    short_in = tokens_of(short_tokens, short_cotangent, short_mask)

    derived = dict(
        r2=((8 * NP, E), F32),
        rowp=((8, E), F32),
        rate=((N, E), F32),
        dtw2=((LT, E), BF),
        xwT=((LT, E), BF),
    )
    unpacked = dict(
        inT=((2 * E, D), BF),
        outw=((E, D), BF),
        pe=((E, LT), BF),
        gain=((8, D), F32),
        edge=((HALO, D), BF),
    )
    started = run(
        "long_start",
        functools.partial(long_start_body, T=span, packed=packed),
        dict(comp=comp, **long_in, **weights_in),
        dict(
            carry=((count * ELEMENT, LT), BF), **prep_outs(span), **derived, **(unpacked if packed else {})
        ),
        dict(
            il=((4 * span, E), BF),
            imb=((8 * span, NP * LT), F32),
            omb=((8 * span, NP * LT), F32),
            ends=((128, E), F32),
            later=((ELEMENT, LT), BF),
            earlier=((ELEMENT, LT), BF),
            carry_sem=pltpu.SemaphoreType.DMA,
            **(dict(edges=((count * 2 * EDGE, LT), BF)) if packed else {}),
        ),
        flops=1 << 33,
        early=PREP_OUTS + tuple(derived) + (tuple(unpacked) if packed else ()),
        placed=("carry",),
        vmem=62,
    )
    weights = {k: started[k] for k in derived}
    for k in unpacked:
        weights[k] = started[k] if packed else weights_in[k]

    elements = lax.all_to_all(started["carry"], "seq", 0, 0, tiled=True)
    shorts = run(
        "short_windows",
        functools.partial(short_windows_body, T=short),
        dict(
            comp=comp,
            **short_in,
            **{
                k: weights[k]
                for k in ("inT", "outw", "pe", "gain", "dtw2", "xwT", "rowp", "r2", "rate")
            },
        ),
        dict(GRADS, **rows_out(short), gated=((4 * short, E), BF)),
        {
            k: v
            for k, v in dict(scan_scratch(short), **post_scratch(short), **prep_outs(short)).items()
            if k != "gated"
        },
        flops=1 << 36,
        vmem=63,
    )

    ins = dict(
        elements=elements,
        comp=comp,
        **{k: weights[k] for k in ("edge", "r2", "rowp", "rate", "gain", "inT", "outw", "xwT", "dtw2")},
        **{k: started[k] for k in PREP_OUTS},
        s_inT=shorts["g_inT"],
        s_out=shorts["g_out"],
        s_peT=shorts["g_peT"],
        s_gain=shorts["g_gain"],
    )
    outs = dict(rows_out(span), gated=((4 * span, E), BF))
    scratch = dict(entering=((16 * NP, E), F32), fold=((16 * NP, E), F32))
    if packed:
        outs.update(give=((count * PACK, LT), BF), keep=((count * GATHER, LT), BF))
        scratch.update(GRADS, pe_out=((E, LT), BF), deltas=((2 * EDGE, LT), BF))
    else:
        outs.update(GRADS, delta=((HALO, D), F32))
    scratch.update(scan_scratch(span))
    scratch.update({k: v for k, v in post_scratch(span).items() if k not in outs})
    longs = run(
        "long_windows",
        functools.partial(long_windows_body, T=span),
        ins,
        outs,
        scratch,
        flops=1 << 35,
        far=tuple(k for k in LONG_FAR),
    )

    outs = dict(
        l_out=((MB * span, D), BF),
        l_ing=((MB * span, D), F32),
        s_out=((MB * short, D), BF),
        s_ing=((MB * short, D), F32),
        mark=((8, LT), F32),
    )
    ins = dict(comp=comp, outw=weights["outw"], gain=weights["gain"])
    ins.update({"l_" + k: v for k, v in long_in.items()}, l_gated=longs["gated"], l_rows=longs["rows"])
    ins.update(
        {"s_" + k: v for k, v in short_in.items()},
        s_gated=shorts["gated"],
        s_rows=shorts["rows"],
    )
    finished = run("outputs", outputs_body, ins, outs, flops=1 << 32, vmem=32)
    ins = dict(ing=finished["l_ing"])
    outs = dict(grad=((MB * span, D), F32))
    if packed:
        ins["own"], ins["got"] = scatter(longs["give"], longs["keep"], finished["mark"])
        outs.update(
            gain=((1, D // (2 * count)), F32),
            in_wT=((IN_ROWS, D), F32),
            conv_w=((4, CH_ROWS), F32),
            conv_b=((1, CH_ROWS), F32),
            x_w=((CH_ROWS, 3 * N), F32),
            dt_w=((N, CH_ROWS), F32),
            dt_b=((1, CH_ROWS), F32),
            a_log=((CH_ROWS, N), F32),
            skip=((1, CH_ROWS), F32),
            out_w=((OUT_ROWS, D), F32),
        )
    else:
        ins["from_next"] = lax.ppermute(longs["delta"], "seq", down)
        ins["from_prev"] = lax.ppermute(longs["delta"], "seq", up)
    done = run("final", functools.partial(final_body, packed=packed), ins, outs, vmem=8)
    if packed:
        grads = {k: done[k] for k in outs if k != "grad"}
        grads["in_w"] = grads["in_wT"].T
        for k in ("gain", "conv_b", "dt_b", "skip"):
            grads[k] = grads[k].reshape(-1)
    else:

        def own(a, axis=0):
            return lax.psum_scatter(a, BOTH, scatter_dimension=axis, tiled=True)

        pe = own(longs["g_peT"].T)
        grads = dict(
            gain=own(longs["g_gain"][0]),
            in_w=own(longs["g_inT"]).T,
            conv_w=pe[:, AT_SMALL : AT_SMALL + 4].T,
            conv_b=pe[:, AT_SMALL + 4],
            x_w=pe[:, : 3 * N],
            dt_w=pe[:, AT_DT : AT_DT + N].T,
            dt_b=pe[:, AT_SMALL + 5],
            a_log=pe[:, AT_A : AT_A + N],
            skip=pe[:, AT_SMALL + 6],
            out_w=own(longs["g_out"]),
        )
    order = ("gain", "in_w", "conv_w", "conv_b", "x_w", "dt_w", "dt_b", "a_log", "skip", "out_w")
    return (
        finished["l_out"].reshape(long_tokens.shape),
        finished["s_out"].reshape(short_tokens.shape),
        done["grad"].reshape(long_tokens.shape),
        finished["s_ing"].reshape(short_tokens.shape),
    ) + tuple(grads[k] for k in order)


def solution(mesh):
    long_spec, short_spec = P(None, "dp", "seq", None), P(None, BOTH, None, None)
    rows, columns, vector = P(BOTH, None), P(None, BOTH), P(BOTH)
    params = (vector, columns, columns, vector, rows, columns, vector, rows, vector, rows)
    return jax.shard_map(
        local,
        mesh=mesh,
        in_specs=(
            long_spec,
            short_spec,
            long_spec,
            short_spec,
            P(None, "dp", "seq"),
            P(None, BOTH, None),
            P(),
        )
        + params,
        out_specs=(long_spec, short_spec, long_spec, short_spec) + params,
        check_vma=False,
    )
```

```python
import functools
import types

import jax
import jax.numpy as jnp
from jax import lax
from jax.experimental import pallas as pl
from jax.experimental.pallas import tpu as pltpu
from jax.sharding import PartitionSpec as P

EPS = 1e-05
D, E, N, MB, HALO = 256, 512, 16, 2, 16
LT = 128
NP = N // 2
LOG2E = 1.4426950408889634
LN2 = 0.6931471805599453
F32, BF = jnp.float32, jnp.bfloat16
NT = (((1,), (1,)), ((), ()))
TN = (((0,), (0,)), ((), ()))
BOTH = ("dp", "seq")
IN_ROWS, OUT_ROWS, CH_ROWS = 32, 16, 16
PACK = 2 * IN_ROWS + 2 * OUT_ROWS + CH_ROWS
EDGE = 16
GATHER = PACK + 2 * EDGE
FAR = (8, 4)
SLOTS = (0, 8, 4, 12)
SUM_SLOTS = (0, 4, 8, 12)
AT_DT, AT_A, AT_SMALL = 48, 64, 96


def mm(a, b, dims=None):
    if dims is None:
        return jnp.dot(a, b, preferred_element_type=F32)
    return lax.dot_general(a, b, dims, preferred_element_type=F32)


def iota(shape, axis):
    return lax.broadcasted_iota(jnp.int32, shape, axis)


def onehot(cond):
    return jnp.where(cond, 1.0, 0.0).astype(BF)


def eye(n):
    return onehot(iota((n, n), 0) == iota((n, n), 1))


def split(x):
    hi = x.astype(BF)
    return hi, (x - hi.astype(F32)).astype(BF)


def silu_of_half(h):
    th = jnp.tanh(h)
    value = h * th + h
    u = 0.5 * th
    return value, (0.5 + u) + value * (0.5 - u)


def plus(total, x):
    return x if total is None else total + x


def loop(count, body):
    lax.fori_loop(0, count, lambda i, c: (body(i), c)[1], 0)


def run(name, body, ins, outs, scratch=None, flops=0, far=(), early=(), placed=(), pin=None, vmem=60):
    scratch = dict(scratch or {}, **{k: outs[k] for k in early})
    scratch.update({k: (ins[k].shape, ins[k].dtype) for k in far})
    if far:
        scratch["in_sems"] = pltpu.SemaphoreType.DMA((len(far),))
    if early:
        scratch["out_sems"] = pltpu.SemaphoreType.DMA((len(early),))
    in_names, scratch_names = [k + "_far" if k in far else k for k in ins], list(scratch)
    out_names = [k + "_out" if k in early or k in placed else k for k in outs]

    def kernel(*refs):
        r = types.SimpleNamespace(**dict(zip(in_names + out_names + scratch_names, refs)))
        r.early, r.sent, r.fetched = tuple(early), [], []
        body(r)
        for copy in r.sent:
            copy.wait()

    def spec(key):
        return pl.BlockSpec(memory_space=pltpu.HBM if key in far else pltpu.VMEM)

    result = pl.pallas_call(
        kernel,
        out_shape=tuple(
            pin[k](*v) if pin and k in pin else jax.ShapeDtypeStruct(*v) for k, v in outs.items()
        ),
        in_specs=[spec(k) for k in ins],
        out_specs=tuple(
            pl.BlockSpec(memory_space=pltpu.HBM if k in early or k in placed else pltpu.VMEM)
            for k in outs
        ),
        scratch_shapes=[
            pltpu.VMEM(*scratch[k]) if isinstance(scratch[k], tuple) else scratch[k]
            for k in scratch_names
        ],
        compiler_params=pltpu.CompilerParams(vmem_limit_bytes=vmem << 20),
        cost_estimate=pl.CostEstimate(flops=flops, bytes_accessed=1 << 20, transcendentals=0),
        name=name,
    )(*ins.values())
    return dict(zip(outs, result))


def send(r, *names):
    for name in names:
        if name in r.early:
            copy = pltpu.make_async_copy(
                getattr(r, name), getattr(r, name + "_out"), r.out_sems.at[r.early.index(name)]
            )
            copy.start()
            r.sent.append(copy)


def fetch(r, *names):
    for name in names:
        copy = pltpu.make_async_copy(
            getattr(r, name + "_far"), getattr(r, name), r.in_sems.at[len(r.fetched)]
        )
        copy.start()
        r.fetched.append((name, copy))


def arrived(r, *names):
    for name, copy in r.fetched:
        if name in names:
            copy.wait()


def pack_body(r):
    r.rows[...] = jnp.zeros((8, CH_ROWS), F32)
    r.rows[0:4, :] = r.conv_w[...]
    r.rows[4:5, :] = r.conv_b[...]
    r.rows[5:6, :] = r.dt_b[...]
    r.rows[6:7, :] = r.skip[...]
    r.rows[7:8, 0 : r.gain.shape[1]] = r.gain[...]
    in_t = r.in_wT[...]
    small = jnp.concatenate(split(r.rows[...]), 0)

    def place(a, at, turned=False):
        n = a.shape[0 if turned else 1]
        return mm(a, onehot(iota((n, LT), 0) + at == iota((n, LT), 1)), TN if turned else None)

    a_hi, a_lo = split(r.a_log[...])
    chan = (
        place(r.x_w[...], 0)
        + place(r.dt_w[...], AT_DT, True)
        + place(a_hi, AT_A)
        + place(a_lo, AT_A + N)
        + place(small, AT_SMALL, True)
    ).astype(BF)
    out_w = r.out_w[...]
    for half in range(2):
        lanes = slice(half * LT, (half + 1) * LT)
        r.buf[half * IN_ROWS : (half + 1) * IN_ROWS, :] = in_t[:, lanes]
        low = 2 * IN_ROWS + half * OUT_ROWS
        r.buf[low : low + OUT_ROWS, :] = out_w[:, lanes]
    r.buf[PACK - CH_ROWS : PACK, :] = chan
    for name in ("comp", "tok", "cot", "mask"):
        getattr(r, name + "_near")[...] = getattr(r, name)[...]
    T = r.tok.shape[0] // MB
    for which, first in enumerate((T - 16, 0)):
        rows = [r.tok[mb * T + first : mb * T + first + 16, :].astype(F32) for mb in range(MB)]
        at = 12 if first else 0
        x = jnp.concatenate([x[at : at + 4] for x in rows], 0)
        r.buf[PACK + which * EDGE : PACK + (which + 1) * EDGE, :] = halves(x)


def halves(x):
    return jnp.concatenate([x[:, :LT], x[:, LT:]], 0).astype(BF)


def get_edges(buf, step, at):
    seq = lax.axis_index("seq")
    count = buf.shape[0] // step
    result = []
    before, after = jnp.maximum(seq - 1, 0), jnp.minimum(seq + 1, count - 1)
    for j, low, there in ((before, at[0], seq > 0), (after, at[1], seq < count - 1)):
        x = buf[pl.ds(pl.multiple_of(j * step + low, 16), EDGE), :].astype(F32)
        x = jnp.concatenate([x[:8], x[8:]], 1)
        result.append(jnp.where(there, x, 0.0))
    return result


def unpack(r):
    mine, seq = lax.axis_index("dp"), lax.axis_index("seq")
    count = E // (2 * OUT_ROWS)
    for near in range(4):
        for src, d in ((getattr(r, f"mine{near}"), mine), (getattr(r, f"other{near}"), 1 - mine)):
            for q, far in enumerate(SLOTS):
                at = q * GATHER
                dev = seq ^ (near | far)
                in_at = pl.multiple_of((d * count + dev) * IN_ROWS, IN_ROWS)
                out_at = pl.multiple_of((d * count + dev) * OUT_ROWS, OUT_ROWS)
                for half in range(2):
                    lanes = slice(half * LT, (half + 1) * LT)
                    r.inT[pl.ds(in_at, IN_ROWS), lanes] = src[
                        at + half * IN_ROWS : at + (half + 1) * IN_ROWS, :
                    ]
                    low = at + 2 * IN_ROWS + half * OUT_ROWS
                    r.outw[pl.ds(out_at, OUT_ROWS), lanes] = src[low : low + OUT_ROWS, :]
                r.pe[pl.ds(out_at, CH_ROWS), :] = src[at + PACK - CH_ROWS : at + PACK, :]
                if d is mine:
                    r.edges[pl.ds(pl.multiple_of(dev * 2 * EDGE, 2 * EDGE), 2 * EDGE), :] = src[
                        at + PACK : at + GATHER, :
                    ]
    r.edge[...] = jnp.concatenate(get_edges(r.edges, 2 * EDGE, (0, EDGE)), 0).astype(BF)


def join_body(r):
    rows = r.a.shape[0]
    r.both[0:rows, :] = r.a[...]
    r.both[rows:, :] = r.b[...]


def gather(buf):
    def swapped(x, mask):
        count = lax.axis_size("seq")
        return lax.ppermute(x, "seq", [(i, i ^ mask) for i in range(count)])

    for mask in FAR:
        buf = run(
            f"join{mask}",
            join_body,
            dict(a=buf, b=swapped(buf, mask)),
            dict(both=((2 * buf.shape[0], LT), BF)),
            vmem=8,
        )["both"]
    mine = [buf] + [swapped(buf, near) for near in range(1, 4)]
    other = [lax.ppermute(x, "dp", [(0, 1), (1, 0)]) for x in mine]
    return dict(
        {f"mine{i}": x for i, x in enumerate(mine)}, **{f"other{i}": x for i, x in enumerate(other)}
    )


def derive(r):
    peT = mm(eye(LT), r.pe[...], NT)
    small = peT[AT_SMALL : AT_SMALL + 8] + peT[AT_SMALL + 8 : AT_SMALL + 16]
    r.rowp[...] = small
    rate = -jnp.exp(peT[AT_A : AT_A + N] + peT[AT_A + N : AT_A + 2 * N])
    r.rate[...] = rate
    for n in range(N):
        r.r2[4 * n : 4 * n + 4, :] = jnp.broadcast_to(rate[n : n + 1] * LOG2E, (4, E))
    dt = peT[AT_DT : AT_DT + N]
    r.dtw2[...] = jnp.concatenate([dt, dt, jnp.zeros((LT - 2 * N, E), F32)], 0).astype(BF)
    r.xwT[...] = jnp.where(iota((LT, E), 0) < 3 * N, peT, 0.0).astype(BF)


def gain_of(r):
    per = E // (D // 8)
    low = mm(eye(LT), r.pe[...], NT)[AT_SMALL : AT_SMALL + 16].astype(BF)
    lane, col = iota((E, D), 0), iota((E, D), 1)
    pick = onehot(((lane // per) == (col // 8)) & ((lane % per) == (col % 8)))
    g = mm(low, pick)
    return g[0:8] + g[8:16]


def placing(T, transposed):
    shape = (2 * MB * T, 2 * MB * T)
    row, col = iota(shape, 1 if transposed else 0), iota(shape, 0 if transposed else 1)
    t, scan = row >> 2, row & 3
    turn = T.bit_length() - 1
    pos, src = col & (T - 1), col >> turn
    want = jnp.where(scan >= 2, T - 1 - t, t)
    return (src == scan) & (pos == want)


def gain_row(r):
    return r.gain[0:1, :] if r.gain.shape[0] == 1 else r.gain[7:8, :]


def normalise(tok):
    source = tok.astype(F32)
    scale = lax.rsqrt(jnp.mean(source * source, 1, keepdims=True) + EPS)
    return source, scale, source * scale


def swap_of(r):
    return onehot(iota((D, D), 0) == jnp.broadcast_to(r.comp[...], (D, D)))


def prep(r, T, halo, ready=None):
    R = 4 * T
    B = 64
    swap = swap_of(r)
    put = placing(T, False)
    mrow = jnp.concatenate([r.mask[0:1, :], r.mask[1:2, :]], 1)
    mrow = jnp.concatenate([mrow, mrow], 1)
    cot = r.cot[...]
    r.GR[...] = mm(
        onehot(put & (mrow != 0)), jnp.concatenate([cot, mm(cot, swap).astype(BF)], 0)
    ).astype(BF)
    _, _, unit = normalise(r.tok[...])
    if ready is not None:
        ready()
    gain = gain_row(r)
    normed = (unit * gain).astype(BF)
    r.V[HALO:, :] = mm(
        onehot(put), jnp.concatenate([normed, mm(normed, swap).astype(BF)], 0)
    ).astype(BF)
    if halo:
        hn = (normalise(r.edge[...])[2] * gain).astype(BF)
        r.V[0:HALO, :] = (
            mm(onehot(edge_place(False)), hn)
            + mm(onehot(edge_place(True)), mm(hn, swap).astype(BF))
        ).astype(BF)
        r.ip[0:HALO, :] = mm(r.V[0:HALO, :], r.inT[0:E, :], NT)
    else:
        r.V[0:HALO, :] = jnp.zeros((HALO, D), BF)
        r.ip[0:HALO, :] = jnp.zeros((HALO, E), F32)
    for c in range(0, E, 256):
        r.ip[HALO:, c : c + 256] = mm(r.V[HALO:, :], r.inT[c : c + 256, :], NT)
        r.silu[:, c : c + 256] = mm(r.V[HALO:, :], r.inT[E + c : E + c + 256, :], NT)
    for c in range(0, E, 256):
        r.gm[:, c : c + 256] = mm(r.GR[...], r.outw[c : c + 256, :], NT)
    w = [0.5 * r.rowp[k : k + 1, :] for k in range(5)]

    def first(i):
        r0 = pl.multiple_of(i * B, B)
        at = pl.ds(r0, B)
        x, mid = shifted(r.ip, r0, True, B)
        half = w[4] + w[0] * mid[8 : 8 + B] + w[1] * x[8 : 8 + B]
        half = half + w[2] * mid[HALO : HALO + B] + w[3] * x[HALO : HALO + B]
        inner, slope = silu_of_half(half)
        r.inner[at, :] = inner
        r.slope[at, :] = slope
        r.il[at, :] = inner.astype(BF)
        silu, slope = silu_of_half(0.5 * r.silu[at, :])
        r.silu[at, :] = silu
        r.gslope[at, :] = slope
        r.gm[at, :] = r.gm[at, :] * silu

    loop(R // B, first)
    sel = mm(r.il[...], r.pe[...])
    r.sel[...] = sel
    lane = iota((R, LT), 1)
    low = jnp.where(lane < N, sel, 0.0)
    hi = low.astype(BF).astype(F32)
    both = (hi + pltpu.roll(low - hi, N, 1)).astype(BF)
    for c in range(0, E, 256):
        r.st[:, c : c + 256] = mm(both, r.dtw2[:, c : c + 256])

    def second(i):
        at = pl.ds(pl.multiple_of(i * B, B), B)
        z = r.st[at, :] + r.rowp[5:6, :]
        u = jnp.exp2(jnp.abs(z) * -LOG2E)
        near = u * (1.0 - u * (0.5 - u * (1.0 / 3.0)))
        st = jnp.maximum(z, 0.0) + jnp.where(u < 0.01, near, jnp.log(1.0 + u))
        r.st[at, :] = st
        r.sz[at, :] = jnp.exp(z - st)
        r.si[at, :] = r.inner[at, :] * st

    loop(R // B, second)


B = 32


def shifted(ref, r0, before, B=B):
    x = ref[pl.ds(r0 + (0 if before else HALO), B + HALO), :]
    return x, pltpu.roll(x, 4 if before else B + HALO - 4, 0)


def edge_place(rev):
    row, col = iota((HALO, HALO), 0), iota((HALO, HALO), 1)
    j, scan = row >> 2, row & 3
    if rev:
        return (scan >= 2) & (col == 8 + (scan - 2) * 4 + (3 - j))
    return (scan < 2) & (col == scan * 4 + j)


def maps(r, T):
    R = 4 * T
    sel = r.sel[...]
    lane = iota((R, LT), 1)
    kept = jnp.where((lane >= N) & (lane < 3 * N), sel, 0.0)
    hi = kept.astype(BF).astype(F32)
    both = (hi + pltpu.roll(kept - hi, 64, 1)).astype(BF)
    G = 128
    r8, r4 = iota((2 * G, G), 0), iota((2 * G, G), 1)
    twice = onehot(((r8 >> 3) * 4 + (r8 & 3)) == r4)
    own = (iota((2 * G, LT), 1) & 1) == ((iota((2 * G, LT), 0) >> 2) & 1)
    l, c = iota((LT, NP * LT), 0), iota((LT, NP * LT), 1)
    l = l & 63
    spread_in = onehot((l >= N) & (l < 2 * N) & (((l - N) >> 1) == (c >> 7)))
    spread_out = onehot((l >= 2 * N) & (l < 3 * N) & (((l - 2 * N) >> 1) == (c >> 7)))
    for g in range(R // G):
        left = jnp.where(own, mm(twice, both[g * G : (g + 1) * G]), 0.0).astype(BF)
        r.imb[g * 2 * G : (g + 1) * 2 * G, :] = mm(left, spread_in)
        r.omb[g * 2 * G : (g + 1) * 2 * G, :] = mm(left, spread_out)


def dup(x, low):
    turned = pltpu.roll(x, 4, 0)
    return jnp.where(low, x, turned), jnp.where(low, turned, x)


def lanes_of(e):
    return slice(e * LT, (e + 1) * LT)


def scan_forward(r, T, start, full, U=16, tiles=range(E // LT)):
    low = iota((8, LT), 0) < 4
    for e in tiles:
        es = lanes_of(e)
        if start is None:
            first = tuple(jnp.zeros((8, LT), F32) for _ in range(NP))
        else:
            first = tuple(start[8 * k : 8 * k + 8, es] for k in range(NP))
        if full:
            for k in range(NP):
                r.states[0, 8 * k : 8 * k + 8, es] = first[k]

        def body(i, state):
            state = list(state)
            for u in range(U // 2):
                pair = i * (U // 2) + u
                row = pl.multiple_of(pair * 8, 8)
                st = dup(r.st[pl.ds(row, 8), es], low)
                si = dup(r.si[pl.ds(row, 8), es], low)
                ys = []
                for h in range(2):
                    t = pair * 2 + h
                    r8 = pl.multiple_of(t * 8, 8)
                    acc = None
                    for k in range(NP):
                        decay = jnp.exp2(st[h] * r.r2[8 * k : 8 * k + 8, es])
                        state[k] = decay * state[k] + si[h] * r.imb[pl.ds(r8, 8), lanes_of(k)]
                        if full:
                            r.states[t + 1, 8 * k : 8 * k + 8, es] = state[k]
                            y = state[k] * r.omb[pl.ds(r8, 8), lanes_of(k)]
                            acc = y if acc is None else acc + y
                    if full:
                        ys.append(acc + pltpu.roll(acc, 4, 0))
                if full:
                    r.mix[pl.ds(row, 8), es] = jnp.where(low, ys[0], ys[1])
            return tuple(state)

        last = lax.fori_loop(0, T // U, body, first)
        if not full:
            for k in range(NP):
                r.ends[8 * k : 8 * k + 8, es] = last[k]


def scan_adjoint_local(r, T, U=8, tiles=range(E // LT)):
    low = iota((8, LT), 0) < 4
    for e in tiles:
        es = lanes_of(e)

        def body(i, b):
            b = list(b)
            for u in range(U // 2):
                pair = T // 2 - 1 - (i * (U // 2) + u)
                row = pl.multiple_of(pair * 8, 8)
                st = dup(r.st[pl.ds(row, 8), es], low)
                gm = dup(r.gm[pl.ds(row, 8), es], low)
                for h in (1, 0):
                    r8 = pl.multiple_of((pair * 2 + h) * 8, 8)
                    for k in range(NP):
                        a = gm[h] * r.omb[pl.ds(r8, 8), lanes_of(k)] + b[k]
                        b[k] = jnp.exp2(st[h] * r.r2[8 * k : 8 * k + 8, es]) * a
            return tuple(b)

        last = lax.fori_loop(0, T // U, body, tuple(jnp.zeros((8, LT), F32) for _ in range(NP)))
        for k in range(NP):
            r.ends[64 + 8 * k : 64 + 8 * k + 8, es] = last[k]


def scan_backward(r, T, start, group=2, unroll=4):
    low = iota((8, LT), 0) < 4
    r.alog[...] = jnp.zeros((8 * NP, E), F32)
    r.b[...] = jnp.zeros((8 * NP, E), F32) if start is None else start[64:128, :]
    groups = E // LT // group
    for g in range(groups):
        tiles = [lanes_of(g * group + e) for e in range(group)]

        def body(i, g=g, tiles=tiles):
            for u in range(unroll):
                pair = T // 2 - 1 - (i * unroll + u)
                row = pl.multiple_of(pair * 8, 8)
                r16 = pl.multiple_of(pair * 16, 16)
                st = [dup(r.st[pl.ds(row, 8), es], low) for es in tiles]
                si = [dup(r.si[pl.ds(row, 8), es], low) for es in tiles]
                gm = [dup(r.gm[pl.ds(row, 8), es], low) for es in tiles]
                q = [[None, None] for _ in tiles]
                p = [[None, None] for _ in tiles]
                for k in range(NP):
                    ks = slice(8 * k, 8 * k + 8)
                    im = [r.imb[pl.ds(r16 + 8 * h, 8), lanes_of(k)] for h in range(2)]
                    om = [r.omb[pl.ds(r16 + 8 * h, 8), lanes_of(k)] for h in range(2)]
                    xi, xo = [None, None], [None, None]
                    for e, es in enumerate(tiles):
                        rk = r.r2[ks, es]
                        b = r.b[ks, es]
                        states = [r.states[2 * pair + h, ks, es] for h in range(3)]
                        rates = None
                        for h in (1, 0):
                            a = gm[e][h] * om[h] + b
                            b = jnp.exp2(st[e][h] * rk) * a
                            w = b * states[h]
                            q[e][h] = plus(q[e][h], w * rk)
                            rates = plus(rates, w * st[e][h])
                            p[e][h] = plus(p[e][h], a * im[h])
                            xi[h] = plus(xi[h], a * si[e][h])
                            xo[h] = plus(xo[h], states[h + 1] * gm[e][h])
                        r.b[ks, es] = b
                        r.alog[ks, es] += rates
                    cs = lanes_of(g * NP + k)
                    r.xi[pl.ds(r16, 16), cs] = jnp.concatenate(xi, 0).astype(BF)
                    r.xo[pl.ds(r16, 16), cs] = jnp.concatenate(xo, 0).astype(BF)
                for e, es in enumerate(tiles):
                    for out, v in ((r.q, q[e]), (r.p, p[e])):
                        v = [x + pltpu.roll(x, 4, 0) for x in v]
                        out[pl.ds(row, 8), es] = jnp.where(low, v[0], v[1])

        loop(T // 2 // unroll, body)
    rl, rc = iota((NP * LT, LT), 0), iota((NP * LT, LT), 1)
    red = onehot((rl >> 7) == (rc >> 1))
    W = NP * LT
    for out, x in ((r.yi, r.xi), (r.yo, r.xo)):
        total = x[:, :W]
        for g in range(1, groups):
            total = total + x[:, g * W : (g + 1) * W]
        out[...] = mm(total, red)
    G = 256
    own = (iota((G, LT), 1) & 1) == ((iota((G, LT), 0) >> 2) & 1)
    valid = own & (iota((G, LT), 1) < N)
    r8, r4 = iota((G // 2, G), 1), iota((G // 2, G), 0)
    fold = onehot(((r8 >> 3) * 4 + (r8 & 3)) == r4)
    for g in range(8 * T // G):
        at = slice(g * G, (g + 1) * G)
        y = pltpu.roll(jnp.where(valid, r.yi[at, :], 0.0), N, 1) + pltpu.roll(
            jnp.where(valid, r.yo[at, :], 0.0), 2 * N, 1
        )
        r.gsel[g * G // 2 : (g + 1) * G // 2, :] = mm(fold, y.astype(BF))


def scan_scratch(T):
    return dict(
        states=((T + 1, 8 * NP, E), F32),
        imb=((8 * T, NP * LT), F32),
        omb=((8 * T, NP * LT), F32),
        xi=((8 * T, 2 * NP * LT), BF),
        xo=((8 * T, 2 * NP * LT), BF),
        b=((8 * NP, E), F32),
        yi=((8 * T, LT), F32),
        yo=((8 * T, LT), F32),
        mix=((4 * T, E), F32),
        q=((4 * T, E), F32),
        p=((4 * T, E), F32),
        alog=((8 * NP, E), F32),
        gsel=((4 * T, LT), F32),
    )


LATE = ("ip", "inner", "slope", "silu", "gslope", "sz", "V", "GR", "xwT", "rate")
LATE_LONG = LATE + ("inT", "outw", "dtw2")


def post(r, T, halo):
    R = 4 * T
    r.acc[...] = jnp.zeros((64, E), F32)
    arrived(r, *LATE)
    for c in range(0, E, 256):
        r.gg[:, c : c + 256] = mm(r.GR[...], r.outw[c : c + 256, :], NT)

    def first(i):
        at = pl.ds(pl.multiple_of(i * B, B), B)
        gp_at = pl.ds(pl.multiple_of(HALO + i * B, 16), B)
        for e in range(E // LT):
            es = lanes_of(e)
            skip = r.rowp[6:7, es]
            inner, gm, p = r.inner[at, es], r.gm[at, es], r.p[at, es]
            mixed = r.mix[at, es] + skip * inner
            r.il[at, es] = inner.astype(BF)
            r.gated[at, es] = (mixed * r.silu[at, es]).astype(BF)
            gate = r.gg[at, es] * mixed * r.gslope[at, es]
            r.gp[gp_at, E + e * LT : E + (e + 1) * LT] = gate.astype(BF)
            r.gz[at, es] = ((r.q[at, es] * LN2 + inner * p) * r.sz[at, es]).astype(BF)
            r.acc[48:56, es] += fold8(gm * inner)
            r.gg[at, es] = r.st[at, es] * p + gm * skip

    loop(R // B, first)
    lane = iota((R, LT), 1)
    gs_low = jnp.where(lane < N, mm(r.gz[...], r.dtw2[...], NT), r.gsel[...])
    gs_low = jnp.where(lane < 3 * N, gs_low, 0.0)
    r.z[...] = (
        gs_low
        + jnp.where((lane >= AT_DT) & (lane < AT_DT + N), pltpu.roll(r.sel[...], AT_DT, 1), 0.0)
        + jnp.where(lane == AT_SMALL + 5, 1.0, 0.0)
    ).astype(BF)
    gsb = gs_low.astype(BF)
    for c in range(0, E, 256):
        r.mix[:, c : c + 256] = mm(gsb, r.xwT[:, c : c + 256])
    r.gco[0:HALO, :] = jnp.zeros((HALO, E), F32)
    r.gco[HALO + R :, :] = jnp.zeros((HALO, E), F32)

    def second(i):
        r0 = pl.multiple_of(i * B, B)
        at = pl.ds(r0, B)
        x, mid = shifted(r.ip, r0, True)
        gco = (r.gg[at, :] + r.mix[at, :]) * r.slope[at, :]
        r.gco[pl.ds(r0 + HALO, B), :] = gco
        taps = (mid[8 : 8 + B], x[8 : 8 + B], mid[HALO : HALO + B], x[HALO : HALO + B])
        for k, v in enumerate(taps):
            r.acc[8 * k : 8 * k + 8, :] += fold8(gco * v)
        r.acc[32:40, :] += fold8(gco)

    loop(R // B, second)
    w = [r.rowp[k : k + 1, :] for k in range(4)]

    def third(i):
        r0 = pl.multiple_of(i * B, B)
        x, mid = shifted(r.gco, r0, False)
        rows = w[3] * x[0:B] + w[2] * mid[0:B] + w[1] * x[8 : 8 + B] + w[0] * mid[8 : 8 + B]
        r.gp[pl.ds(pl.multiple_of(r0 + HALO, 16), B), :E] = rows.astype(BF)

    loop(R // B, third)
    if halo:
        x = r.gco[0 : 2 * HALO, :]
        mid = pltpu.roll(x, 2 * HALO - 4, 0)
        rows = w[3] * x[0:16] + w[2] * mid[0:16] + w[1] * x[8:24] + w[0] * mid[8:24]
        r.gp[0:HALO, :E] = rows.astype(BF)
        r.gp[0:HALO, E:] = jnp.zeros((HALO, E), BF)
    else:
        r.gp[0:HALO, :] = jnp.zeros((HALO, 2 * E), BF)


def fold8(x):
    result = x[0:8]
    for j in range(8, x.shape[0], 8):
        result = result + x[j : j + 8]
    return result


def param_grads(r):
    zT = mm(eye(LT), r.z[...], NT).astype(BF)
    row = iota((LT, E), 0)
    peT = jnp.where(row < AT_DT, mm(zT, r.il[...]), 0.0)
    from_gz = ((row >= AT_DT) & (row < AT_A)) | (row == AT_SMALL + 5)
    peT = peT + jnp.where(from_gz, mm(zT, r.gz[...]), 0.0)
    rr, cc = iota((LT, 64), 0), iota((LT, 64), 1)
    hi, lo = split(r.alog[...])
    fold = onehot((rr >= AT_A) & (rr - AT_A == (cc >> 2)))
    rate = jnp.concatenate(
        [jnp.zeros((AT_A, E), F32), r.rate[...], jnp.zeros((LT - AT_A - N, E), F32)], 0
    )
    peT = peT + (mm(fold, hi) + mm(fold, lo)) * rate
    hi, lo = split(r.acc[...])
    fold = onehot((rr >= AT_SMALL) & (rr - AT_SMALL == (cc >> 3)))
    r.g_peT[...] = peT + mm(fold, hi) + mm(fold, lo)
    r.g_out[...] = mm(r.gated[...], r.GR[...], TN)
    for c in range(0, 2 * E, 256):
        r.g_inT[c : c + 256, :] = mm(r.gp[:, c : c + 256], r.V[...], TN)
    rows = mm(r.gp[...], r.inT[...])
    r.rows[...] = rows
    term = rows * r.V[...].astype(F32)
    first = (iota(term.shape, 0) & 3) < 2
    fwd = jnp.sum(jnp.where(first, term, 0.0), 0, keepdims=True)
    rev = jnp.sum(jnp.where(first, 0.0, term), 0, keepdims=True)
    both = jnp.concatenate([fwd, rev, jnp.zeros((6, D), F32)], 0)
    hi, lo = split(both)
    swap = swap_of(r)
    r.g_gain[...] = both + pltpu.roll(mm(hi, swap) + mm(lo, swap), 7, 0)


def edge_delta(r):
    swap = swap_of(r)
    hi, lo = split(r.rows[0:HALO, :])
    grad = jnp.where(
        (iota((HALO, D), 0) & 3) < 2, r.rows[0:HALO, :], mm(hi, swap) + mm(lo, swap)
    )
    _, scale, unit = normalise(mm(onehot(edge_place(False) | edge_place(True)), r.edge[...]))
    g = grad * gain_row(r)
    return scale * (g - unit * jnp.mean(g * unit, 1, keepdims=True))


def window_outputs(r, tok, cot, mask, gated, rows, out, ing):
    half = tok.shape[0]
    T = half // MB
    gain = gain_row(r)
    swap = swap_of(r)
    back = onehot(placing(T, True))
    g = mm(back, gated[...]).astype(BF)
    source, scale, unit = normalise(tok[...])
    outs = mm(r.outw[...], swap).astype(BF)
    out[...] = (source + mm(g[:half], r.outw[...]) + mm(g[half:], outs)).astype(BF)
    hi, lo = split(rows[HALO:, :])
    grad = (
        mm(back[:half], hi)
        + mm(back[:half], lo)
        + mm(back[half:], mm(hi, swap).astype(BF))
        + mm(back[half:], mm(lo, swap).astype(BF))
    )
    g = grad * gain
    mrow = jnp.concatenate([mask[0:1, :], mask[1:2, :]], 1)
    keep = onehot((iota((half, half), 0) == iota((half, half), 1)) & (mrow != 0))
    ing[...] = scale * (g - unit * jnp.mean(g * unit, 1, keepdims=True)) + mm(keep, cot[...])


def outputs_body(r):
    window_outputs(r, r.l_tok, r.l_cot, r.l_mask, r.l_gated, r.l_rows, r.l_out, r.l_ing)
    window_outputs(r, r.s_tok, r.s_cot, r.s_mask, r.s_gated, r.s_rows, r.s_out, r.s_ing)
    r.mark[...] = jnp.zeros((8, LT), F32)


def post_scratch(T):
    R = 4 * T
    return dict(
        acc=((64, E), F32),
        gg=((R, E), F32),
        gco=((R + 2 * HALO, E), F32),
        il=((R, E), BF),
        gated=((R, E), BF),
        gz=((R, E), BF),
        z=((R, LT), BF),
        gp=((R + HALO, 2 * E), BF),
    )


GRADS = dict(
    g_inT=((2 * E, D), F32), g_out=((E, D), F32), g_peT=((LT, E), F32), g_gain=((8, D), F32)
)


def rows_out(T):
    return dict(rows=((4 * T + HALO, D), F32))


STATE_ROWS = 4 * 8 * NP
ELEMENT = STATE_ROWS + 4 * 8


def to_spans(r, at, rows):
    seq = lax.axis_index("seq")
    count = r.carry_out.shape[0] // ELEMENT

    def start(j):
        dst = r.carry_out.at[pl.ds(pl.multiple_of(j * ELEMENT + at, 32), rows), :]

        @pl.when(j > seq)
        def _():
            pltpu.make_async_copy(r.later.at[at : at + rows, :], dst, r.carry_sem).start()

        @pl.when(j <= seq)
        def _():
            pltpu.make_async_copy(r.earlier.at[at : at + rows, :], dst, r.carry_sem).start()

    loop(count, start)


def send_sums(r, T):
    def add(i, total):
        return total + r.st[pl.ds(pl.multiple_of(i * 8, 8), 8), :]

    sums = lax.fori_loop(0, T // 2, add, jnp.zeros((8, E), F32))
    sums = sums + pltpu.roll(sums, 4, 0)
    sums = jnp.concatenate([sums[:, lanes_of(e)] for e in range(E // LT)], 0).astype(BF)
    r.later[STATE_ROWS:, :] = sums
    r.earlier[STATE_ROWS:, :] = sums
    to_spans(r, STATE_ROWS, 32)


def send_elements(r, e):
    normed = (iota((8 * NP, LT), 0) & 3) < 2
    state, adjoint = r.ends[0:64, lanes_of(e)], r.ends[64:128, lanes_of(e)]
    at = 64 * e
    r.later[at : at + 64, :] = jnp.where(normed, state, adjoint).astype(BF)
    r.earlier[at : at + 64, :] = jnp.where(normed, adjoint, state).astype(BF)
    to_spans(r, at, 64)


def wait_elements(r):
    pltpu.make_async_copy(r.carry_out, r.carry_out, r.carry_sem).wait()


def enter(r):
    seq = lax.axis_index("seq")
    count = r.elements.shape[0] // ELEMENT
    r.fold[...] = jnp.zeros((16 * NP, E), F32)

    def add(half, j):
        base = j * ELEMENT
        sums = r.elements[pl.ds(pl.multiple_of(base + STATE_ROWS, 32), 32), :].astype(F32)
        for e in range(E // LT):
            es = lanes_of(e)
            x = r.elements[pl.ds(pl.multiple_of(base + e * 64, 32), 64), :].astype(F32)
            for k in range(NP):
                ks = slice(8 * k, 8 * k + 8)
                at = slice(64 * half + 8 * k, 64 * half + 8 * k + 8)
                decay = jnp.exp2(r.r2[ks, es] * sums[8 * e : 8 * e + 8])
                r.fold[at, es] = decay * r.fold[at, es] + x[ks]

    loop(seq, lambda i: add(0, i))
    loop(count - 1 - seq, lambda i: add(1, count - 1 - i))
    normed = (iota((8 * NP, E), 0) & 3) < 2
    r.entering[0:64, :] = jnp.where(normed, r.fold[0:64, :], r.fold[64:128, :])
    r.entering[64:128, :] = jnp.where(normed, r.fold[64:128, :], r.fold[0:64, :])


def long_start_body(r, T, packed):

    def ready():
        if packed:
            unpack(r)
            r.gain[...] = gain_of(r)
        derive(r)
        send(r, *(k for k in r.early if k not in PREP_OUTS))

    prep(r, T, True, ready)
    send(r, *PREP_OUTS)
    maps(r, T)
    send_sums(r, T)
    for e in range(E // LT):
        scan_forward(r, T, None, False, tiles=(e,))
        scan_adjoint_local(r, T, tiles=(e,))
        send_elements(r, e)
    wait_elements(r)


def short_windows_body(r, T):
    prep(r, T, False)
    maps(r, T)
    scan_forward(r, T, None, True)
    scan_backward(r, T, None)
    post(r, T, False)
    param_grads(r)


FROM_SHORT = ("s_inT", "s_out", "s_peT", "s_gain")
LONG_FIRST = ("sel", "elements", "r2", "st", "si", "gm")
LONG_FAR = LONG_FIRST + LATE_LONG + FROM_SHORT


def long_windows_body(r, T):
    fetch(r, *LONG_FIRST)
    arrived(r, "sel")
    maps(r, T)
    arrived(r, "elements", "r2")
    enter(r)
    arrived(r, "st", "si", "gm")
    fetch(r, *LATE_LONG, *FROM_SHORT)
    scan_forward(r, T, r.entering, True)
    scan_backward(r, T, r.entering)
    arrived(r, "inT", "outw", "dtw2")
    post(r, T, True)
    param_grads(r)
    arrived(r, *FROM_SHORT)
    finish_grads(r)


def finish_grads(r):
    r.g_peT[...] += r.s_peT[...]
    r.g_gain[...] = (r.g_gain[...] + r.s_gain[...]) / gain_row(r)
    if not hasattr(r, "give"):
        r.g_inT[...] += r.s_inT[...]
        r.g_out[...] += r.s_out[...]
        r.delta[...] = edge_delta(r)
        return
    lane, col = iota((D, E), 1), iota((D, E), 0)
    pick = onehot(((lane // 16) == (col // 8)) & ((lane % 16) == (col % 8)))
    peT = r.g_peT[...] + jnp.where(
        iota((LT, E), 0) == AT_SMALL + 7, mm(r.g_gain[0:1, :].astype(BF), pick), 0.0
    )
    r.pe_out[...] = peT.T.astype(BF)
    mine, seq = lax.axis_index("dp"), lax.axis_index("seq")
    count = E // (2 * OUT_ROWS)
    delta = edge_delta(r).astype(BF)
    row, col = iota((8, HALO), 0), iota((8, HALO), 1)
    of = 4 * (row & 3) + (row >> 2)
    r.deltas[0:EDGE, :] = halves(mm(onehot(col == of), delta))
    r.deltas[EDGE:, :] = halves(mm(onehot(col == of + 2), delta))
    slots = [(4 * near + q, seq ^ (near | far)) for near in range(4) for q, far in enumerate(SUM_SLOTS)]
    for dst, d, step in ((r.give, 1 - mine, PACK), (r.keep, mine, GATHER)):
        for slot, dev in slots:
            at = slot * step
            in_at = pl.multiple_of((d * count + dev) * IN_ROWS, IN_ROWS)
            out_at = pl.multiple_of((d * count + dev) * OUT_ROWS, OUT_ROWS)
            for half in range(2):
                lanes = slice(half * LT, (half + 1) * LT)
                rows = pl.ds(in_at, IN_ROWS)
                dst[at + half * IN_ROWS : at + (half + 1) * IN_ROWS, :] = (
                    r.g_inT[rows, lanes] + r.s_inT[rows, lanes]
                ).astype(BF)
                low = at + 2 * IN_ROWS + half * OUT_ROWS
                rows = pl.ds(out_at, OUT_ROWS)
                dst[low : low + OUT_ROWS, :] = (r.g_out[rows, lanes] + r.s_out[rows, lanes]).astype(BF)
            dst[at + PACK - CH_ROWS : at + PACK, :] = r.pe_out[pl.ds(out_at, CH_ROWS), :]
    zero = jnp.zeros((EDGE, LT), BF)
    for slot, dev in slots:
        at = slot * GATHER + PACK
        r.keep[at : at + EDGE, :] = jnp.where(dev == seq - 1, r.deltas[0:EDGE, :], zero)
        r.keep[at + EDGE : at + 2 * EDGE, :] = jnp.where(dev == seq + 1, r.deltas[EDGE:, :], zero)


def total(*parts):
    result = parts[0].astype(F32)
    for x in parts[1:]:
        result = result + x.astype(F32)
    return result


def add_core_body(r):
    fetch(r, "keep")
    arrived(r, "keep")
    for near in range(4):
        part = getattr(r, f"part{near}")
        for q in range(4):
            at, keep, got = q * GATHER, (4 * near + q) * GATHER, (4 * near + q) * PACK
            part[at : at + PACK, :] = total(
                r.keep[keep : keep + PACK, :], r.got[got : got + PACK, :]
            ).astype(BF)
            part[at + PACK : at + GATHER, :] = r.keep[keep + PACK : keep + GATHER, :]


def add_near_body(r):
    for i, dst in enumerate((r.low, r.high)):
        at = slice(i * 2 * GATHER, (i + 1) * 2 * GATHER)
        dst[...] = total(r.part0[at, :], r.got1[at, :], r.got2[at, :], r.got3[at, :]).astype(BF)


def add_far_body(r):
    r.own[...] = total(r.low[0:GATHER, :], r.got[0:GATHER, :]).astype(BF)
    r.last[...] = total(r.low[GATHER:, :], r.got[GATHER:, :]).astype(BF)


def scatter(give, keep, after):
    def swapped(x, mask):
        count = lax.axis_size("seq")
        return lax.ppermute(x, "seq", [(i, i ^ mask) for i in range(count)])

    got = lax.ppermute(give, "dp", [(0, 1), (1, 0)])
    four = ((4 * GATHER, LT), BF)
    parts = run(
        "add_core",
        add_core_body,
        dict(got=got, keep=keep),
        {f"part{i}": four for i in range(4)},
        far=("keep",),
        vmem=8,
    )
    near = {f"got{i}": swapped(parts[f"part{i}"], i) for i in range(1, 4)}
    two = ((2 * GATHER, LT), BF)
    sums = run(
        "add_near",
        add_near_body,
        dict(part0=parts["part0"], after=after, **near),
        dict(low=two, high=two),
        vmem=8,
    )
    one = ((GATHER, LT), BF)
    ends = run(
        "add_far",
        add_far_body,
        dict(low=sums["low"], got=swapped(sums["high"], 8)),
        dict(own=one, last=one),
        vmem=8,
    )
    return ends["own"], swapped(ends["last"], 4)


def final_body(r, packed):
    r.grad[...] = r.ing[...]
    T = r.grad.shape[0] // MB
    if packed:
        block = total(r.own[...], r.got[...])
        from_next, from_prev = (
            jnp.concatenate([x[:8], x[8:]], 1)
            for x in (block[PACK : PACK + EDGE], block[PACK + EDGE :])
        )
    else:
        from_prev, from_next = r.from_prev[...], r.from_next[...]
    for mb in range(MB):
        for j in range(4):
            prev = 4 * mb + j if packed else 4 * j + 2 + mb
            follow = 4 * mb + j if packed else 4 * j + mb
            row = mb * T + T - 4 + j
            r.grad[row : row + 1, :] += from_next[follow : follow + 1, :]
            row = mb * T + 3 - j
            r.grad[row : row + 1, :] += from_prev[prev : prev + 1, :]
    if not packed:
        return
    for half in range(2):
        lanes = slice(half * LT, (half + 1) * LT)
        r.in_wT[:, lanes] = block[half * IN_ROWS : (half + 1) * IN_ROWS]
        low = 2 * IN_ROWS + half * OUT_ROWS
        r.out_w[:, lanes] = block[low : low + OUT_ROWS]
    pe = block[PACK - CH_ROWS : PACK]
    hi, lo = split(pe)
    peT = mm(eye(LT), hi, NT) + mm(eye(LT), lo, NT)
    r.x_w[...] = pe[:, : 3 * N]
    r.a_log[...] = pe[:, AT_A : AT_A + N]
    r.dt_w[...] = peT[AT_DT : AT_DT + N]
    small = peT[AT_SMALL : AT_SMALL + 8]
    r.conv_w[...] = small[0:4]
    r.conv_b[...] = small[4:5]
    r.dt_b[...] = small[5:6]
    r.skip[...] = small[6:7]
    r.gain[...] = small[7:8, 0 : r.gain.shape[1]]


PREP_OUTS = ("V", "GR", "ip", "inner", "slope", "silu", "gslope", "st", "sz", "si", "gm", "sel")


def prep_outs(T):
    R = 4 * T
    wide = ((R, E), F32)
    return dict(
        V=((R + HALO, D), BF),
        GR=((R, D), BF),
        ip=((R + HALO, E), F32),
        inner=wide,
        slope=wide,
        silu=wide,
        gslope=wide,
        st=wide,
        sz=wide,
        si=wide,
        gm=wide,
        sel=((R, LT), F32),
    )


def local(
    long_tokens,
    short_tokens,
    long_cotangent,
    short_cotangent,
    long_mask,
    short_mask,
    complement,
    norm_gain,
    in_weight,
    conv_weight,
    conv_bias,
    x_weight,
    dt_weight,
    dt_bias,
    a_log,
    d_skip,
    out_weight,
):
    count = lax.axis_size("seq")
    span, short = long_tokens.shape[2], short_tokens.shape[2]
    packed = count == 16 and out_weight.shape[0] == OUT_ROWS and in_weight.shape[1] == IN_ROWS
    comp = complement.reshape(1, D)
    up = [(i, i + 1) for i in range(count - 1)]
    down = [(i + 1, i) for i in range(count - 1)]

    def tokens_of(tok, cot, mask):
        T = tok.shape[2]
        return dict(
            tok=tok.reshape(MB * T, D), cot=cot.reshape(MB * T, D), mask=mask.reshape(MB, T)
        )

    long_in = tokens_of(long_tokens, long_cotangent, long_mask)
    short_in = tokens_of(short_tokens, short_cotangent, short_mask)

    near = dict(comp=comp, **long_in)

    if packed:
        packing = run(
            "pack",
            pack_body,
            dict(
                gain=norm_gain.reshape(1, -1),
                in_wT=in_weight.T,
                conv_w=conv_weight,
                conv_b=conv_bias.reshape(1, -1),
                x_w=x_weight,
                dt_w=dt_weight,
                dt_b=dt_bias.reshape(1, -1),
                a_log=a_log,
                skip=d_skip.reshape(1, -1),
                out_w=out_weight,
                comp=comp,
                **long_in,
            ),
            dict(
                buf=((GATHER, LT), BF),
                **{k + "_near": (v.shape, v.dtype) for k, v in near.items()},
            ),
            dict(rows=((8, CH_ROWS), F32)),
            pin={k: pltpu.VMEM for k in ("buf", *(k + "_near" for k in near))},
        )
        weights_in = gather(packing["buf"])
        near = {k: packing[k + "_near"] for k in near}
    else:
        tail = lax.ppermute(long_tokens[:, 0, span - 4 :, :].reshape(8, D), "seq", up)
        head = lax.ppermute(long_tokens[:, 0, :4, :].reshape(8, D), "seq", down)

        def whole(a, axis):
            return lax.all_gather(a, BOTH, axis=axis, tiled=True)

        small = jnp.stack([*conv_weight, conv_bias, dt_bias, d_skip, jnp.zeros_like(d_skip)])
        columns = jnp.concatenate([a_log, small.T], 1)
        hi = columns.astype(BF)
        lo = (columns - hi.astype(F32)).astype(BF)
        zero = jnp.zeros((columns.shape[0], LT - AT_SMALL - 16), BF)
        chan = jnp.concatenate(
            [x_weight, dt_weight.T, hi[:, :N], lo[:, :N], hi[:, N:], lo[:, N:], zero], 1
        )
        weights_in = dict(
            inT=whole(in_weight.T, 0),
            outw=whole(out_weight, 0),
            pe=whole(chan, 0),
            gain=whole(norm_gain, 0).reshape(1, D),
            edge=jnp.concatenate([tail, head], 0),
        )

    derived = dict(
        r2=((8 * NP, E), F32),
        rowp=((8, E), F32),
        rate=((N, E), F32),
        dtw2=((LT, E), BF),
        xwT=((LT, E), BF),
    )
    unpacked = dict(
        inT=((2 * E, D), BF),
        outw=((E, D), BF),
        pe=((E, LT), BF),
        gain=((8, D), F32),
        edge=((HALO, D), BF),
    )
    started = run(
        "long_start",
        functools.partial(long_start_body, T=span, packed=packed),
        dict(near, **weights_in),
        dict(
            carry=((count * ELEMENT, LT), BF), **prep_outs(span), **derived, **(unpacked if packed else {})
        ),
        dict(
            il=((4 * span, E), BF),
            imb=((8 * span, NP * LT), F32),
            omb=((8 * span, NP * LT), F32),
            ends=((128, E), F32),
            later=((ELEMENT, LT), BF),
            earlier=((ELEMENT, LT), BF),
            carry_sem=pltpu.SemaphoreType.DMA,
            **(dict(edges=((count * 2 * EDGE, LT), BF)) if packed else {}),
        ),
        flops=1 << 33,
        early=PREP_OUTS + tuple(derived) + (tuple(unpacked) if packed else ()),
        placed=("carry",),
        pin={
            k: pltpu.HBM
            for k in PREP_OUTS + tuple(derived) + (tuple(unpacked) if packed else ()) + ("carry",)
        },
        vmem=40,
    )
    weights = {k: started[k] for k in derived}
    for k in unpacked:
        weights[k] = started[k] if packed else weights_in[k]

    elements = lax.all_to_all(started["carry"], "seq", 0, 0, tiled=True)
    shorts = run(
        "short_windows",
        functools.partial(short_windows_body, T=short),
        dict(
            comp=comp,
            **short_in,
            **{
                k: weights[k]
                for k in ("inT", "outw", "pe", "gain", "dtw2", "xwT", "rowp", "r2", "rate")
            },
        ),
        dict(GRADS, **rows_out(short), gated=((4 * short, E), BF)),
        {
            k: v
            for k, v in dict(scan_scratch(short), **post_scratch(short), **prep_outs(short)).items()
            if k != "gated"
        },
        flops=1 << 36,
        vmem=63,
    )

    ins = dict(
        elements=elements,
        comp=comp,
        **{k: weights[k] for k in ("edge", "r2", "rowp", "rate", "gain", "inT", "outw", "xwT", "dtw2")},
        **{k: started[k] for k in PREP_OUTS},
        s_inT=shorts["g_inT"],
        s_out=shorts["g_out"],
        s_peT=shorts["g_peT"],
        s_gain=shorts["g_gain"],
    )
    outs = dict(rows_out(span), gated=((4 * span, E), BF))
    scratch = dict(entering=((16 * NP, E), F32), fold=((16 * NP, E), F32))
    if packed:
        outs.update(give=((count * PACK, LT), BF), keep=((count * GATHER, LT), BF))
        scratch.update(GRADS, pe_out=((E, LT), BF), deltas=((2 * EDGE, LT), BF))
    else:
        outs.update(GRADS, delta=((HALO, D), F32))
    scratch.update(scan_scratch(span))
    scratch.update({k: v for k, v in post_scratch(span).items() if k not in outs})
    longs = run(
        "long_windows",
        functools.partial(long_windows_body, T=span),
        ins,
        outs,
        scratch,
        flops=1 << 35,
        far=tuple(k for k in LONG_FAR),
        pin=dict(give=pltpu.VMEM, keep=pltpu.VMEM) if packed else None,
        vmem=56,
    )

    outs = dict(
        l_out=((MB * span, D), BF),
        l_ing=((MB * span, D), F32),
        s_out=((MB * short, D), BF),
        s_ing=((MB * short, D), F32),
        mark=((8, LT), F32),
    )
    ins = dict(comp=comp, outw=weights["outw"], gain=weights["gain"])
    ins.update({"l_" + k: v for k, v in long_in.items()}, l_gated=longs["gated"], l_rows=longs["rows"])
    ins.update(
        {"s_" + k: v for k, v in short_in.items()},
        s_gated=shorts["gated"],
        s_rows=shorts["rows"],
    )
    finished = run("outputs", outputs_body, ins, outs, flops=1 << 32, vmem=32)
    ins = dict(ing=finished["l_ing"])
    outs = dict(grad=((MB * span, D), F32))
    if packed:
        ins["own"], ins["got"] = scatter(longs["give"], longs["keep"], finished["mark"])
        outs.update(
            gain=((1, D // (2 * count)), F32),
            in_wT=((IN_ROWS, D), F32),
            conv_w=((4, CH_ROWS), F32),
            conv_b=((1, CH_ROWS), F32),
            x_w=((CH_ROWS, 3 * N), F32),
            dt_w=((N, CH_ROWS), F32),
            dt_b=((1, CH_ROWS), F32),
            a_log=((CH_ROWS, N), F32),
            skip=((1, CH_ROWS), F32),
            out_w=((OUT_ROWS, D), F32),
        )
    else:
        ins["from_next"] = lax.ppermute(longs["delta"], "seq", down)
        ins["from_prev"] = lax.ppermute(longs["delta"], "seq", up)
    done = run("final", functools.partial(final_body, packed=packed), ins, outs, vmem=8)
    if packed:
        grads = {k: done[k] for k in outs if k != "grad"}
        grads["in_w"] = grads["in_wT"].T
        for k in ("gain", "conv_b", "dt_b", "skip"):
            grads[k] = grads[k].reshape(-1)
    else:

        def own(a, axis=0):
            return lax.psum_scatter(a, BOTH, scatter_dimension=axis, tiled=True)

        pe = own(longs["g_peT"].T)
        grads = dict(
            gain=own(longs["g_gain"][0]),
            in_w=own(longs["g_inT"]).T,
            conv_w=pe[:, AT_SMALL : AT_SMALL + 4].T,
            conv_b=pe[:, AT_SMALL + 4],
            x_w=pe[:, : 3 * N],
            dt_w=pe[:, AT_DT : AT_DT + N].T,
            dt_b=pe[:, AT_SMALL + 5],
            a_log=pe[:, AT_A : AT_A + N],
            skip=pe[:, AT_SMALL + 6],
            out_w=own(longs["g_out"]),
        )
    order = ("gain", "in_w", "conv_w", "conv_b", "x_w", "dt_w", "dt_b", "a_log", "skip", "out_w")
    return (
        finished["l_out"].reshape(long_tokens.shape),
        finished["s_out"].reshape(short_tokens.shape),
        done["grad"].reshape(long_tokens.shape),
        finished["s_ing"].reshape(short_tokens.shape),
    ) + tuple(grads[k] for k in order)


def solution(mesh):
    long_spec, short_spec = P(None, "dp", "seq", None), P(None, BOTH, None, None)
    rows, columns, vector = P(BOTH, None), P(None, BOTH), P(BOTH)
    params = (vector, columns, columns, vector, rows, columns, vector, rows, vector, rows)
    return jax.shard_map(
        local,
        mesh=mesh,
        in_specs=(
            long_spec,
            short_spec,
            long_spec,
            short_spec,
            P(None, "dp", "seq"),
            P(None, BOTH, None),
            P(),
        )
        + params,
        out_specs=(long_spec, short_spec, long_spec, short_spec) + params,
        check_vma=False,
    )
```

```python
import functools
import types

import jax
import jax.numpy as jnp
from jax import lax
from jax.experimental import pallas as pl
from jax.experimental.pallas import tpu as pltpu
from jax.sharding import PartitionSpec as P

EPS = 1e-05
D, E, N, MB, HALO = 256, 512, 16, 2, 16
LT = 128
NP = N // 2
LOG2E = 1.4426950408889634
LN2 = 0.6931471805599453
F32, BF = jnp.float32, jnp.bfloat16
NT = (((1,), (1,)), ((), ()))
TN = (((0,), (0,)), ((), ()))
BOTH = ("dp", "seq")
IN_ROWS, OUT_ROWS, CH_ROWS = 32, 16, 16
PACK = 2 * IN_ROWS + 2 * OUT_ROWS + CH_ROWS
EDGE = 16
GATHER = PACK + 2 * EDGE
FAR = (8, 4)
SLOTS = (0, 8, 4, 12)
SUM_SLOTS = (0, 4, 8, 12)
AT_DT, AT_A, AT_SMALL = 48, 64, 96


def mm(a, b, dims=None):
    if dims is None:
        return jnp.dot(a, b, preferred_element_type=F32)
    return lax.dot_general(a, b, dims, preferred_element_type=F32)


def iota(shape, axis):
    return lax.broadcasted_iota(jnp.int32, shape, axis)


def onehot(cond):
    return jnp.where(cond, 1.0, 0.0).astype(BF)


def eye(n):
    return onehot(iota((n, n), 0) == iota((n, n), 1))


def split(x):
    hi = x.astype(BF)
    return hi, (x - hi.astype(F32)).astype(BF)


def silu_of_half(h):
    th = jnp.tanh(h)
    value = h * th + h
    u = 0.5 * th
    return value, (0.5 + u) + value * (0.5 - u)


def plus(total, x):
    return x if total is None else total + x


def loop(count, body):
    lax.fori_loop(0, count, lambda i, c: (body(i), c)[1], 0)


def run(name, body, ins, outs, scratch=None, flops=0, far=(), early=(), placed=(), pin=None, hold=(), vmem=60):
    scratch = dict(scratch or {}, **{k: outs[k] for k in early})
    scratch.update({k: (ins[k].shape, ins[k].dtype) for k in far})
    if far:
        scratch["in_sems"] = pltpu.SemaphoreType.DMA((len(far),))
    if early:
        scratch["out_sems"] = pltpu.SemaphoreType.DMA((len(early),))
    in_names, scratch_names = [k + "_far" if k in far else k for k in ins], list(scratch)
    out_names = [k + "_out" if k in early or k in placed else k for k in outs]

    def kernel(*refs):
        r = types.SimpleNamespace(**dict(zip(in_names + out_names + scratch_names, refs)))
        r.early, r.sent, r.fetched = tuple(early), [], []
        body(r)
        for copy in r.sent:
            copy.wait()

    def spec(key):
        return pl.BlockSpec(memory_space=pltpu.HBM if key in far else pltpu.VMEM)

    def at(key, value):
        if key in hold or key in far:
            return pltpu.with_memory_space_constraint(value, pltpu.HBM if key in far else pltpu.VMEM)
        return value

    result = pl.pallas_call(
        kernel,
        out_shape=tuple(
            pin[k](*v) if pin and k in pin else jax.ShapeDtypeStruct(*v) for k, v in outs.items()
        ),
        in_specs=[spec(k) for k in ins],
        out_specs=tuple(
            pl.BlockSpec(memory_space=pltpu.HBM if k in early or k in placed else pltpu.VMEM)
            for k in outs
        ),
        scratch_shapes=[
            pltpu.VMEM(*scratch[k]) if isinstance(scratch[k], tuple) else scratch[k]
            for k in scratch_names
        ],
        compiler_params=pltpu.CompilerParams(vmem_limit_bytes=vmem << 20),
        cost_estimate=pl.CostEstimate(flops=flops, bytes_accessed=1 << 20, transcendentals=0),
        name=name,
    )(*(at(k, v) for k, v in ins.items()))
    return dict(zip(outs, result))


def send(r, *names):
    for name in names:
        if name in r.early:
            copy = pltpu.make_async_copy(
                getattr(r, name), getattr(r, name + "_out"), r.out_sems.at[r.early.index(name)]
            )
            copy.start()
            r.sent.append(copy)


def fetch(r, *names):
    for name in names:
        copy = pltpu.make_async_copy(
            getattr(r, name + "_far"), getattr(r, name), r.in_sems.at[len(r.fetched)]
        )
        copy.start()
        r.fetched.append((name, copy))


def arrived(r, *names):
    for name, copy in r.fetched:
        if name in names:
            copy.wait()


def pack_body(r):
    r.rows[...] = jnp.zeros((8, CH_ROWS), F32)
    r.rows[0:4, :] = r.conv_w[...]
    r.rows[4:5, :] = r.conv_b[...]
    r.rows[5:6, :] = r.dt_b[...]
    r.rows[6:7, :] = r.skip[...]
    r.rows[7:8, 0 : r.gain.shape[1]] = r.gain[...]
    in_t = r.in_wT[...]
    small = jnp.concatenate(split(r.rows[...]), 0)

    def place(a, at, turned=False):
        n = a.shape[0 if turned else 1]
        return mm(a, onehot(iota((n, LT), 0) + at == iota((n, LT), 1)), TN if turned else None)

    a_hi, a_lo = split(r.a_log[...])
    chan = (
        place(r.x_w[...], 0)
        + place(r.dt_w[...], AT_DT, True)
        + place(a_hi, AT_A)
        + place(a_lo, AT_A + N)
        + place(small, AT_SMALL, True)
    ).astype(BF)
    out_w = r.out_w[...]
    for half in range(2):
        lanes = slice(half * LT, (half + 1) * LT)
        r.buf[half * IN_ROWS : (half + 1) * IN_ROWS, :] = in_t[:, lanes]
        low = 2 * IN_ROWS + half * OUT_ROWS
        r.buf[low : low + OUT_ROWS, :] = out_w[:, lanes]
    r.buf[PACK - CH_ROWS : PACK, :] = chan
    for name in ("comp", "tok", "cot", "mask", "s_tok", "s_cot", "s_mask"):
        getattr(r, name + "_near")[...] = getattr(r, name)[...]
    T = r.tok.shape[0] // MB
    for which, first in enumerate((T - 16, 0)):
        rows = [r.tok[mb * T + first : mb * T + first + 16, :].astype(F32) for mb in range(MB)]
        at = 12 if first else 0
        x = jnp.concatenate([x[at : at + 4] for x in rows], 0)
        r.buf[PACK + which * EDGE : PACK + (which + 1) * EDGE, :] = halves(x)


def halves(x):
    return jnp.concatenate([x[:, :LT], x[:, LT:]], 0).astype(BF)


def get_edges(buf, step, at):
    seq = lax.axis_index("seq")
    count = buf.shape[0] // step
    result = []
    before, after = jnp.maximum(seq - 1, 0), jnp.minimum(seq + 1, count - 1)
    for j, low, there in ((before, at[0], seq > 0), (after, at[1], seq < count - 1)):
        x = buf[pl.ds(pl.multiple_of(j * step + low, 16), EDGE), :].astype(F32)
        x = jnp.concatenate([x[:8], x[8:]], 1)
        result.append(jnp.where(there, x, 0.0))
    return result


def unpack(r):
    mine, seq = lax.axis_index("dp"), lax.axis_index("seq")
    count = E // (2 * OUT_ROWS)
    for near in range(4):
        for src, d in ((getattr(r, f"mine{near}"), mine), (getattr(r, f"other{near}"), 1 - mine)):
            for q, far in enumerate(SLOTS):
                at = q * GATHER
                dev = seq ^ (near | far)
                in_at = pl.multiple_of((d * count + dev) * IN_ROWS, IN_ROWS)
                out_at = pl.multiple_of((d * count + dev) * OUT_ROWS, OUT_ROWS)
                for half in range(2):
                    lanes = slice(half * LT, (half + 1) * LT)
                    r.inT[pl.ds(in_at, IN_ROWS), lanes] = src[
                        at + half * IN_ROWS : at + (half + 1) * IN_ROWS, :
                    ]
                    low = at + 2 * IN_ROWS + half * OUT_ROWS
                    r.outw[pl.ds(out_at, OUT_ROWS), lanes] = src[low : low + OUT_ROWS, :]
                r.pe[pl.ds(out_at, CH_ROWS), :] = src[at + PACK - CH_ROWS : at + PACK, :]
                if d is mine:
                    r.edges[pl.ds(pl.multiple_of(dev * 2 * EDGE, 2 * EDGE), 2 * EDGE), :] = src[
                        at + PACK : at + GATHER, :
                    ]
    r.edge[...] = jnp.concatenate(get_edges(r.edges, 2 * EDGE, (0, EDGE)), 0).astype(BF)


def join_body(r):
    rows = r.a.shape[0]
    r.both[0:rows, :] = r.a[...]
    r.both[rows:, :] = r.b[...]


def gather(buf):
    def swapped(x, mask):
        count = lax.axis_size("seq")
        return lax.ppermute(x, "seq", [(i, i ^ mask) for i in range(count)])

    for mask in FAR:
        buf = run(
            f"join{mask}",
            join_body,
            dict(a=buf, b=swapped(buf, mask)),
            dict(both=((2 * buf.shape[0], LT), BF)),
            vmem=8,
        )["both"]
    mine = [buf] + [swapped(buf, near) for near in range(1, 4)]
    other = [lax.ppermute(x, "dp", [(0, 1), (1, 0)]) for x in mine]
    return dict(
        {f"mine{i}": x for i, x in enumerate(mine)}, **{f"other{i}": x for i, x in enumerate(other)}
    )


def derive(r):
    peT = mm(eye(LT), r.pe[...], NT)
    small = peT[AT_SMALL : AT_SMALL + 8] + peT[AT_SMALL + 8 : AT_SMALL + 16]
    r.rowp[...] = small
    rate = -jnp.exp(peT[AT_A : AT_A + N] + peT[AT_A + N : AT_A + 2 * N])
    r.rate[...] = rate
    for n in range(N):
        r.r2[4 * n : 4 * n + 4, :] = jnp.broadcast_to(rate[n : n + 1] * LOG2E, (4, E))
    dt = peT[AT_DT : AT_DT + N]
    r.dtw2[...] = jnp.concatenate([dt, dt, jnp.zeros((LT - 2 * N, E), F32)], 0).astype(BF)
    r.xwT[...] = jnp.where(iota((LT, E), 0) < 3 * N, peT, 0.0).astype(BF)


def gain_of(r):
    per = E // (D // 8)
    low = mm(eye(LT), r.pe[...], NT)[AT_SMALL : AT_SMALL + 16].astype(BF)
    lane, col = iota((E, D), 0), iota((E, D), 1)
    pick = onehot(((lane // per) == (col // 8)) & ((lane % per) == (col % 8)))
    g = mm(low, pick)
    return g[0:8] + g[8:16]


def placing(T, transposed):
    shape = (2 * MB * T, 2 * MB * T)
    row, col = iota(shape, 1 if transposed else 0), iota(shape, 0 if transposed else 1)
    t, scan = row >> 2, row & 3
    turn = T.bit_length() - 1
    pos, src = col & (T - 1), col >> turn
    want = jnp.where(scan >= 2, T - 1 - t, t)
    return (src == scan) & (pos == want)


def gain_row(r):
    return r.gain[0:1, :] if r.gain.shape[0] == 1 else r.gain[7:8, :]


def normalise(tok):
    source = tok.astype(F32)
    scale = lax.rsqrt(jnp.mean(source * source, 1, keepdims=True) + EPS)
    return source, scale, source * scale


def swap_of(r):
    return onehot(iota((D, D), 0) == jnp.broadcast_to(r.comp[...], (D, D)))


def prep(r, T, halo, ready=None):
    R = 4 * T
    B = 64
    swap = swap_of(r)
    put = placing(T, False)
    mrow = jnp.concatenate([r.mask[0:1, :], r.mask[1:2, :]], 1)
    mrow = jnp.concatenate([mrow, mrow], 1)
    cot = r.cot[...]
    r.GR[...] = mm(
        onehot(put & (mrow != 0)), jnp.concatenate([cot, mm(cot, swap).astype(BF)], 0)
    ).astype(BF)
    _, _, unit = normalise(r.tok[...])
    if ready is not None:
        ready()
    gain = gain_row(r)
    normed = (unit * gain).astype(BF)
    r.V[HALO:, :] = mm(
        onehot(put), jnp.concatenate([normed, mm(normed, swap).astype(BF)], 0)
    ).astype(BF)
    if halo:
        hn = (normalise(r.edge[...])[2] * gain).astype(BF)
        r.V[0:HALO, :] = (
            mm(onehot(edge_place(False)), hn)
            + mm(onehot(edge_place(True)), mm(hn, swap).astype(BF))
        ).astype(BF)
        r.ip[0:HALO, :] = mm(r.V[0:HALO, :], r.inT[0:E, :], NT)
    else:
        r.V[0:HALO, :] = jnp.zeros((HALO, D), BF)
        r.ip[0:HALO, :] = jnp.zeros((HALO, E), F32)
    for c in range(0, E, 256):
        r.ip[HALO:, c : c + 256] = mm(r.V[HALO:, :], r.inT[c : c + 256, :], NT)
        r.silu[:, c : c + 256] = mm(r.V[HALO:, :], r.inT[E + c : E + c + 256, :], NT)
    for c in range(0, E, 256):
        r.gm[:, c : c + 256] = mm(r.GR[...], r.outw[c : c + 256, :], NT)
    w = [0.5 * r.rowp[k : k + 1, :] for k in range(5)]

    def first(i):
        r0 = pl.multiple_of(i * B, B)
        at = pl.ds(r0, B)
        x, mid = shifted(r.ip, r0, True, B)
        half = w[4] + w[0] * mid[8 : 8 + B] + w[1] * x[8 : 8 + B]
        half = half + w[2] * mid[HALO : HALO + B] + w[3] * x[HALO : HALO + B]
        inner, slope = silu_of_half(half)
        r.inner[at, :] = inner
        r.slope[at, :] = slope
        r.il[at, :] = inner.astype(BF)
        silu, slope = silu_of_half(0.5 * r.silu[at, :])
        r.silu[at, :] = silu
        r.gslope[at, :] = slope
        r.gm[at, :] = r.gm[at, :] * silu

    loop(R // B, first)
    sel = mm(r.il[...], r.pe[...])
    r.sel[...] = sel
    lane = iota((R, LT), 1)
    low = jnp.where(lane < N, sel, 0.0)
    hi = low.astype(BF).astype(F32)
    both = (hi + pltpu.roll(low - hi, N, 1)).astype(BF)
    for c in range(0, E, 256):
        r.st[:, c : c + 256] = mm(both, r.dtw2[:, c : c + 256])

    def second(i):
        at = pl.ds(pl.multiple_of(i * B, B), B)
        z = r.st[at, :] + r.rowp[5:6, :]
        u = jnp.exp2(jnp.abs(z) * -LOG2E)
        near = u * (1.0 - u * (0.5 - u * (1.0 / 3.0)))
        st = jnp.maximum(z, 0.0) + jnp.where(u < 0.01, near, jnp.log(1.0 + u))
        r.st[at, :] = st
        r.sz[at, :] = jnp.exp(z - st)
        r.si[at, :] = r.inner[at, :] * st

    loop(R // B, second)


B = 32


def shifted(ref, r0, before, B=B):
    x = ref[pl.ds(r0 + (0 if before else HALO), B + HALO), :]
    return x, pltpu.roll(x, 4 if before else B + HALO - 4, 0)


def edge_place(rev):
    row, col = iota((HALO, HALO), 0), iota((HALO, HALO), 1)
    j, scan = row >> 2, row & 3
    if rev:
        return (scan >= 2) & (col == 8 + (scan - 2) * 4 + (3 - j))
    return (scan < 2) & (col == scan * 4 + j)


def maps(r, T):
    R = 4 * T
    sel = r.sel[...]
    lane = iota((R, LT), 1)
    kept = jnp.where((lane >= N) & (lane < 3 * N), sel, 0.0)
    hi = kept.astype(BF).astype(F32)
    both = (hi + pltpu.roll(kept - hi, 64, 1)).astype(BF)
    G = 128
    r8, r4 = iota((2 * G, G), 0), iota((2 * G, G), 1)
    twice = onehot(((r8 >> 3) * 4 + (r8 & 3)) == r4)
    own = (iota((2 * G, LT), 1) & 1) == ((iota((2 * G, LT), 0) >> 2) & 1)
    l, c = iota((LT, NP * LT), 0), iota((LT, NP * LT), 1)
    l = l & 63
    spread_in = onehot((l >= N) & (l < 2 * N) & (((l - N) >> 1) == (c >> 7)))
    spread_out = onehot((l >= 2 * N) & (l < 3 * N) & (((l - 2 * N) >> 1) == (c >> 7)))
    for g in range(R // G):
        left = jnp.where(own, mm(twice, both[g * G : (g + 1) * G]), 0.0).astype(BF)
        r.imb[g * 2 * G : (g + 1) * 2 * G, :] = mm(left, spread_in)
        r.omb[g * 2 * G : (g + 1) * 2 * G, :] = mm(left, spread_out)


def dup(x, low):
    turned = pltpu.roll(x, 4, 0)
    return jnp.where(low, x, turned), jnp.where(low, turned, x)


def lanes_of(e):
    return slice(e * LT, (e + 1) * LT)


def scan_forward(r, T, start, full, U=16, tiles=range(E // LT)):
    low = iota((8, LT), 0) < 4
    for e in tiles:
        es = lanes_of(e)
        if start is None:
            first = tuple(jnp.zeros((8, LT), F32) for _ in range(NP))
        else:
            first = tuple(start[8 * k : 8 * k + 8, es] for k in range(NP))
        if full:
            for k in range(NP):
                r.states[0, 8 * k : 8 * k + 8, es] = first[k]

        def body(i, state):
            state = list(state)
            for u in range(U // 2):
                pair = i * (U // 2) + u
                row = pl.multiple_of(pair * 8, 8)
                st = dup(r.st[pl.ds(row, 8), es], low)
                si = dup(r.si[pl.ds(row, 8), es], low)
                ys = []
                for h in range(2):
                    t = pair * 2 + h
                    r8 = pl.multiple_of(t * 8, 8)
                    acc = None
                    for k in range(NP):
                        decay = jnp.exp2(st[h] * r.r2[8 * k : 8 * k + 8, es])
                        state[k] = decay * state[k] + si[h] * r.imb[pl.ds(r8, 8), lanes_of(k)]
                        if full:
                            r.states[t + 1, 8 * k : 8 * k + 8, es] = state[k]
                            y = state[k] * r.omb[pl.ds(r8, 8), lanes_of(k)]
                            acc = y if acc is None else acc + y
                    if full:
                        ys.append(acc + pltpu.roll(acc, 4, 0))
                if full:
                    r.mix[pl.ds(row, 8), es] = jnp.where(low, ys[0], ys[1])
            return tuple(state)

        last = lax.fori_loop(0, T // U, body, first)
        if not full:
            for k in range(NP):
                r.ends[8 * k : 8 * k + 8, es] = last[k]


def scan_adjoint_local(r, T, U=8, tiles=range(E // LT)):
    low = iota((8, LT), 0) < 4
    for e in tiles:
        es = lanes_of(e)

        def body(i, b):
            b = list(b)
            for u in range(U // 2):
                pair = T // 2 - 1 - (i * (U // 2) + u)
                row = pl.multiple_of(pair * 8, 8)
                st = dup(r.st[pl.ds(row, 8), es], low)
                gm = dup(r.gm[pl.ds(row, 8), es], low)
                for h in (1, 0):
                    r8 = pl.multiple_of((pair * 2 + h) * 8, 8)
                    for k in range(NP):
                        a = gm[h] * r.omb[pl.ds(r8, 8), lanes_of(k)] + b[k]
                        b[k] = jnp.exp2(st[h] * r.r2[8 * k : 8 * k + 8, es]) * a
            return tuple(b)

        last = lax.fori_loop(0, T // U, body, tuple(jnp.zeros((8, LT), F32) for _ in range(NP)))
        for k in range(NP):
            r.ends[64 + 8 * k : 64 + 8 * k + 8, es] = last[k]


def scan_backward(r, T, start, group=2, unroll=4):
    low = iota((8, LT), 0) < 4
    r.alog[...] = jnp.zeros((8 * NP, E), F32)
    r.b[...] = jnp.zeros((8 * NP, E), F32) if start is None else start[64:128, :]
    groups = E // LT // group
    for g in range(groups):
        tiles = [lanes_of(g * group + e) for e in range(group)]

        def body(i, g=g, tiles=tiles):
            for u in range(unroll):
                pair = T // 2 - 1 - (i * unroll + u)
                row = pl.multiple_of(pair * 8, 8)
                r16 = pl.multiple_of(pair * 16, 16)
                st = [dup(r.st[pl.ds(row, 8), es], low) for es in tiles]
                si = [dup(r.si[pl.ds(row, 8), es], low) for es in tiles]
                gm = [dup(r.gm[pl.ds(row, 8), es], low) for es in tiles]
                q = [[None, None] for _ in tiles]
                p = [[None, None] for _ in tiles]
                for k in range(NP):
                    ks = slice(8 * k, 8 * k + 8)
                    im = [r.imb[pl.ds(r16 + 8 * h, 8), lanes_of(k)] for h in range(2)]
                    om = [r.omb[pl.ds(r16 + 8 * h, 8), lanes_of(k)] for h in range(2)]
                    xi, xo = [None, None], [None, None]
                    for e, es in enumerate(tiles):
                        rk = r.r2[ks, es]
                        b = r.b[ks, es]
                        states = [r.states[2 * pair + h, ks, es] for h in range(3)]
                        rates = None
                        for h in (1, 0):
                            a = gm[e][h] * om[h] + b
                            b = jnp.exp2(st[e][h] * rk) * a
                            w = b * states[h]
                            q[e][h] = plus(q[e][h], w * rk)
                            rates = plus(rates, w * st[e][h])
                            p[e][h] = plus(p[e][h], a * im[h])
                            xi[h] = plus(xi[h], a * si[e][h])
                            xo[h] = plus(xo[h], states[h + 1] * gm[e][h])
                        r.b[ks, es] = b
                        r.alog[ks, es] += rates
                    cs = lanes_of(g * NP + k)
                    r.xi[pl.ds(r16, 16), cs] = jnp.concatenate(xi, 0).astype(BF)
                    r.xo[pl.ds(r16, 16), cs] = jnp.concatenate(xo, 0).astype(BF)
                for e, es in enumerate(tiles):
                    for out, v in ((r.q, q[e]), (r.p, p[e])):
                        v = [x + pltpu.roll(x, 4, 0) for x in v]
                        out[pl.ds(row, 8), es] = jnp.where(low, v[0], v[1])

        loop(T // 2 // unroll, body)
    rl, rc = iota((NP * LT, LT), 0), iota((NP * LT, LT), 1)
    red = onehot((rl >> 7) == (rc >> 1))
    W = NP * LT
    for out, x in ((r.yi, r.xi), (r.yo, r.xo)):
        total = x[:, :W]
        for g in range(1, groups):
            total = total + x[:, g * W : (g + 1) * W]
        out[...] = mm(total, red)
    G = 256
    own = (iota((G, LT), 1) & 1) == ((iota((G, LT), 0) >> 2) & 1)
    valid = own & (iota((G, LT), 1) < N)
    r8, r4 = iota((G // 2, G), 1), iota((G // 2, G), 0)
    fold = onehot(((r8 >> 3) * 4 + (r8 & 3)) == r4)
    for g in range(8 * T // G):
        at = slice(g * G, (g + 1) * G)
        y = pltpu.roll(jnp.where(valid, r.yi[at, :], 0.0), N, 1) + pltpu.roll(
            jnp.where(valid, r.yo[at, :], 0.0), 2 * N, 1
        )
        r.gsel[g * G // 2 : (g + 1) * G // 2, :] = mm(fold, y.astype(BF))


def scan_scratch(T):
    return dict(
        states=((T + 1, 8 * NP, E), F32),
        imb=((8 * T, NP * LT), F32),
        omb=((8 * T, NP * LT), F32),
        xi=((8 * T, 2 * NP * LT), BF),
        xo=((8 * T, 2 * NP * LT), BF),
        b=((8 * NP, E), F32),
        yi=((8 * T, LT), F32),
        yo=((8 * T, LT), F32),
        mix=((4 * T, E), F32),
        q=((4 * T, E), F32),
        p=((4 * T, E), F32),
        alog=((8 * NP, E), F32),
        gsel=((4 * T, LT), F32),
    )


LATE = ("ip", "inner", "slope", "silu", "gslope", "sz", "V", "GR")
LATE_LONG = LATE


def post(r, T, halo):
    R = 4 * T
    r.acc[...] = jnp.zeros((64, E), F32)
    arrived(r, *LATE)
    for c in range(0, E, 256):
        r.gg[:, c : c + 256] = mm(r.GR[...], r.outw[c : c + 256, :], NT)

    def first(i):
        at = pl.ds(pl.multiple_of(i * B, B), B)
        gp_at = pl.ds(pl.multiple_of(HALO + i * B, 16), B)
        for e in range(E // LT):
            es = lanes_of(e)
            skip = r.rowp[6:7, es]
            inner, gm, p = r.inner[at, es], r.gm[at, es], r.p[at, es]
            mixed = r.mix[at, es] + skip * inner
            r.il[at, es] = inner.astype(BF)
            r.gated[at, es] = (mixed * r.silu[at, es]).astype(BF)
            gate = r.gg[at, es] * mixed * r.gslope[at, es]
            r.gp[gp_at, E + e * LT : E + (e + 1) * LT] = gate.astype(BF)
            r.gz[at, es] = ((r.q[at, es] * LN2 + inner * p) * r.sz[at, es]).astype(BF)
            r.acc[48:56, es] += fold8(gm * inner)
            r.gg[at, es] = r.st[at, es] * p + gm * skip

    loop(R // B, first)
    lane = iota((R, LT), 1)
    gs_low = jnp.where(lane < N, mm(r.gz[...], r.dtw2[...], NT), r.gsel[...])
    gs_low = jnp.where(lane < 3 * N, gs_low, 0.0)
    r.z[...] = (
        gs_low
        + jnp.where((lane >= AT_DT) & (lane < AT_DT + N), pltpu.roll(r.sel[...], AT_DT, 1), 0.0)
        + jnp.where(lane == AT_SMALL + 5, 1.0, 0.0)
    ).astype(BF)
    gsb = gs_low.astype(BF)
    for c in range(0, E, 256):
        r.mix[:, c : c + 256] = mm(gsb, r.xwT[:, c : c + 256])
    r.gco[0:HALO, :] = jnp.zeros((HALO, E), F32)
    r.gco[HALO + R :, :] = jnp.zeros((HALO, E), F32)

    def second(i):
        r0 = pl.multiple_of(i * B, B)
        at = pl.ds(r0, B)
        x, mid = shifted(r.ip, r0, True)
        gco = (r.gg[at, :] + r.mix[at, :]) * r.slope[at, :]
        r.gco[pl.ds(r0 + HALO, B), :] = gco
        taps = (mid[8 : 8 + B], x[8 : 8 + B], mid[HALO : HALO + B], x[HALO : HALO + B])
        for k, v in enumerate(taps):
            r.acc[8 * k : 8 * k + 8, :] += fold8(gco * v)
        r.acc[32:40, :] += fold8(gco)

    loop(R // B, second)
    w = [r.rowp[k : k + 1, :] for k in range(4)]

    def third(i):
        r0 = pl.multiple_of(i * B, B)
        x, mid = shifted(r.gco, r0, False)
        rows = w[3] * x[0:B] + w[2] * mid[0:B] + w[1] * x[8 : 8 + B] + w[0] * mid[8 : 8 + B]
        r.gp[pl.ds(pl.multiple_of(r0 + HALO, 16), B), :E] = rows.astype(BF)

    loop(R // B, third)
    if halo:
        x = r.gco[0 : 2 * HALO, :]
        mid = pltpu.roll(x, 2 * HALO - 4, 0)
        rows = w[3] * x[0:16] + w[2] * mid[0:16] + w[1] * x[8:24] + w[0] * mid[8:24]
        r.gp[0:HALO, :E] = rows.astype(BF)
        r.gp[0:HALO, E:] = jnp.zeros((HALO, E), BF)
    else:
        r.gp[0:HALO, :] = jnp.zeros((HALO, 2 * E), BF)


def fold8(x):
    result = x[0:8]
    for j in range(8, x.shape[0], 8):
        result = result + x[j : j + 8]
    return result


def param_grads(r):
    zT = mm(eye(LT), r.z[...], NT).astype(BF)
    row = iota((LT, E), 0)
    peT = jnp.where(row < AT_DT, mm(zT, r.il[...]), 0.0)
    from_gz = ((row >= AT_DT) & (row < AT_A)) | (row == AT_SMALL + 5)
    peT = peT + jnp.where(from_gz, mm(zT, r.gz[...]), 0.0)
    rr, cc = iota((LT, 64), 0), iota((LT, 64), 1)
    hi, lo = split(r.alog[...])
    fold = onehot((rr >= AT_A) & (rr - AT_A == (cc >> 2)))
    rate = jnp.concatenate(
        [jnp.zeros((AT_A, E), F32), r.rate[...], jnp.zeros((LT - AT_A - N, E), F32)], 0
    )
    peT = peT + (mm(fold, hi) + mm(fold, lo)) * rate
    hi, lo = split(r.acc[...])
    fold = onehot((rr >= AT_SMALL) & (rr - AT_SMALL == (cc >> 3)))
    r.g_peT[...] = peT + mm(fold, hi) + mm(fold, lo)
    r.g_out[...] = mm(r.gated[...], r.GR[...], TN)
    for c in range(0, 2 * E, 256):
        r.g_inT[c : c + 256, :] = mm(r.gp[:, c : c + 256], r.V[...], TN)
    rows = mm(r.gp[...], r.inT[...])
    r.rows[...] = rows
    term = rows * r.V[...].astype(F32)
    first = (iota(term.shape, 0) & 3) < 2
    fwd = jnp.sum(jnp.where(first, term, 0.0), 0, keepdims=True)
    rev = jnp.sum(jnp.where(first, 0.0, term), 0, keepdims=True)
    both = jnp.concatenate([fwd, rev, jnp.zeros((6, D), F32)], 0)
    hi, lo = split(both)
    swap = swap_of(r)
    r.g_gain[...] = both + pltpu.roll(mm(hi, swap) + mm(lo, swap), 7, 0)


def edge_delta(r):
    swap = swap_of(r)
    hi, lo = split(r.rows[0:HALO, :])
    grad = jnp.where(
        (iota((HALO, D), 0) & 3) < 2, r.rows[0:HALO, :], mm(hi, swap) + mm(lo, swap)
    )
    _, scale, unit = normalise(mm(onehot(edge_place(False) | edge_place(True)), r.edge[...]))
    g = grad * gain_row(r)
    return scale * (g - unit * jnp.mean(g * unit, 1, keepdims=True))


def window_outputs(r, tok, cot, mask, gated, rows, out, ing):
    half = tok.shape[0]
    T = half // MB
    gain = gain_row(r)
    swap = swap_of(r)
    back = onehot(placing(T, True))
    g = mm(back, gated[...]).astype(BF)
    source, scale, unit = normalise(tok[...])
    outs = mm(r.outw[...], swap).astype(BF)
    out[...] = (source + mm(g[:half], r.outw[...]) + mm(g[half:], outs)).astype(BF)
    hi, lo = split(rows[HALO:, :])
    grad = (
        mm(back[:half], hi)
        + mm(back[:half], lo)
        + mm(back[half:], mm(hi, swap).astype(BF))
        + mm(back[half:], mm(lo, swap).astype(BF))
    )
    g = grad * gain
    mrow = jnp.concatenate([mask[0:1, :], mask[1:2, :]], 1)
    keep = onehot((iota((half, half), 0) == iota((half, half), 1)) & (mrow != 0))
    ing[...] = scale * (g - unit * jnp.mean(g * unit, 1, keepdims=True)) + mm(keep, cot[...])


def outputs_body(r):
    window_outputs(r, r.l_tok, r.l_cot, r.l_mask, r.l_gated, r.l_rows, r.l_out, r.l_ing)
    window_outputs(r, r.s_tok, r.s_cot, r.s_mask, r.s_gated, r.s_rows, r.s_out, r.s_ing)
    r.mark[...] = jnp.zeros((8, LT), F32)


def post_scratch(T):
    R = 4 * T
    return dict(
        acc=((64, E), F32),
        gg=((R, E), F32),
        gco=((R + 2 * HALO, E), F32),
        il=((R, E), BF),
        gated=((R, E), BF),
        gz=((R, E), BF),
        z=((R, LT), BF),
        gp=((R + HALO, 2 * E), BF),
    )


GRADS = dict(
    g_inT=((2 * E, D), F32), g_out=((E, D), F32), g_peT=((LT, E), F32), g_gain=((8, D), F32)
)


def rows_out(T):
    return dict(rows=((4 * T + HALO, D), F32))


STATE_ROWS = 4 * 8 * NP
ELEMENT = STATE_ROWS + 4 * 8


def to_spans(r, at, rows):
    seq = lax.axis_index("seq")
    count = r.carry_out.shape[0] // ELEMENT

    def start(j):
        dst = r.carry_out.at[pl.ds(pl.multiple_of(j * ELEMENT + at, 32), rows), :]

        @pl.when(j > seq)
        def _():
            pltpu.make_async_copy(r.later.at[at : at + rows, :], dst, r.carry_sem).start()

        @pl.when(j <= seq)
        def _():
            pltpu.make_async_copy(r.earlier.at[at : at + rows, :], dst, r.carry_sem).start()

    loop(count, start)


def send_sums(r, T):
    def add(i, total):
        return total + r.st[pl.ds(pl.multiple_of(i * 8, 8), 8), :]

    sums = lax.fori_loop(0, T // 2, add, jnp.zeros((8, E), F32))
    sums = sums + pltpu.roll(sums, 4, 0)
    sums = jnp.concatenate([sums[:, lanes_of(e)] for e in range(E // LT)], 0).astype(BF)
    r.later[STATE_ROWS:, :] = sums
    r.earlier[STATE_ROWS:, :] = sums
    to_spans(r, STATE_ROWS, 32)


def send_elements(r, e):
    normed = (iota((8 * NP, LT), 0) & 3) < 2
    state, adjoint = r.ends[0:64, lanes_of(e)], r.ends[64:128, lanes_of(e)]
    at = 64 * e
    r.later[at : at + 64, :] = jnp.where(normed, state, adjoint).astype(BF)
    r.earlier[at : at + 64, :] = jnp.where(normed, adjoint, state).astype(BF)
    to_spans(r, at, 64)


def wait_elements(r):
    pltpu.make_async_copy(r.carry_out, r.carry_out, r.carry_sem).wait()


def enter(r):
    seq = lax.axis_index("seq")
    count = r.elements.shape[0] // ELEMENT
    r.fold[...] = jnp.zeros((16 * NP, E), F32)

    def add(half, j):
        base = j * ELEMENT
        sums = r.elements[pl.ds(pl.multiple_of(base + STATE_ROWS, 32), 32), :].astype(F32)
        for e in range(E // LT):
            es = lanes_of(e)
            x = r.elements[pl.ds(pl.multiple_of(base + e * 64, 32), 64), :].astype(F32)
            for k in range(NP):
                ks = slice(8 * k, 8 * k + 8)
                at = slice(64 * half + 8 * k, 64 * half + 8 * k + 8)
                decay = jnp.exp2(r.r2[ks, es] * sums[8 * e : 8 * e + 8])
                r.fold[at, es] = decay * r.fold[at, es] + x[ks]

    loop(seq, lambda i: add(0, i))
    loop(count - 1 - seq, lambda i: add(1, count - 1 - i))
    normed = (iota((8 * NP, E), 0) & 3) < 2
    r.entering[0:64, :] = jnp.where(normed, r.fold[0:64, :], r.fold[64:128, :])
    r.entering[64:128, :] = jnp.where(normed, r.fold[64:128, :], r.fold[0:64, :])


def long_start_body(r, T, packed):

    def ready():
        if packed:
            unpack(r)
            r.gain[...] = gain_of(r)
        derive(r)

    prep(r, T, True, ready)
    send(r, *PREP_OUTS)
    maps(r, T)
    send_sums(r, T)
    for e in range(E // LT):
        scan_forward(r, T, None, False, tiles=(e,))
        scan_adjoint_local(r, T, tiles=(e,))
        send_elements(r, e)
    wait_elements(r)


def short_windows_body(r, T):
    prep(r, T, False)
    maps(r, T)
    scan_forward(r, T, None, True)
    scan_backward(r, T, None)
    post(r, T, False)
    param_grads(r)


FROM_SHORT = ("s_inT", "s_out", "s_peT", "s_gain")
LONG_FIRST = ("sel", "st", "si", "gm")
LONG_FAR = LONG_FIRST + LATE_LONG + FROM_SHORT


def long_windows_body(r, T):
    fetch(r, *LONG_FIRST)
    arrived(r, "sel")
    maps(r, T)
    enter(r)
    arrived(r, "st", "si", "gm")
    fetch(r, *LATE_LONG, *FROM_SHORT)
    scan_forward(r, T, r.entering, True)
    scan_backward(r, T, r.entering)
    post(r, T, True)
    param_grads(r)
    arrived(r, *FROM_SHORT)
    finish_grads(r)


def finish_grads(r):
    r.g_peT[...] += r.s_peT[...]
    r.g_gain[...] = (r.g_gain[...] + r.s_gain[...]) / gain_row(r)
    if not hasattr(r, "give"):
        r.g_inT[...] += r.s_inT[...]
        r.g_out[...] += r.s_out[...]
        r.delta[...] = edge_delta(r)
        return
    lane, col = iota((D, E), 1), iota((D, E), 0)
    pick = onehot(((lane // 16) == (col // 8)) & ((lane % 16) == (col % 8)))
    peT = r.g_peT[...] + jnp.where(
        iota((LT, E), 0) == AT_SMALL + 7, mm(r.g_gain[0:1, :].astype(BF), pick), 0.0
    )
    r.pe_out[...] = peT.T.astype(BF)
    mine, seq = lax.axis_index("dp"), lax.axis_index("seq")
    count = E // (2 * OUT_ROWS)
    delta = edge_delta(r).astype(BF)
    row, col = iota((8, HALO), 0), iota((8, HALO), 1)
    of = 4 * (row & 3) + (row >> 2)
    r.deltas[0:EDGE, :] = halves(mm(onehot(col == of), delta))
    r.deltas[EDGE:, :] = halves(mm(onehot(col == of + 2), delta))
    slots = [(4 * near + q, seq ^ (near | far)) for near in range(4) for q, far in enumerate(SUM_SLOTS)]
    for dst, d, step in ((r.give, 1 - mine, PACK), (r.keep, mine, GATHER)):
        for slot, dev in slots:
            at = slot * step
            in_at = pl.multiple_of((d * count + dev) * IN_ROWS, IN_ROWS)
            out_at = pl.multiple_of((d * count + dev) * OUT_ROWS, OUT_ROWS)
            for half in range(2):
                lanes = slice(half * LT, (half + 1) * LT)
                rows = pl.ds(in_at, IN_ROWS)
                dst[at + half * IN_ROWS : at + (half + 1) * IN_ROWS, :] = (
                    r.g_inT[rows, lanes] + r.s_inT[rows, lanes]
                ).astype(BF)
                low = at + 2 * IN_ROWS + half * OUT_ROWS
                rows = pl.ds(out_at, OUT_ROWS)
                dst[low : low + OUT_ROWS, :] = (r.g_out[rows, lanes] + r.s_out[rows, lanes]).astype(BF)
            dst[at + PACK - CH_ROWS : at + PACK, :] = r.pe_out[pl.ds(out_at, CH_ROWS), :]
    zero = jnp.zeros((EDGE, LT), BF)
    for slot, dev in slots:
        at = slot * GATHER + PACK
        r.keep[at : at + EDGE, :] = jnp.where(dev == seq - 1, r.deltas[0:EDGE, :], zero)
        r.keep[at + EDGE : at + 2 * EDGE, :] = jnp.where(dev == seq + 1, r.deltas[EDGE:, :], zero)


def total(*parts):
    result = parts[0].astype(F32)
    for x in parts[1:]:
        result = result + x.astype(F32)
    return result


def add_core_body(r):
    for near in range(4):
        part = getattr(r, f"part{near}")
        for q in range(4):
            at, keep, got = q * GATHER, (4 * near + q) * GATHER, (4 * near + q) * PACK
            part[at : at + PACK, :] = total(
                r.keep[keep : keep + PACK, :], r.got[got : got + PACK, :]
            ).astype(BF)
            part[at + PACK : at + GATHER, :] = r.keep[keep + PACK : keep + GATHER, :]


def add_near_body(r):
    for i, dst in enumerate((r.low, r.high)):
        at = slice(i * 2 * GATHER, (i + 1) * 2 * GATHER)
        dst[...] = total(r.part0[at, :], r.got1[at, :], r.got2[at, :], r.got3[at, :]).astype(BF)


def add_far_body(r):
    r.own[...] = total(r.low[0:GATHER, :], r.got[0:GATHER, :]).astype(BF)
    r.last[...] = total(r.low[GATHER:, :], r.got[GATHER:, :]).astype(BF)


def scatter(give, keep, after):
    def swapped(x, mask):
        count = lax.axis_size("seq")
        return lax.ppermute(x, "seq", [(i, i ^ mask) for i in range(count)])

    got = lax.ppermute(give, "dp", [(0, 1), (1, 0)])
    four = ((4 * GATHER, LT), BF)
    parts = run(
        "add_core",
        add_core_body,
        dict(got=got, keep=keep),
        {f"part{i}": four for i in range(4)},
        hold=("keep", "got"),
        vmem=8,
    )
    near = {f"got{i}": swapped(parts[f"part{i}"], i) for i in range(1, 4)}
    two = ((2 * GATHER, LT), BF)
    sums = run(
        "add_near",
        add_near_body,
        dict(part0=parts["part0"], after=after, **near),
        dict(low=two, high=two),
        vmem=8,
    )
    one = ((GATHER, LT), BF)
    ends = run(
        "add_far",
        add_far_body,
        dict(low=sums["low"], got=swapped(sums["high"], 8)),
        dict(own=one, last=one),
        vmem=8,
    )
    return ends["own"], swapped(ends["last"], 4)


def final_body(r, packed):
    r.grad[...] = r.ing[...]
    T = r.grad.shape[0] // MB
    if packed:
        block = total(r.own[...], r.got[...])
        from_next, from_prev = (
            jnp.concatenate([x[:8], x[8:]], 1)
            for x in (block[PACK : PACK + EDGE], block[PACK + EDGE :])
        )
    else:
        from_prev, from_next = r.from_prev[...], r.from_next[...]
    for mb in range(MB):
        for j in range(4):
            prev = 4 * mb + j if packed else 4 * j + 2 + mb
            follow = 4 * mb + j if packed else 4 * j + mb
            row = mb * T + T - 4 + j
            r.grad[row : row + 1, :] += from_next[follow : follow + 1, :]
            row = mb * T + 3 - j
            r.grad[row : row + 1, :] += from_prev[prev : prev + 1, :]
    if not packed:
        return
    for half in range(2):
        lanes = slice(half * LT, (half + 1) * LT)
        r.in_wT[:, lanes] = block[half * IN_ROWS : (half + 1) * IN_ROWS]
        low = 2 * IN_ROWS + half * OUT_ROWS
        r.out_w[:, lanes] = block[low : low + OUT_ROWS]
    pe = block[PACK - CH_ROWS : PACK]
    hi, lo = split(pe)
    peT = mm(eye(LT), hi, NT) + mm(eye(LT), lo, NT)
    r.x_w[...] = pe[:, : 3 * N]
    r.a_log[...] = pe[:, AT_A : AT_A + N]
    r.dt_w[...] = peT[AT_DT : AT_DT + N]
    small = peT[AT_SMALL : AT_SMALL + 8]
    r.conv_w[...] = small[0:4]
    r.conv_b[...] = small[4:5]
    r.dt_b[...] = small[5:6]
    r.skip[...] = small[6:7]
    r.gain[...] = small[7:8, 0 : r.gain.shape[1]]


PREP_OUTS = ("V", "GR", "ip", "inner", "slope", "silu", "gslope", "st", "sz", "si", "gm", "sel")


def prep_outs(T):
    R = 4 * T
    wide = ((R, E), F32)
    return dict(
        V=((R + HALO, D), BF),
        GR=((R, D), BF),
        ip=((R + HALO, E), F32),
        inner=wide,
        slope=wide,
        silu=wide,
        gslope=wide,
        st=wide,
        sz=wide,
        si=wide,
        gm=wide,
        sel=((R, LT), F32),
    )


def local(
    long_tokens,
    short_tokens,
    long_cotangent,
    short_cotangent,
    long_mask,
    short_mask,
    complement,
    norm_gain,
    in_weight,
    conv_weight,
    conv_bias,
    x_weight,
    dt_weight,
    dt_bias,
    a_log,
    d_skip,
    out_weight,
):
    count = lax.axis_size("seq")
    span, short = long_tokens.shape[2], short_tokens.shape[2]
    packed = count == 16 and out_weight.shape[0] == OUT_ROWS and in_weight.shape[1] == IN_ROWS
    comp = complement.reshape(1, D)
    up = [(i, i + 1) for i in range(count - 1)]
    down = [(i + 1, i) for i in range(count - 1)]

    def tokens_of(tok, cot, mask):
        T = tok.shape[2]
        return dict(
            tok=tok.reshape(MB * T, D), cot=cot.reshape(MB * T, D), mask=mask.reshape(MB, T)
        )

    long_in = tokens_of(long_tokens, long_cotangent, long_mask)
    short_in = tokens_of(short_tokens, short_cotangent, short_mask)

    near = dict(comp=comp, **long_in, **{"s_" + k: v for k, v in short_in.items()})

    if packed:
        packing = run(
            "pack",
            pack_body,
            dict(
                gain=norm_gain.reshape(1, -1),
                in_wT=in_weight.T,
                conv_w=conv_weight,
                conv_b=conv_bias.reshape(1, -1),
                x_w=x_weight,
                dt_w=dt_weight,
                dt_b=dt_bias.reshape(1, -1),
                a_log=a_log,
                skip=d_skip.reshape(1, -1),
                out_w=out_weight,
                **near,
            ),
            dict(
                buf=((GATHER, LT), BF),
                **{k + "_near": (v.shape, v.dtype) for k, v in near.items()},
            ),
            dict(rows=((8, CH_ROWS), F32)),
            pin={k: pltpu.VMEM for k in ("buf", *(k + "_near" for k in near))},
        )
        weights_in = gather(packing["buf"])
        near = {k: packing[k + "_near"] for k in near}
    else:
        tail = lax.ppermute(long_tokens[:, 0, span - 4 :, :].reshape(8, D), "seq", up)
        head = lax.ppermute(long_tokens[:, 0, :4, :].reshape(8, D), "seq", down)

        def whole(a, axis):
            return lax.all_gather(a, BOTH, axis=axis, tiled=True)

        small = jnp.stack([*conv_weight, conv_bias, dt_bias, d_skip, jnp.zeros_like(d_skip)])
        columns = jnp.concatenate([a_log, small.T], 1)
        hi = columns.astype(BF)
        lo = (columns - hi.astype(F32)).astype(BF)
        zero = jnp.zeros((columns.shape[0], LT - AT_SMALL - 16), BF)
        chan = jnp.concatenate(
            [x_weight, dt_weight.T, hi[:, :N], lo[:, :N], hi[:, N:], lo[:, N:], zero], 1
        )
        weights_in = dict(
            inT=whole(in_weight.T, 0),
            outw=whole(out_weight, 0),
            pe=whole(chan, 0),
            gain=whole(norm_gain, 0).reshape(1, D),
            edge=jnp.concatenate([tail, head], 0),
        )

    derived = dict(
        r2=((8 * NP, E), F32),
        rowp=((8, E), F32),
        rate=((N, E), F32),
        dtw2=((LT, E), BF),
        xwT=((LT, E), BF),
    )
    unpacked = dict(
        inT=((2 * E, D), BF),
        outw=((E, D), BF),
        pe=((E, LT), BF),
        gain=((8, D), F32),
        edge=((HALO, D), BF),
    )
    started = run(
        "long_start",
        functools.partial(long_start_body, T=span, packed=packed),
        dict({k: near[k] for k in ("comp", *long_in)}, **weights_in),
        dict(
            carry=((count * ELEMENT, LT), BF), **prep_outs(span), **derived, **(unpacked if packed else {})
        ),
        dict(
            il=((4 * span, E), BF),
            imb=((8 * span, NP * LT), F32),
            omb=((8 * span, NP * LT), F32),
            ends=((128, E), F32),
            later=((ELEMENT, LT), BF),
            earlier=((ELEMENT, LT), BF),
            carry_sem=pltpu.SemaphoreType.DMA,
            **(dict(edges=((count * 2 * EDGE, LT), BF)) if packed else {}),
        ),
        flops=1 << 33,
        early=PREP_OUTS,
        placed=("carry",),
        pin=dict(
            {k: pltpu.HBM for k in PREP_OUTS + ("carry",)},
            **{k: pltpu.VMEM for k in (*derived, *(unpacked if packed else ()))},
        ),
        vmem=40,
    )
    weights = {k: started[k] for k in derived}
    for k in unpacked:
        weights[k] = started[k] if packed else weights_in[k]

    elements = lax.all_to_all(started["carry"], "seq", 0, 0, tiled=True)
    shorts = run(
        "short_windows",
        functools.partial(short_windows_body, T=short),
        dict(
            comp=near["comp"],
            **{k: near["s_" + k] for k in short_in},
            **{
                k: weights[k]
                for k in ("inT", "outw", "pe", "gain", "dtw2", "xwT", "rowp", "r2", "rate")
            },
        ),
        dict(GRADS, **rows_out(short), gated=((4 * short, E), BF)),
        {
            k: v
            for k, v in dict(scan_scratch(short), **post_scratch(short), **prep_outs(short)).items()
            if k != "gated"
        },
        flops=1 << 36,
        hold=("inT", "outw", "pe", "dtw2", "xwT", "rowp", "r2", "rate", "gain", "comp", "tok", "cot", "mask"),
        vmem=56,
    )

    ins = dict(
        elements=elements,
        comp=comp,
        **{k: weights[k] for k in ("edge", "r2", "rowp", "rate", "gain", "inT", "outw", "xwT", "dtw2")},
        **{k: started[k] for k in PREP_OUTS},
        s_inT=shorts["g_inT"],
        s_out=shorts["g_out"],
        s_peT=shorts["g_peT"],
        s_gain=shorts["g_gain"],
    )
    outs = dict(rows_out(span), gated=((4 * span, E), BF))
    scratch = dict(entering=((16 * NP, E), F32), fold=((16 * NP, E), F32))
    if packed:
        outs.update(give=((count * PACK, LT), BF), keep=((count * GATHER, LT), BF))
        scratch.update(GRADS, pe_out=((E, LT), BF), deltas=((2 * EDGE, LT), BF))
    else:
        outs.update(GRADS, delta=((HALO, D), F32))
    scratch.update(scan_scratch(span))
    scratch.update({k: v for k, v in post_scratch(span).items() if k not in outs})
    longs = run(
        "long_windows",
        functools.partial(long_windows_body, T=span),
        ins,
        outs,
        scratch,
        flops=1 << 35,
        far=LONG_FAR,
        hold=(*(("elements",) if packed else ()), "edge", "r2", "rowp", "rate", "gain", "inT", "outw", "xwT", "dtw2"),
        pin={k: pltpu.VMEM for k in ("rows", "gated", *(("give", "keep") if packed else ()))},
        vmem=56,
    )

    outs = dict(
        l_out=((MB * span, D), BF),
        l_ing=((MB * span, D), F32),
        s_out=((MB * short, D), BF),
        s_ing=((MB * short, D), F32),
        mark=((8, LT), F32),
    )
    ins = dict(comp=comp, outw=weights["outw"], gain=weights["gain"])
    ins.update({"l_" + k: v for k, v in long_in.items()}, l_gated=longs["gated"], l_rows=longs["rows"])
    ins.update(
        {"s_" + k: v for k, v in short_in.items()},
        s_gated=shorts["gated"],
        s_rows=shorts["rows"],
    )
    finished = run("outputs", outputs_body, ins, outs, flops=1 << 32, hold=("l_rows", "l_gated"), vmem=32)
    ins = dict(ing=finished["l_ing"])
    outs = dict(grad=((MB * span, D), F32))
    if packed:
        ins["own"], ins["got"] = scatter(longs["give"], longs["keep"], finished["mark"])
        outs.update(
            gain=((1, D // (2 * count)), F32),
            in_wT=((IN_ROWS, D), F32),
            conv_w=((4, CH_ROWS), F32),
            conv_b=((1, CH_ROWS), F32),
            x_w=((CH_ROWS, 3 * N), F32),
            dt_w=((N, CH_ROWS), F32),
            dt_b=((1, CH_ROWS), F32),
            a_log=((CH_ROWS, N), F32),
            skip=((1, CH_ROWS), F32),
            out_w=((OUT_ROWS, D), F32),
        )
    else:
        ins["from_next"] = lax.ppermute(longs["delta"], "seq", down)
        ins["from_prev"] = lax.ppermute(longs["delta"], "seq", up)
    done = run("final", functools.partial(final_body, packed=packed), ins, outs, vmem=8)
    if packed:
        grads = {k: done[k] for k in outs if k != "grad"}
        grads["in_w"] = grads["in_wT"].T
        for k in ("gain", "conv_b", "dt_b", "skip"):
            grads[k] = grads[k].reshape(-1)
    else:

        def own(a, axis=0):
            return lax.psum_scatter(a, BOTH, scatter_dimension=axis, tiled=True)

        pe = own(longs["g_peT"].T)
        grads = dict(
            gain=own(longs["g_gain"][0]),
            in_w=own(longs["g_inT"]).T,
            conv_w=pe[:, AT_SMALL : AT_SMALL + 4].T,
            conv_b=pe[:, AT_SMALL + 4],
            x_w=pe[:, : 3 * N],
            dt_w=pe[:, AT_DT : AT_DT + N].T,
            dt_b=pe[:, AT_SMALL + 5],
            a_log=pe[:, AT_A : AT_A + N],
            skip=pe[:, AT_SMALL + 6],
            out_w=own(longs["g_out"]),
        )
    order = ("gain", "in_w", "conv_w", "conv_b", "x_w", "dt_w", "dt_b", "a_log", "skip", "out_w")
    return (
        finished["l_out"].reshape(long_tokens.shape),
        finished["s_out"].reshape(short_tokens.shape),
        done["grad"].reshape(long_tokens.shape),
        finished["s_ing"].reshape(short_tokens.shape),
    ) + tuple(grads[k] for k in order)


def solution(mesh):
    long_spec, short_spec = P(None, "dp", "seq", None), P(None, BOTH, None, None)
    rows, columns, vector = P(BOTH, None), P(None, BOTH), P(BOTH)
    params = (vector, columns, columns, vector, rows, columns, vector, rows, vector, rows)
    return jax.shard_map(
        local,
        mesh=mesh,
        in_specs=(
            long_spec,
            short_spec,
            long_spec,
            short_spec,
            P(None, "dp", "seq"),
            P(None, BOTH, None),
            P(),
        )
        + params,
        out_specs=(long_spec, short_spec, long_spec, short_spec) + params,
        check_vma=False,
    )
```

```python
import functools
import types

import jax
import jax.numpy as jnp
from jax import lax
from jax.experimental import pallas as pl
from jax.experimental.pallas import tpu as pltpu
from jax.sharding import PartitionSpec as P

EPS = 1e-05
D, E, N, MB, HALO = 256, 512, 16, 2, 16
LT = 128
NP = N // 2
LOG2E = 1.4426950408889634
LN2 = 0.6931471805599453
F32, BF = jnp.float32, jnp.bfloat16
NT = (((1,), (1,)), ((), ()))
TN = (((0,), (0,)), ((), ()))
BOTH = ("dp", "seq")
IN_ROWS, OUT_ROWS, CH_ROWS = 32, 16, 16
PACK = 2 * IN_ROWS + 2 * OUT_ROWS + CH_ROWS
EDGE = 16
GATHER = PACK + 2 * EDGE
FAR = (8, 4)
SLOTS = (0, 8, 4, 12)
SUM_SLOTS = (0, 8, 4, 12)
AT_DT, AT_A, AT_SMALL = 48, 64, 96


def mm(a, b, dims=None):
    if dims is None:
        return jnp.dot(a, b, preferred_element_type=F32)
    return lax.dot_general(a, b, dims, preferred_element_type=F32)


def iota(shape, axis):
    return lax.broadcasted_iota(jnp.int32, shape, axis)


def onehot(cond):
    return jnp.where(cond, 1.0, 0.0).astype(BF)


def eye(n):
    return onehot(iota((n, n), 0) == iota((n, n), 1))


def split(x):
    hi = x.astype(BF)
    return hi, (x - hi.astype(F32)).astype(BF)


def silu_of_half(h):
    th = jnp.tanh(h)
    value = h * th + h
    u = 0.5 * th
    return value, (0.5 + u) + value * (0.5 - u)


def plus(total, x):
    return x if total is None else total + x


def loop(count, body):
    lax.fori_loop(0, count, lambda i, c: (body(i), c)[1], 0)


def run(name, body, ins, outs, scratch=None, flops=0, far=(), early=(), placed=(), pin=None, hold=(), vmem=60):
    scratch = dict(scratch or {}, **{k: outs[k] for k in early})
    scratch.update({k: (ins[k].shape, ins[k].dtype) for k in far})
    if far:
        scratch["in_sems"] = pltpu.SemaphoreType.DMA((len(far),))
    if early:
        scratch["out_sems"] = pltpu.SemaphoreType.DMA((len(early),))
    in_names, scratch_names = [k + "_far" if k in far else k for k in ins], list(scratch)
    out_names = [k + "_out" if k in early or k in placed else k for k in outs]

    def kernel(*refs):
        r = types.SimpleNamespace(**dict(zip(in_names + out_names + scratch_names, refs)))
        r.early, r.sent, r.fetched = tuple(early), [], []
        body(r)
        for copy in r.sent:
            copy.wait()

    def spec(key):
        return pl.BlockSpec(memory_space=pltpu.HBM if key in far else pltpu.VMEM)

    def at(key, value):
        if key in hold or key in far:
            return pltpu.with_memory_space_constraint(value, pltpu.HBM if key in far else pltpu.VMEM)
        return value

    result = pl.pallas_call(
        kernel,
        out_shape=tuple(
            pin[k](*v) if pin and k in pin else jax.ShapeDtypeStruct(*v) for k, v in outs.items()
        ),
        in_specs=[spec(k) for k in ins],
        out_specs=tuple(
            pl.BlockSpec(memory_space=pltpu.HBM if k in early or k in placed else pltpu.VMEM)
            for k in outs
        ),
        scratch_shapes=[
            pltpu.VMEM(*scratch[k]) if isinstance(scratch[k], tuple) else scratch[k]
            for k in scratch_names
        ],
        compiler_params=pltpu.CompilerParams(vmem_limit_bytes=vmem << 20),
        cost_estimate=pl.CostEstimate(flops=flops, bytes_accessed=1 << 20, transcendentals=0),
        name=name,
    )(*(at(k, v) for k, v in ins.items()))
    return dict(zip(outs, result))


def send(r, *names):
    for name in names:
        if name in r.early:
            copy = pltpu.make_async_copy(
                getattr(r, name), getattr(r, name + "_out"), r.out_sems.at[r.early.index(name)]
            )
            copy.start()
            r.sent.append(copy)


def fetch(r, *names):
    for name in names:
        copy = pltpu.make_async_copy(
            getattr(r, name + "_far"), getattr(r, name), r.in_sems.at[len(r.fetched)]
        )
        copy.start()
        r.fetched.append((name, copy))


def arrived(r, *names):
    for name, copy in r.fetched:
        if name in names:
            copy.wait()


def pack_body(r):
    r.rows[...] = jnp.zeros((8, CH_ROWS), F32)
    r.rows[0:4, :] = r.conv_w[...]
    r.rows[4:5, :] = r.conv_b[...]
    r.rows[5:6, :] = r.dt_b[...]
    r.rows[6:7, :] = r.skip[...]
    r.rows[7:8, 0 : r.gain.shape[1]] = r.gain[...]
    in_t = r.in_wT[...]
    small = jnp.concatenate(split(r.rows[...]), 0)

    def place(a, at, turned=False):
        n = a.shape[0 if turned else 1]
        return mm(a, onehot(iota((n, LT), 0) + at == iota((n, LT), 1)), TN if turned else None)

    a_hi, a_lo = split(r.a_log[...])
    chan = (
        place(r.x_w[...], 0)
        + place(r.dt_w[...], AT_DT, True)
        + place(a_hi, AT_A)
        + place(a_lo, AT_A + N)
        + place(small, AT_SMALL, True)
    ).astype(BF)
    out_w = r.out_w[...]
    for half in range(2):
        lanes = slice(half * LT, (half + 1) * LT)
        r.buf[half * IN_ROWS : (half + 1) * IN_ROWS, :] = in_t[:, lanes]
        low = 2 * IN_ROWS + half * OUT_ROWS
        r.buf[low : low + OUT_ROWS, :] = out_w[:, lanes]
    r.buf[PACK - CH_ROWS : PACK, :] = chan
    for name in ("comp", "tok", "cot", "mask", "s_tok", "s_cot", "s_mask"):
        getattr(r, name + "_near")[...] = getattr(r, name)[...]
    T = r.tok.shape[0] // MB
    for which, first in enumerate((T - 16, 0)):
        rows = [r.tok[mb * T + first : mb * T + first + 16, :].astype(F32) for mb in range(MB)]
        at = 12 if first else 0
        x = jnp.concatenate([x[at : at + 4] for x in rows], 0)
        r.buf[PACK + which * EDGE : PACK + (which + 1) * EDGE, :] = halves(x)


def halves(x):
    return jnp.concatenate([x[:, :LT], x[:, LT:]], 0).astype(BF)


def get_edges(buf, step, at):
    seq = lax.axis_index("seq")
    count = buf.shape[0] // step
    result = []
    before, after = jnp.maximum(seq - 1, 0), jnp.minimum(seq + 1, count - 1)
    for j, low, there in ((before, at[0], seq > 0), (after, at[1], seq < count - 1)):
        x = buf[pl.ds(pl.multiple_of(j * step + low, 16), EDGE), :].astype(F32)
        x = jnp.concatenate([x[:8], x[8:]], 1)
        result.append(jnp.where(there, x, 0.0))
    return result


def unpack(r):
    mine, seq = lax.axis_index("dp"), lax.axis_index("seq")
    count = E // (2 * OUT_ROWS)
    for near in range(4):
        for src, d in ((getattr(r, f"mine{near}"), mine), (getattr(r, f"other{near}"), 1 - mine)):
            for q, far in enumerate(SLOTS):
                at = q * GATHER
                dev = seq ^ (near | far)
                in_at = pl.multiple_of((d * count + dev) * IN_ROWS, IN_ROWS)
                out_at = pl.multiple_of((d * count + dev) * OUT_ROWS, OUT_ROWS)
                for half in range(2):
                    lanes = slice(half * LT, (half + 1) * LT)
                    r.inT[pl.ds(in_at, IN_ROWS), lanes] = src[
                        at + half * IN_ROWS : at + (half + 1) * IN_ROWS, :
                    ]
                    low = at + 2 * IN_ROWS + half * OUT_ROWS
                    r.outw[pl.ds(out_at, OUT_ROWS), lanes] = src[low : low + OUT_ROWS, :]
                r.pe[pl.ds(out_at, CH_ROWS), :] = src[at + PACK - CH_ROWS : at + PACK, :]
                if d is mine:
                    r.edges[pl.ds(pl.multiple_of(dev * 2 * EDGE, 2 * EDGE), 2 * EDGE), :] = src[
                        at + PACK : at + GATHER, :
                    ]
    r.edge[...] = jnp.concatenate(get_edges(r.edges, 2 * EDGE, (0, EDGE)), 0).astype(BF)


def join_body(r):
    rows = r.a.shape[0]
    r.both[0:rows, :] = r.a[...]
    r.both[rows:, :] = r.b[...]


def gather(buf):
    def swapped(x, mask):
        count = lax.axis_size("seq")
        return lax.ppermute(x, "seq", [(i, i ^ mask) for i in range(count)])

    for mask in FAR:
        buf = run(
            f"join{mask}",
            join_body,
            dict(a=buf, b=swapped(buf, mask)),
            dict(both=((2 * buf.shape[0], LT), BF)),
            vmem=8,
        )["both"]
    mine = [buf] + [swapped(buf, near) for near in range(1, 4)]
    other = [lax.ppermute(x, "dp", [(0, 1), (1, 0)]) for x in mine]
    return dict(
        {f"mine{i}": x for i, x in enumerate(mine)}, **{f"other{i}": x for i, x in enumerate(other)}
    )


def derive(r):
    peT = mm(eye(LT), r.pe[...], NT)
    small = peT[AT_SMALL : AT_SMALL + 8] + peT[AT_SMALL + 8 : AT_SMALL + 16]
    r.rowp[...] = small
    rate = -jnp.exp(peT[AT_A : AT_A + N] + peT[AT_A + N : AT_A + 2 * N])
    r.rate[...] = rate
    for n in range(N):
        r.r2[4 * n : 4 * n + 4, :] = jnp.broadcast_to(rate[n : n + 1] * LOG2E, (4, E))
    dt = peT[AT_DT : AT_DT + N]
    r.dtw2[...] = jnp.concatenate([dt, dt, jnp.zeros((LT - 2 * N, E), F32)], 0).astype(BF)
    r.xwT[...] = jnp.where(iota((LT, E), 0) < 3 * N, peT, 0.0).astype(BF)


def gain_of(r):
    per = E // (D // 8)
    low = mm(eye(LT), r.pe[...], NT)[AT_SMALL : AT_SMALL + 16].astype(BF)
    lane, col = iota((E, D), 0), iota((E, D), 1)
    pick = onehot(((lane // per) == (col // 8)) & ((lane % per) == (col % 8)))
    g = mm(low, pick)
    return g[0:8] + g[8:16]


def placing(T, transposed):
    shape = (2 * MB * T, 2 * MB * T)
    row, col = iota(shape, 1 if transposed else 0), iota(shape, 0 if transposed else 1)
    t, scan = row >> 2, row & 3
    turn = T.bit_length() - 1
    pos, src = col & (T - 1), col >> turn
    want = jnp.where(scan >= 2, T - 1 - t, t)
    return (src == scan) & (pos == want)


def gain_row(r):
    return r.gain[0:1, :] if r.gain.shape[0] == 1 else r.gain[7:8, :]


def normalise(tok):
    source = tok.astype(F32)
    scale = lax.rsqrt(jnp.mean(source * source, 1, keepdims=True) + EPS)
    return source, scale, source * scale


def swap_of(r):
    return onehot(iota((D, D), 0) == jnp.broadcast_to(r.comp[...], (D, D)))


def prep(r, T, halo, ready=None):
    R = 4 * T
    B = 64
    swap = swap_of(r)
    put = placing(T, False)
    mrow = jnp.concatenate([r.mask[0:1, :], r.mask[1:2, :]], 1)
    mrow = jnp.concatenate([mrow, mrow], 1)
    cot = r.cot[...]
    r.GR[...] = mm(
        onehot(put & (mrow != 0)), jnp.concatenate([cot, mm(cot, swap).astype(BF)], 0)
    ).astype(BF)
    _, _, unit = normalise(r.tok[...])
    if ready is not None:
        ready()
    gain = gain_row(r)
    normed = (unit * gain).astype(BF)
    r.V[HALO:, :] = mm(
        onehot(put), jnp.concatenate([normed, mm(normed, swap).astype(BF)], 0)
    ).astype(BF)
    if halo:
        hn = (normalise(r.edge[...])[2] * gain).astype(BF)
        r.V[0:HALO, :] = (
            mm(onehot(edge_place(False)), hn)
            + mm(onehot(edge_place(True)), mm(hn, swap).astype(BF))
        ).astype(BF)
        r.ip[0:HALO, :] = mm(r.V[0:HALO, :], r.inT[0:E, :], NT)
    else:
        r.V[0:HALO, :] = jnp.zeros((HALO, D), BF)
        r.ip[0:HALO, :] = jnp.zeros((HALO, E), F32)
    for c in range(0, E, 256):
        r.ip[HALO:, c : c + 256] = mm(r.V[HALO:, :], r.inT[c : c + 256, :], NT)
        r.silu[:, c : c + 256] = mm(r.V[HALO:, :], r.inT[E + c : E + c + 256, :], NT)
    for c in range(0, E, 256):
        r.gm[:, c : c + 256] = mm(r.GR[...], r.outw[c : c + 256, :], NT)
    w = [0.5 * r.rowp[k : k + 1, :] for k in range(5)]

    def first(i):
        r0 = pl.multiple_of(i * B, B)
        at = pl.ds(r0, B)
        x, mid = shifted(r.ip, r0, True, B)
        half = w[4] + w[0] * mid[8 : 8 + B] + w[1] * x[8 : 8 + B]
        half = half + w[2] * mid[HALO : HALO + B] + w[3] * x[HALO : HALO + B]
        inner, slope = silu_of_half(half)
        r.inner[at, :] = inner
        r.slope[at, :] = slope
        r.il[at, :] = inner.astype(BF)
        silu, slope = silu_of_half(0.5 * r.silu[at, :])
        r.silu[at, :] = silu
        r.gslope[at, :] = slope
        r.gm[at, :] = r.gm[at, :] * silu

    loop(R // B, first)
    sel = mm(r.il[...], r.pe[...])
    r.sel[...] = sel
    lane = iota((R, LT), 1)
    low = jnp.where(lane < N, sel, 0.0)
    hi = low.astype(BF).astype(F32)
    both = (hi + pltpu.roll(low - hi, N, 1)).astype(BF)
    for c in range(0, E, 256):
        r.st[:, c : c + 256] = mm(both, r.dtw2[:, c : c + 256])

    def second(i):
        at = pl.ds(pl.multiple_of(i * B, B), B)
        z = r.st[at, :] + r.rowp[5:6, :]
        u = jnp.exp2(jnp.abs(z) * -LOG2E)
        near = u * (1.0 - u * (0.5 - u * (1.0 / 3.0)))
        st = jnp.maximum(z, 0.0) + jnp.where(u < 0.01, near, jnp.log(1.0 + u))
        r.st[at, :] = st
        r.sz[at, :] = jnp.exp(z - st)
        r.si[at, :] = r.inner[at, :] * st

    loop(R // B, second)


B = 32


def shifted(ref, r0, before, B=B):
    x = ref[pl.ds(r0 + (0 if before else HALO), B + HALO), :]
    return x, pltpu.roll(x, 4 if before else B + HALO - 4, 0)


def edge_place(rev):
    row, col = iota((HALO, HALO), 0), iota((HALO, HALO), 1)
    j, scan = row >> 2, row & 3
    if rev:
        return (scan >= 2) & (col == 8 + (scan - 2) * 4 + (3 - j))
    return (scan < 2) & (col == scan * 4 + j)


def maps(r, T):
    R = 4 * T
    sel = r.sel[...]
    lane = iota((R, LT), 1)
    kept = jnp.where((lane >= N) & (lane < 3 * N), sel, 0.0)
    hi = kept.astype(BF).astype(F32)
    both = (hi + pltpu.roll(kept - hi, 64, 1)).astype(BF)
    G = 128
    r8, r4 = iota((2 * G, G), 0), iota((2 * G, G), 1)
    twice = onehot(((r8 >> 3) * 4 + (r8 & 3)) == r4)
    own = (iota((2 * G, LT), 1) & 1) == ((iota((2 * G, LT), 0) >> 2) & 1)
    l, c = iota((LT, NP * LT), 0), iota((LT, NP * LT), 1)
    l = l & 63
    spread_in = onehot((l >= N) & (l < 2 * N) & (((l - N) >> 1) == (c >> 7)))
    spread_out = onehot((l >= 2 * N) & (l < 3 * N) & (((l - 2 * N) >> 1) == (c >> 7)))
    for g in range(R // G):
        left = jnp.where(own, mm(twice, both[g * G : (g + 1) * G]), 0.0).astype(BF)
        r.imb[g * 2 * G : (g + 1) * 2 * G, :] = mm(left, spread_in)
        r.omb[g * 2 * G : (g + 1) * 2 * G, :] = mm(left, spread_out)


def dup(x, low):
    turned = pltpu.roll(x, 4, 0)
    return jnp.where(low, x, turned), jnp.where(low, turned, x)


def lanes_of(e):
    return slice(e * LT, (e + 1) * LT)


def scan_forward(r, T, start, full, U=32, tiles=range(E // LT)):
    low = iota((8, LT), 0) < 4
    for e in tiles:
        es = lanes_of(e)
        if start is None:
            first = tuple(jnp.zeros((8, LT), F32) for _ in range(NP))
        else:
            first = tuple(start[8 * k : 8 * k + 8, es] for k in range(NP))
        if full:
            for k in range(NP):
                r.states[0, 8 * k : 8 * k + 8, es] = first[k]

        def body(i, state):
            state = list(state)
            for u in range(U // 2):
                pair = i * (U // 2) + u
                row = pl.multiple_of(pair * 8, 8)
                st = dup(r.st[pl.ds(row, 8), es], low)
                si = dup(r.si[pl.ds(row, 8), es], low)
                ys = []
                for h in range(2):
                    t = pair * 2 + h
                    r8 = pl.multiple_of(t * 8, 8)
                    acc = None
                    for k in range(NP):
                        decay = jnp.exp2(st[h] * r.r2[8 * k : 8 * k + 8, es])
                        state[k] = decay * state[k] + si[h] * r.imb[pl.ds(r8, 8), lanes_of(k)]
                        if full:
                            r.states[t + 1, 8 * k : 8 * k + 8, es] = state[k]
                            y = state[k] * r.omb[pl.ds(r8, 8), lanes_of(k)]
                            acc = y if acc is None else acc + y
                    if full:
                        ys.append(acc + pltpu.roll(acc, 4, 0))
                if full:
                    r.mix[pl.ds(row, 8), es] = jnp.where(low, ys[0], ys[1])
            return tuple(state)

        last = lax.fori_loop(0, T // U, body, first)
        if not full:
            for k in range(NP):
                r.ends[8 * k : 8 * k + 8, es] = last[k]


def scan_adjoint_local(r, T, U=16, tiles=range(E // LT)):
    low = iota((8, LT), 0) < 4
    for e in tiles:
        es = lanes_of(e)

        def body(i, b):
            b = list(b)
            for u in range(U // 2):
                pair = T // 2 - 1 - (i * (U // 2) + u)
                row = pl.multiple_of(pair * 8, 8)
                st = dup(r.st[pl.ds(row, 8), es], low)
                gm = dup(r.gm[pl.ds(row, 8), es], low)
                for h in (1, 0):
                    r8 = pl.multiple_of((pair * 2 + h) * 8, 8)
                    for k in range(NP):
                        a = gm[h] * r.omb[pl.ds(r8, 8), lanes_of(k)] + b[k]
                        b[k] = jnp.exp2(st[h] * r.r2[8 * k : 8 * k + 8, es]) * a
            return tuple(b)

        last = lax.fori_loop(0, T // U, body, tuple(jnp.zeros((8, LT), F32) for _ in range(NP)))
        for k in range(NP):
            r.ends[64 + 8 * k : 64 + 8 * k + 8, es] = last[k]


def scan_backward(r, T, start, group=2, unroll=4):
    low = iota((8, LT), 0) < 4
    r.alog[...] = jnp.zeros((8 * NP, E), F32)
    r.b[...] = jnp.zeros((8 * NP, E), F32) if start is None else start[64:128, :]
    groups = E // LT // group
    for g in range(groups):
        tiles = [lanes_of(g * group + e) for e in range(group)]

        def body(i, g=g, tiles=tiles):
            for u in range(unroll):
                pair = T // 2 - 1 - (i * unroll + u)
                row = pl.multiple_of(pair * 8, 8)
                r16 = pl.multiple_of(pair * 16, 16)
                st = [dup(r.st[pl.ds(row, 8), es], low) for es in tiles]
                si = [dup(r.si[pl.ds(row, 8), es], low) for es in tiles]
                gm = [dup(r.gm[pl.ds(row, 8), es], low) for es in tiles]
                q = [[None, None] for _ in tiles]
                p = [[None, None] for _ in tiles]
                for k in range(NP):
                    ks = slice(8 * k, 8 * k + 8)
                    im = [r.imb[pl.ds(r16 + 8 * h, 8), lanes_of(k)] for h in range(2)]
                    om = [r.omb[pl.ds(r16 + 8 * h, 8), lanes_of(k)] for h in range(2)]
                    xi, xo = [None, None], [None, None]
                    for e, es in enumerate(tiles):
                        rk = r.r2[ks, es]
                        b = r.b[ks, es]
                        states = [r.states[2 * pair + h, ks, es] for h in range(3)]
                        rates = None
                        for h in (1, 0):
                            a = gm[e][h] * om[h] + b
                            b = jnp.exp2(st[e][h] * rk) * a
                            w = b * states[h]
                            q[e][h] = plus(q[e][h], w * rk)
                            rates = plus(rates, w * st[e][h])
                            p[e][h] = plus(p[e][h], a * im[h])
                            xi[h] = plus(xi[h], a * si[e][h])
                            xo[h] = plus(xo[h], states[h + 1] * gm[e][h])
                        r.b[ks, es] = b
                        r.alog[ks, es] += rates
                    cs = lanes_of(g * NP + k)
                    r.xi[pl.ds(r16, 16), cs] = jnp.concatenate(xi, 0).astype(BF)
                    r.xo[pl.ds(r16, 16), cs] = jnp.concatenate(xo, 0).astype(BF)
                for e, es in enumerate(tiles):
                    for out, v in ((r.q, q[e]), (r.p, p[e])):
                        v = [x + pltpu.roll(x, 4, 0) for x in v]
                        out[pl.ds(row, 8), es] = jnp.where(low, v[0], v[1])

        loop(T // 2 // unroll, body)
    rl, rc = iota((NP * LT, LT), 0), iota((NP * LT, LT), 1)
    red = onehot((rl >> 7) == (rc >> 1))
    W = NP * LT
    for out, x in ((r.yi, r.xi), (r.yo, r.xo)):
        total = x[:, :W]
        for g in range(1, groups):
            total = total + x[:, g * W : (g + 1) * W]
        out[...] = mm(total, red)
    G = 256
    own = (iota((G, LT), 1) & 1) == ((iota((G, LT), 0) >> 2) & 1)
    valid = own & (iota((G, LT), 1) < N)
    r8, r4 = iota((G // 2, G), 1), iota((G // 2, G), 0)
    fold = onehot(((r8 >> 3) * 4 + (r8 & 3)) == r4)
    for g in range(8 * T // G):
        at = slice(g * G, (g + 1) * G)
        y = pltpu.roll(jnp.where(valid, r.yi[at, :], 0.0), N, 1) + pltpu.roll(
            jnp.where(valid, r.yo[at, :], 0.0), 2 * N, 1
        )
        r.gsel[g * G // 2 : (g + 1) * G // 2, :] = mm(fold, y.astype(BF))


def scan_scratch(T):
    return dict(
        states=((T + 1, 8 * NP, E), F32),
        imb=((8 * T, NP * LT), F32),
        omb=((8 * T, NP * LT), F32),
        xi=((8 * T, 2 * NP * LT), BF),
        xo=((8 * T, 2 * NP * LT), BF),
        b=((8 * NP, E), F32),
        yi=((8 * T, LT), F32),
        yo=((8 * T, LT), F32),
        mix=((4 * T, E), F32),
        q=((4 * T, E), F32),
        p=((4 * T, E), F32),
        alog=((8 * NP, E), F32),
        gsel=((4 * T, LT), F32),
    )


LATE = ("ip", "inner", "slope", "silu", "gslope", "sz", "V", "GR")
LATE_LONG = LATE


def post(r, T, halo):
    R = 4 * T
    r.acc[...] = jnp.zeros((64, E), F32)
    arrived(r, *LATE)
    for c in range(0, E, 256):
        r.gg[:, c : c + 256] = mm(r.GR[...], r.outw[c : c + 256, :], NT)

    def first(i):
        at = pl.ds(pl.multiple_of(i * B, B), B)
        gp_at = pl.ds(pl.multiple_of(HALO + i * B, 16), B)
        for e in range(E // LT):
            es = lanes_of(e)
            skip = r.rowp[6:7, es]
            inner, gm, p = r.inner[at, es], r.gm[at, es], r.p[at, es]
            mixed = r.mix[at, es] + skip * inner
            r.il[at, es] = inner.astype(BF)
            r.gated[at, es] = (mixed * r.silu[at, es]).astype(BF)
            gate = r.gg[at, es] * mixed * r.gslope[at, es]
            r.gp[gp_at, E + e * LT : E + (e + 1) * LT] = gate.astype(BF)
            r.gz[at, es] = ((r.q[at, es] * LN2 + inner * p) * r.sz[at, es]).astype(BF)
            r.acc[48:56, es] += fold8(gm * inner)
            r.gg[at, es] = r.st[at, es] * p + gm * skip

    loop(R // B, first)
    lane = iota((R, LT), 1)
    gs_low = jnp.where(lane < N, mm(r.gz[...], r.dtw2[...], NT), r.gsel[...])
    gs_low = jnp.where(lane < 3 * N, gs_low, 0.0)
    r.z[...] = (
        gs_low
        + jnp.where((lane >= AT_DT) & (lane < AT_DT + N), pltpu.roll(r.sel[...], AT_DT, 1), 0.0)
        + jnp.where(lane == AT_SMALL + 5, 1.0, 0.0)
    ).astype(BF)
    gsb = gs_low.astype(BF)
    for c in range(0, E, 256):
        r.mix[:, c : c + 256] = mm(gsb, r.xwT[:, c : c + 256])
    r.gco[0:HALO, :] = jnp.zeros((HALO, E), F32)
    r.gco[HALO + R :, :] = jnp.zeros((HALO, E), F32)

    def second(i):
        r0 = pl.multiple_of(i * B, B)
        at = pl.ds(r0, B)
        x, mid = shifted(r.ip, r0, True)
        gco = (r.gg[at, :] + r.mix[at, :]) * r.slope[at, :]
        r.gco[pl.ds(r0 + HALO, B), :] = gco
        taps = (mid[8 : 8 + B], x[8 : 8 + B], mid[HALO : HALO + B], x[HALO : HALO + B])
        for k, v in enumerate(taps):
            r.acc[8 * k : 8 * k + 8, :] += fold8(gco * v)
        r.acc[32:40, :] += fold8(gco)

    loop(R // B, second)
    w = [r.rowp[k : k + 1, :] for k in range(4)]

    def third(i):
        r0 = pl.multiple_of(i * B, B)
        x, mid = shifted(r.gco, r0, False)
        rows = w[3] * x[0:B] + w[2] * mid[0:B] + w[1] * x[8 : 8 + B] + w[0] * mid[8 : 8 + B]
        r.gp[pl.ds(pl.multiple_of(r0 + HALO, 16), B), :E] = rows.astype(BF)

    loop(R // B, third)
    if halo:
        x = r.gco[0 : 2 * HALO, :]
        mid = pltpu.roll(x, 2 * HALO - 4, 0)
        rows = w[3] * x[0:16] + w[2] * mid[0:16] + w[1] * x[8:24] + w[0] * mid[8:24]
        r.gp[0:HALO, :E] = rows.astype(BF)
        r.gp[0:HALO, E:] = jnp.zeros((HALO, E), BF)
    else:
        r.gp[0:HALO, :] = jnp.zeros((HALO, 2 * E), BF)


def fold8(x):
    result = x[0:8]
    for j in range(8, x.shape[0], 8):
        result = result + x[j : j + 8]
    return result


def param_grads(r):
    zT = mm(eye(LT), r.z[...], NT).astype(BF)
    row = iota((LT, E), 0)
    peT = jnp.where(row < AT_DT, mm(zT, r.il[...]), 0.0)
    from_gz = ((row >= AT_DT) & (row < AT_A)) | (row == AT_SMALL + 5)
    peT = peT + jnp.where(from_gz, mm(zT, r.gz[...]), 0.0)
    rr, cc = iota((LT, 64), 0), iota((LT, 64), 1)
    hi, lo = split(r.alog[...])
    fold = onehot((rr >= AT_A) & (rr - AT_A == (cc >> 2)))
    rate = jnp.concatenate(
        [jnp.zeros((AT_A, E), F32), r.rate[...], jnp.zeros((LT - AT_A - N, E), F32)], 0
    )
    peT = peT + (mm(fold, hi) + mm(fold, lo)) * rate
    hi, lo = split(r.acc[...])
    fold = onehot((rr >= AT_SMALL) & (rr - AT_SMALL == (cc >> 3)))
    r.g_peT[...] = peT + mm(fold, hi) + mm(fold, lo)
    r.g_out[...] = mm(r.gated[...], r.GR[...], TN)
    for c in range(0, 2 * E, 256):
        r.g_inT[c : c + 256, :] = mm(r.gp[:, c : c + 256], r.V[...], TN)
    rows = mm(r.gp[...], r.inT[...])
    r.rows[...] = rows
    term = rows * r.V[...].astype(F32)
    first = (iota(term.shape, 0) & 3) < 2
    fwd = jnp.sum(jnp.where(first, term, 0.0), 0, keepdims=True)
    rev = jnp.sum(jnp.where(first, 0.0, term), 0, keepdims=True)
    both = jnp.concatenate([fwd, rev, jnp.zeros((6, D), F32)], 0)
    hi, lo = split(both)
    swap = swap_of(r)
    r.g_gain[...] = both + pltpu.roll(mm(hi, swap) + mm(lo, swap), 7, 0)


def edge_delta(r):
    swap = swap_of(r)
    hi, lo = split(r.rows[0:HALO, :])
    grad = jnp.where(
        (iota((HALO, D), 0) & 3) < 2, r.rows[0:HALO, :], mm(hi, swap) + mm(lo, swap)
    )
    _, scale, unit = normalise(mm(onehot(edge_place(False) | edge_place(True)), r.edge[...]))
    g = grad * gain_row(r)
    return scale * (g - unit * jnp.mean(g * unit, 1, keepdims=True))


def window_outputs(r, tok, cot, mask, gated, rows, out, ing):
    half = tok.shape[0]
    T = half // MB
    gain = gain_row(r)
    swap = swap_of(r)
    back = onehot(placing(T, True))
    g = mm(back, gated[...]).astype(BF)
    source, scale, unit = normalise(tok[...])
    outs = mm(r.outw[...], swap).astype(BF)
    out[...] = (source + mm(g[:half], r.outw[...]) + mm(g[half:], outs)).astype(BF)
    hi, lo = split(rows[HALO:, :])
    grad = (
        mm(back[:half], hi)
        + mm(back[:half], lo)
        + mm(back[half:], mm(hi, swap).astype(BF))
        + mm(back[half:], mm(lo, swap).astype(BF))
    )
    g = grad * gain
    mrow = jnp.concatenate([mask[0:1, :], mask[1:2, :]], 1)
    keep = onehot((iota((half, half), 0) == iota((half, half), 1)) & (mrow != 0))
    ing[...] = scale * (g - unit * jnp.mean(g * unit, 1, keepdims=True)) + mm(keep, cot[...])


def outputs_body(r):
    window_outputs(r, r.l_tok, r.l_cot, r.l_mask, r.l_gated, r.l_rows, r.l_out, r.l_ing)
    window_outputs(r, r.s_tok, r.s_cot, r.s_mask, r.s_gated, r.s_rows, r.s_out, r.s_ing)
    r.mark[...] = jnp.zeros((8, LT), F32)


def post_scratch(T):
    R = 4 * T
    return dict(
        acc=((64, E), F32),
        gg=((R, E), F32),
        gco=((R + 2 * HALO, E), F32),
        il=((R, E), BF),
        gated=((R, E), BF),
        gz=((R, E), BF),
        z=((R, LT), BF),
        gp=((R + HALO, 2 * E), BF),
    )


GRADS = dict(
    g_inT=((2 * E, D), F32), g_out=((E, D), F32), g_peT=((LT, E), F32), g_gain=((8, D), F32)
)


def rows_out(T):
    return dict(rows=((4 * T + HALO, D), F32))


STATE_ROWS = 4 * 8 * NP
ELEMENT = STATE_ROWS + 4 * 8


def to_spans(r, at, rows):
    seq = lax.axis_index("seq")
    count = r.carry_out.shape[0] // ELEMENT

    def start(j):
        dst = r.carry_out.at[pl.ds(pl.multiple_of(j * ELEMENT + at, 32), rows), :]

        @pl.when(j > seq)
        def _():
            pltpu.make_async_copy(r.later.at[at : at + rows, :], dst, r.carry_sem).start()

        @pl.when(j <= seq)
        def _():
            pltpu.make_async_copy(r.earlier.at[at : at + rows, :], dst, r.carry_sem).start()

    loop(count, start)


def send_sums(r, T):
    def add(i, total):
        return total + r.st[pl.ds(pl.multiple_of(i * 8, 8), 8), :]

    sums = lax.fori_loop(0, T // 2, add, jnp.zeros((8, E), F32))
    sums = sums + pltpu.roll(sums, 4, 0)
    sums = jnp.concatenate([sums[:, lanes_of(e)] for e in range(E // LT)], 0).astype(BF)
    r.later[STATE_ROWS:, :] = sums
    r.earlier[STATE_ROWS:, :] = sums
    to_spans(r, STATE_ROWS, 32)


def send_elements(r, e):
    normed = (iota((8 * NP, LT), 0) & 3) < 2
    state, adjoint = r.ends[0:64, lanes_of(e)], r.ends[64:128, lanes_of(e)]
    at = 64 * e
    r.later[at : at + 64, :] = jnp.where(normed, state, adjoint).astype(BF)
    r.earlier[at : at + 64, :] = jnp.where(normed, adjoint, state).astype(BF)
    to_spans(r, at, 64)


def wait_elements(r):
    pltpu.make_async_copy(r.carry_out, r.carry_out, r.carry_sem).wait()


def enter(r):
    seq = lax.axis_index("seq")
    count = r.elements.shape[0] // ELEMENT
    r.fold[...] = jnp.zeros((16 * NP, E), F32)

    def add(half, j):
        base = j * ELEMENT
        sums = r.elements[pl.ds(pl.multiple_of(base + STATE_ROWS, 32), 32), :].astype(F32)
        for e in range(E // LT):
            es = lanes_of(e)
            x = r.elements[pl.ds(pl.multiple_of(base + e * 64, 32), 64), :].astype(F32)
            for k in range(NP):
                ks = slice(8 * k, 8 * k + 8)
                at = slice(64 * half + 8 * k, 64 * half + 8 * k + 8)
                decay = jnp.exp2(r.r2[ks, es] * sums[8 * e : 8 * e + 8])
                r.fold[at, es] = decay * r.fold[at, es] + x[ks]

    loop(seq, lambda i: add(0, i))
    loop(count - 1 - seq, lambda i: add(1, count - 1 - i))
    normed = (iota((8 * NP, E), 0) & 3) < 2
    r.entering[0:64, :] = jnp.where(normed, r.fold[0:64, :], r.fold[64:128, :])
    r.entering[64:128, :] = jnp.where(normed, r.fold[64:128, :], r.fold[0:64, :])


def long_start_body(r, T, packed):

    def ready():
        if packed:
            unpack(r)
            r.gain[...] = gain_of(r)
        derive(r)

    prep(r, T, True, ready)
    send(r, *PREP_OUTS)
    maps(r, T)
    send_sums(r, T)
    for e in range(E // LT):
        scan_forward(r, T, None, False, tiles=(e,))
        scan_adjoint_local(r, T, tiles=(e,))
        send_elements(r, e)
    wait_elements(r)


def short_windows_body(r, T):
    prep(r, T, False)
    maps(r, T)
    scan_forward(r, T, None, True)
    scan_backward(r, T, None)
    post(r, T, False)
    param_grads(r)


FROM_SHORT = ("s_inT", "s_out", "s_peT", "s_gain")
LONG_FIRST = ("sel", "st", "si", "gm")
LONG_FAR = LONG_FIRST + LATE_LONG + FROM_SHORT


def long_windows_body(r, T):
    fetch(r, *LONG_FIRST)
    arrived(r, "sel")
    maps(r, T)
    enter(r)
    arrived(r, "st", "si", "gm")
    fetch(r, *LATE_LONG, *FROM_SHORT)
    scan_forward(r, T, r.entering, True)
    scan_backward(r, T, r.entering)
    post(r, T, True)
    param_grads(r)
    arrived(r, *FROM_SHORT)
    finish_grads(r)


def finish_grads(r):
    r.g_peT[...] += r.s_peT[...]
    r.g_gain[...] = (r.g_gain[...] + r.s_gain[...]) / gain_row(r)
    if not hasattr(r, "give"):
        r.g_inT[...] += r.s_inT[...]
        r.g_out[...] += r.s_out[...]
        r.delta[...] = edge_delta(r)
        return
    lane, col = iota((D, E), 1), iota((D, E), 0)
    pick = onehot(((lane // 16) == (col // 8)) & ((lane % 16) == (col % 8)))
    peT = r.g_peT[...] + jnp.where(
        iota((LT, E), 0) == AT_SMALL + 7, mm(r.g_gain[0:1, :].astype(BF), pick), 0.0
    )
    r.pe_out[...] = peT.T.astype(BF)
    mine, seq = lax.axis_index("dp"), lax.axis_index("seq")
    count = E // (2 * OUT_ROWS)
    delta = edge_delta(r).astype(BF)
    row, col = iota((8, HALO), 0), iota((8, HALO), 1)
    of = 4 * (row & 3) + (row >> 2)
    r.deltas[0:EDGE, :] = halves(mm(onehot(col == of), delta))
    r.deltas[EDGE:, :] = halves(mm(onehot(col == of + 2), delta))
    slots = [(4 * near + q, seq ^ (near | far)) for near in range(4) for q, far in enumerate(SUM_SLOTS)]
    for dst, d, step in ((r.give, 1 - mine, PACK), (r.keep, mine, GATHER)):
        for slot, dev in slots:
            at = slot * step
            in_at = pl.multiple_of((d * count + dev) * IN_ROWS, IN_ROWS)
            out_at = pl.multiple_of((d * count + dev) * OUT_ROWS, OUT_ROWS)
            for half in range(2):
                lanes = slice(half * LT, (half + 1) * LT)
                rows = pl.ds(in_at, IN_ROWS)
                dst[at + half * IN_ROWS : at + (half + 1) * IN_ROWS, :] = (
                    r.g_inT[rows, lanes] + r.s_inT[rows, lanes]
                ).astype(BF)
                low = at + 2 * IN_ROWS + half * OUT_ROWS
                rows = pl.ds(out_at, OUT_ROWS)
                dst[low : low + OUT_ROWS, :] = (r.g_out[rows, lanes] + r.s_out[rows, lanes]).astype(BF)
            dst[at + PACK - CH_ROWS : at + PACK, :] = r.pe_out[pl.ds(out_at, CH_ROWS), :]
    zero = jnp.zeros((EDGE, LT), BF)
    for slot, dev in slots:
        at = slot * GATHER + PACK
        r.keep[at : at + EDGE, :] = jnp.where(dev == seq - 1, r.deltas[0:EDGE, :], zero)
        r.keep[at + EDGE : at + 2 * EDGE, :] = jnp.where(dev == seq + 1, r.deltas[EDGE:, :], zero)


def total(*parts):
    result = parts[0].astype(F32)
    for x in parts[1:]:
        result = result + x.astype(F32)
    return result


def add_core_body(r):
    for near in range(4):
        part = getattr(r, f"part{near}")
        for q in range(4):
            at, keep, got = q * GATHER, (4 * near + q) * GATHER, (4 * near + q) * PACK
            part[at : at + PACK, :] = total(
                r.keep[keep : keep + PACK, :], r.got[got : got + PACK, :]
            ).astype(BF)
            part[at + PACK : at + GATHER, :] = r.keep[keep + PACK : keep + GATHER, :]


def add_near_body(r):
    for i, dst in enumerate((r.low, r.high)):
        at = slice(i * 2 * GATHER, (i + 1) * 2 * GATHER)
        dst[...] = total(r.part0[at, :], r.got1[at, :], r.got2[at, :], r.got3[at, :]).astype(BF)


def add_far_body(r):
    r.own[...] = total(r.low[0:GATHER, :], r.got[0:GATHER, :]).astype(BF)
    r.last[...] = total(r.low[GATHER:, :], r.got[GATHER:, :]).astype(BF)


def scatter(give, keep, after):
    def swapped(x, mask):
        count = lax.axis_size("seq")
        return lax.ppermute(x, "seq", [(i, i ^ mask) for i in range(count)])

    got = lax.ppermute(give, "dp", [(0, 1), (1, 0)])
    four = ((4 * GATHER, LT), BF)
    parts = run(
        "add_core",
        add_core_body,
        dict(got=got, keep=keep),
        {f"part{i}": four for i in range(4)},
        hold=("keep", "got"),
        vmem=8,
    )
    near = {f"got{i}": swapped(parts[f"part{i}"], i) for i in range(1, 4)}
    two = ((2 * GATHER, LT), BF)
    sums = run(
        "add_near",
        add_near_body,
        dict(part0=parts["part0"], after=after, **near),
        dict(low=two, high=two),
        vmem=8,
    )
    one = ((GATHER, LT), BF)
    ends = run(
        "add_far",
        add_far_body,
        dict(low=sums["low"], got=swapped(sums["high"], 4)),
        dict(own=one, last=one),
        vmem=8,
    )
    return ends["own"], swapped(ends["last"], 8)


def final_body(r, packed):
    r.grad[...] = r.ing[...]
    T = r.grad.shape[0] // MB
    if packed:
        block = total(r.own[...], r.got[...])
        from_next, from_prev = (
            jnp.concatenate([x[:8], x[8:]], 1)
            for x in (block[PACK : PACK + EDGE], block[PACK + EDGE :])
        )
    else:
        from_prev, from_next = r.from_prev[...], r.from_next[...]
    for mb in range(MB):
        for j in range(4):
            prev = 4 * mb + j if packed else 4 * j + 2 + mb
            follow = 4 * mb + j if packed else 4 * j + mb
            row = mb * T + T - 4 + j
            r.grad[row : row + 1, :] += from_next[follow : follow + 1, :]
            row = mb * T + 3 - j
            r.grad[row : row + 1, :] += from_prev[prev : prev + 1, :]
    if not packed:
        return
    for half in range(2):
        lanes = slice(half * LT, (half + 1) * LT)
        r.in_wT[:, lanes] = block[half * IN_ROWS : (half + 1) * IN_ROWS]
        low = 2 * IN_ROWS + half * OUT_ROWS
        r.out_w[:, lanes] = block[low : low + OUT_ROWS]
    pe = block[PACK - CH_ROWS : PACK]
    hi, lo = split(pe)
    peT = mm(eye(LT), hi, NT) + mm(eye(LT), lo, NT)
    r.x_w[...] = pe[:, : 3 * N]
    r.a_log[...] = pe[:, AT_A : AT_A + N]
    r.dt_w[...] = peT[AT_DT : AT_DT + N]
    small = peT[AT_SMALL : AT_SMALL + 8]
    r.conv_w[...] = small[0:4]
    r.conv_b[...] = small[4:5]
    r.dt_b[...] = small[5:6]
    r.skip[...] = small[6:7]
    r.gain[...] = small[7:8, 0 : r.gain.shape[1]]


PREP_OUTS = ("V", "GR", "ip", "inner", "slope", "silu", "gslope", "st", "sz", "si", "gm", "sel")


def prep_outs(T):
    R = 4 * T
    wide = ((R, E), F32)
    return dict(
        V=((R + HALO, D), BF),
        GR=((R, D), BF),
        ip=((R + HALO, E), F32),
        inner=wide,
        slope=wide,
        silu=wide,
        gslope=wide,
        st=wide,
        sz=wide,
        si=wide,
        gm=wide,
        sel=((R, LT), F32),
    )


def local(
    long_tokens,
    short_tokens,
    long_cotangent,
    short_cotangent,
    long_mask,
    short_mask,
    complement,
    norm_gain,
    in_weight,
    conv_weight,
    conv_bias,
    x_weight,
    dt_weight,
    dt_bias,
    a_log,
    d_skip,
    out_weight,
):
    count = lax.axis_size("seq")
    span, short = long_tokens.shape[2], short_tokens.shape[2]
    packed = count == 16 and out_weight.shape[0] == OUT_ROWS and in_weight.shape[1] == IN_ROWS
    comp = complement.reshape(1, D)
    up = [(i, i + 1) for i in range(count - 1)]
    down = [(i + 1, i) for i in range(count - 1)]

    def tokens_of(tok, cot, mask):
        T = tok.shape[2]
        return dict(
            tok=tok.reshape(MB * T, D), cot=cot.reshape(MB * T, D), mask=mask.reshape(MB, T)
        )

    long_in = tokens_of(long_tokens, long_cotangent, long_mask)
    short_in = tokens_of(short_tokens, short_cotangent, short_mask)

    near = dict(comp=comp, **long_in, **{"s_" + k: v for k, v in short_in.items()})

    if packed:
        packing = run(
            "pack",
            pack_body,
            dict(
                gain=norm_gain.reshape(1, -1),
                in_wT=in_weight.T,
                conv_w=conv_weight,
                conv_b=conv_bias.reshape(1, -1),
                x_w=x_weight,
                dt_w=dt_weight,
                dt_b=dt_bias.reshape(1, -1),
                a_log=a_log,
                skip=d_skip.reshape(1, -1),
                out_w=out_weight,
                **near,
            ),
            dict(
                buf=((GATHER, LT), BF),
                **{k + "_near": (v.shape, v.dtype) for k, v in near.items()},
            ),
            dict(rows=((8, CH_ROWS), F32)),
            pin={k: pltpu.VMEM for k in ("buf", *(k + "_near" for k in near))},
        )
        weights_in = gather(packing["buf"])
        near = {k: packing[k + "_near"] for k in near}
    else:
        tail = lax.ppermute(long_tokens[:, 0, span - 4 :, :].reshape(8, D), "seq", up)
        head = lax.ppermute(long_tokens[:, 0, :4, :].reshape(8, D), "seq", down)

        def whole(a, axis):
            return lax.all_gather(a, BOTH, axis=axis, tiled=True)

        small = jnp.stack([*conv_weight, conv_bias, dt_bias, d_skip, jnp.zeros_like(d_skip)])
        columns = jnp.concatenate([a_log, small.T], 1)
        hi = columns.astype(BF)
        lo = (columns - hi.astype(F32)).astype(BF)
        zero = jnp.zeros((columns.shape[0], LT - AT_SMALL - 16), BF)
        chan = jnp.concatenate(
            [x_weight, dt_weight.T, hi[:, :N], lo[:, :N], hi[:, N:], lo[:, N:], zero], 1
        )
        weights_in = dict(
            inT=whole(in_weight.T, 0),
            outw=whole(out_weight, 0),
            pe=whole(chan, 0),
            gain=whole(norm_gain, 0).reshape(1, D),
            edge=jnp.concatenate([tail, head], 0),
        )

    derived = dict(
        r2=((8 * NP, E), F32),
        rowp=((8, E), F32),
        rate=((N, E), F32),
        dtw2=((LT, E), BF),
        xwT=((LT, E), BF),
    )
    unpacked = dict(
        inT=((2 * E, D), BF),
        outw=((E, D), BF),
        pe=((E, LT), BF),
        gain=((8, D), F32),
        edge=((HALO, D), BF),
    )
    started = run(
        "long_start",
        functools.partial(long_start_body, T=span, packed=packed),
        dict({k: near[k] for k in ("comp", *long_in)}, **weights_in),
        dict(
            carry=((count * ELEMENT, LT), BF), **prep_outs(span), **derived, **(unpacked if packed else {})
        ),
        dict(
            il=((4 * span, E), BF),
            imb=((8 * span, NP * LT), F32),
            omb=((8 * span, NP * LT), F32),
            ends=((128, E), F32),
            later=((ELEMENT, LT), BF),
            earlier=((ELEMENT, LT), BF),
            carry_sem=pltpu.SemaphoreType.DMA,
            **(dict(edges=((count * 2 * EDGE, LT), BF)) if packed else {}),
        ),
        flops=1 << 33,
        early=PREP_OUTS,
        placed=("carry",),
        pin=dict(
            {k: pltpu.HBM for k in PREP_OUTS + ("carry",)},
            **{k: pltpu.VMEM for k in (*derived, *(unpacked if packed else ()))},
        ),
        vmem=40,
    )
    weights = {k: started[k] for k in derived}
    for k in unpacked:
        weights[k] = started[k] if packed else weights_in[k]

    elements = lax.all_to_all(started["carry"], "seq", 0, 0, tiled=True)
    shorts = run(
        "short_windows",
        functools.partial(short_windows_body, T=short),
        dict(
            comp=near["comp"],
            **{k: near["s_" + k] for k in short_in},
            **{
                k: weights[k]
                for k in ("inT", "outw", "pe", "gain", "dtw2", "xwT", "rowp", "r2", "rate")
            },
        ),
        dict(GRADS, **rows_out(short), gated=((4 * short, E), BF)),
        {
            k: v
            for k, v in dict(scan_scratch(short), **post_scratch(short), **prep_outs(short)).items()
            if k != "gated"
        },
        flops=1 << 36,
        hold=("inT", "outw", "pe", "dtw2", "xwT", "rowp", "r2", "rate", "gain", "comp", "tok", "cot", "mask"),
        vmem=56,
    )

    ins = dict(
        elements=elements,
        comp=comp,
        **{k: weights[k] for k in ("edge", "r2", "rowp", "rate", "gain", "inT", "outw", "xwT", "dtw2")},
        **{k: started[k] for k in PREP_OUTS},
        s_inT=shorts["g_inT"],
        s_out=shorts["g_out"],
        s_peT=shorts["g_peT"],
        s_gain=shorts["g_gain"],
    )
    outs = dict(rows_out(span), gated=((4 * span, E), BF))
    scratch = dict(entering=((16 * NP, E), F32), fold=((16 * NP, E), F32))
    if packed:
        outs.update(give=((count * PACK, LT), BF), keep=((count * GATHER, LT), BF))
        scratch.update(GRADS, pe_out=((E, LT), BF), deltas=((2 * EDGE, LT), BF))
    else:
        outs.update(GRADS, delta=((HALO, D), F32))
    scratch.update(scan_scratch(span))
    scratch.update({k: v for k, v in post_scratch(span).items() if k not in outs})
    longs = run(
        "long_windows",
        functools.partial(long_windows_body, T=span),
        ins,
        outs,
        scratch,
        flops=1 << 35,
        far=LONG_FAR,
        hold=(*(("elements",) if packed else ()), "edge", "r2", "rowp", "rate", "gain", "inT", "outw", "xwT", "dtw2"),
        pin={k: pltpu.VMEM for k in ("rows", "gated", *(("give", "keep") if packed else ()))},
        vmem=56,
    )

    outs = dict(
        l_out=((MB * span, D), BF),
        l_ing=((MB * span, D), F32),
        s_out=((MB * short, D), BF),
        s_ing=((MB * short, D), F32),
        mark=((8, LT), F32),
    )
    ins = dict(comp=comp, outw=weights["outw"], gain=weights["gain"])
    ins.update({"l_" + k: v for k, v in long_in.items()}, l_gated=longs["gated"], l_rows=longs["rows"])
    ins.update(
        {"s_" + k: v for k, v in short_in.items()},
        s_gated=shorts["gated"],
        s_rows=shorts["rows"],
    )
    finished = run("outputs", outputs_body, ins, outs, flops=1 << 32, hold=("l_rows", "l_gated"), vmem=32)
    ins = dict(ing=finished["l_ing"])
    outs = dict(grad=((MB * span, D), F32))
    if packed:
        ins["own"], ins["got"] = scatter(longs["give"], longs["keep"], finished["mark"])
        outs.update(
            gain=((1, D // (2 * count)), F32),
            in_wT=((IN_ROWS, D), F32),
            conv_w=((4, CH_ROWS), F32),
            conv_b=((1, CH_ROWS), F32),
            x_w=((CH_ROWS, 3 * N), F32),
            dt_w=((N, CH_ROWS), F32),
            dt_b=((1, CH_ROWS), F32),
            a_log=((CH_ROWS, N), F32),
            skip=((1, CH_ROWS), F32),
            out_w=((OUT_ROWS, D), F32),
        )
    else:
        ins["from_next"] = lax.ppermute(longs["delta"], "seq", down)
        ins["from_prev"] = lax.ppermute(longs["delta"], "seq", up)
    done = run("final", functools.partial(final_body, packed=packed), ins, outs, vmem=8)
    if packed:
        grads = {k: done[k] for k in outs if k != "grad"}
        grads["in_w"] = grads["in_wT"].T
        for k in ("gain", "conv_b", "dt_b", "skip"):
            grads[k] = grads[k].reshape(-1)
    else:

        def own(a, axis=0):
            return lax.psum_scatter(a, BOTH, scatter_dimension=axis, tiled=True)

        pe = own(longs["g_peT"].T)
        grads = dict(
            gain=own(longs["g_gain"][0]),
            in_w=own(longs["g_inT"]).T,
            conv_w=pe[:, AT_SMALL : AT_SMALL + 4].T,
            conv_b=pe[:, AT_SMALL + 4],
            x_w=pe[:, : 3 * N],
            dt_w=pe[:, AT_DT : AT_DT + N].T,
            dt_b=pe[:, AT_SMALL + 5],
            a_log=pe[:, AT_A : AT_A + N],
            skip=pe[:, AT_SMALL + 6],
            out_w=own(longs["g_out"]),
        )
    order = ("gain", "in_w", "conv_w", "conv_b", "x_w", "dt_w", "dt_b", "a_log", "skip", "out_w")
    return (
        finished["l_out"].reshape(long_tokens.shape),
        finished["s_out"].reshape(short_tokens.shape),
        done["grad"].reshape(long_tokens.shape),
        finished["s_ing"].reshape(short_tokens.shape),
    ) + tuple(grads[k] for k in order)


def solution(mesh):
    long_spec, short_spec = P(None, "dp", "seq", None), P(None, BOTH, None, None)
    rows, columns, vector = P(BOTH, None), P(None, BOTH), P(BOTH)
    params = (vector, columns, columns, vector, rows, columns, vector, rows, vector, rows)
    return jax.shard_map(
        local,
        mesh=mesh,
        in_specs=(
            long_spec,
            short_spec,
            long_spec,
            short_spec,
            P(None, "dp", "seq"),
            P(None, BOTH, None),
            P(),
        )
        + params,
        out_specs=(long_spec, short_spec, long_spec, short_spec) + params,
        check_vma=False,
    )
```
